32 devices in a mesh: step: 8 (over z, x), seq: 4 (over y, core).
Axes of the slice: x: 2, y: 2, z: 4, core: 2. Of those that a mesh axis runs over, the one named last changes fastest.
Arguments:
- trajectory: float32 [8, 512, 3072], P('step', 'seq'), may hold values from -6 to 6
- x_start: float32 [512, 3072], P('seq'), may hold values from -6 to 6
- t_idx: int32 [8], P('step'), may hold values from 0 to 49
- mod_table: float32 [50, 9216], replicated, may hold values from -3 to 3
- step_sizes: float32 [50], replicated, may hold values from 0.05 to 0.3
- q_gain: float32 [128], replicated, may hold values from 1 to 10, as said below
- k_gain: float32 [128], replicated, may hold values from 1 to 10, as said below
- w_qkv: bfloat16 [3, 3072, 2048], P(None, None, 'seq'), may hold values from -0.109375 to 0.109375
- w_mlp_in: bfloat16 [3072, 6144], P(None, 'seq'), may hold values from -0.109375 to 0.109375
- w_out_attn: bfloat16 [2048, 3072], P('seq'), may hold values from -0.0625 to 0.0625
- w_out_mlp: bfloat16 [6144, 3072], P('seq'), may hold values from -0.0625 to 0.0625
Outputs:
- x_next: float32 [8, 512, 3072], P('step', 'seq')
The draws below stay inside these ranges and needn't reach their ends.
Inputs may be any that keep to these rules, and one draw needn't show every extreme that they name: `q_gain`: positive gains. `k_gain`: positive gains.
All inputs are finite; a program needn't handle non-finite values.
Results may differ from the reference program's by a relative error of at most 0.011.
Values may be sent and summed in bfloat16 or wider, within the bound.
No kernel may reach another device: no remote copies, remote signals or barrier semaphores. Data moves between devices by JAX's collectives and lax.ppermute only.
A program may use at most 128 MiB of HBM per device.

```python
import math
import jax
import jax.numpy as jnp
from jax import lax

D = 3072
HEAD_DIM = 128
H = 16
FF = 6144
NT = 50
TOKENS = 512
SLOTS = 8
N_SEQ = 4


def gain_draw(key, lowest, highest):
    return jnp.exp(jax.random.uniform(key, (HEAD_DIM,), jnp.float32, math.log(lowest), math.log(highest)))


def draw_q_gain(key, part):
    key = jax.random.fold_in(key, 11)
    return gain_draw(key, 1.0, 2.5)


def draw_k_gain(key, part):
    key = jax.random.fold_in(key, 23)
    return gain_draw(key, 1.0, 2.5)


def plant(values, stream_key, smallest, high):
    shape = values.shape
    place = [jax.random.randint(jax.random.fold_in(stream_key, axis), (), 0, shape[axis]) for axis in range(len(shape))]
    values = values.at[tuple(place)].set(smallest)
    longest = shape.index(max(shape))
    place[longest] = (place[longest] + 1) % shape[longest]
    return values.at[tuple(place)].set(high)


def steps_of(own_key, extent, split, least, top_value):
    level, own = 1.0, jax.random.fold_in(own_key, 6)
    for position, shards_of in split:
        steps = jnp.exp(jax.random.uniform(jax.random.fold_in(own, position), (shards_of,), jnp.float32, least / len(split), top_value / len(split)))
        level = level * jnp.repeat(steps, extent[position] // shards_of).reshape([-1 if axis == position else 1 for axis in range(len(extent))])
    return level


def scatter_about(own_key, extent, scale, reach, split=(), held_as=jnp.bfloat16):
    level = steps_of(own_key, extent, split, -0.22, 0.18) if split else 1.0
    values = jax.random.normal(own_key, extent, jnp.float32) * scale * level
    return jnp.minimum(jnp.maximum(values, -reach), reach).astype(held_as)


def setup_inputs(seed: int = 0) -> dict:
    key_list = jax.random.split(jax.random.key(seed), 12)
    trajectory = scatter_about(key_list[0], (SLOTS, TOKENS, D), 1.0, 6.0, ((0, 8), (1, 4)), jnp.float32)
    x_start = scatter_about(key_list[1], (TOKENS, D), 1.0, 6.0, ((0, 4),), jnp.float32)
    t_idx = plant(jax.random.randint(key_list[2], (SLOTS,), 0, NT), jax.random.fold_in(key_list[2], 1), 0, NT - 1).astype(jnp.int32)
    mod_table = scatter_about(key_list[3], (NT, 3 * D), 0.5, 3.0, (), jnp.float32)
    step_sizes = jnp.clip(jnp.exp(jax.random.uniform(key_list[4], (NT,), jnp.float32, math.log(0.05), math.log(0.3))), 0.05, 0.3)
    q_gain = draw_q_gain(jax.random.fold_in(key_list[11], 71), 0)
    k_gain = draw_k_gain(jax.random.fold_in(key_list[11], 71), 0)
    w_qkv = scatter_about(key_list[7], (3, D, H * HEAD_DIM), D ** -0.5, 0.109375, ((2, 4),))
    w_mlp_in = scatter_about(key_list[8], (D, FF), D ** -0.5, 0.109375, ((1, 4),))
    w_out_attn = scatter_about(key_list[9], (H * HEAD_DIM, D), (H * HEAD_DIM + FF) ** -0.5, 0.0625, ((0, 4),))
    w_out_mlp = scatter_about(key_list[10], (FF, D), (H * HEAD_DIM + FF) ** -0.5, 0.0625, ((0, 4),))
    return dict(trajectory=trajectory, x_start=x_start, t_idx=t_idx, mod_table=mod_table, step_sizes=step_sizes, q_gain=q_gain, k_gain=k_gain, w_qkv=w_qkv, w_mlp_in=w_mlp_in, w_out_attn=w_out_attn, w_out_mlp=w_out_mlp)


eps = 1e-06

def layer_norm(state):
    center = state - lax.optimization_barrier(jnp.mean(state, axis=-1, keepdims=True))
    spread = lax.optimization_barrier(jnp.mean(center * center, axis=-1, keepdims=True))
    return center * lax.rsqrt(spread + eps)

def head_norm(projected, gain):
    square = lax.optimization_barrier(jnp.mean(projected * projected, axis=-1, keepdims=True))
    return (projected * lax.rsqrt(square + eps) * gain).astype(jnp.bfloat16)

def one_slot(state, t_index, mod_table, step_sizes, q_gain, k_gain, w_qkv, w_mlp_in, w_out_attn, w_out_mlp):
    width = state.shape[1]
    head_dim = q_gain.shape[0]
    tok_rows = state.shape[0]
    modulation = mod_table[t_index]
    shift_mod = modulation[:width]
    scale_mod = modulation[width:2 * width]
    gate_mod = modulation[2 * width:]
    modulated = (layer_norm(state) * (1.0 + scale_mod) + shift_mod).astype(jnp.bfloat16)

    def project(which):
        return jnp.dot(modulated, w_qkv[which], preferred_element_type=jnp.float32).reshape(tok_rows, -1, head_dim)
    queries = head_norm(project(0), q_gain)
    key_rows = head_norm(project(1), k_gain)
    value_rows = project(2).astype(jnp.bfloat16)
    scores = jnp.einsum('qhd,khd->hqk', queries.astype(jnp.float32), key_rows.astype(jnp.float32), precision=lax.Precision.HIGHEST) / math.sqrt(head_dim)
    probs = jax.nn.softmax(scores, axis=-1).astype(jnp.bfloat16)
    attended = jnp.einsum('hqk,khd->qhd', probs.astype(jnp.float32), value_rows.astype(jnp.float32), precision=lax.Precision.HIGHEST).astype(jnp.bfloat16).reshape(tok_rows, -1)
    activated = jax.nn.gelu(jnp.dot(modulated, w_mlp_in, preferred_element_type=jnp.float32), approximate=True).astype(jnp.bfloat16)
    attn_block = attended.shape[1] // N_SEQ
    mlp_block = activated.shape[1] // N_SEQ
    branch = jnp.zeros((tok_rows, width), jnp.float32)
    for shard_idx in range(N_SEQ):
        attn_lo = shard_idx * attn_block
        mlp_lo = shard_idx * mlp_block
        term = jnp.dot(attended[:, attn_lo:attn_lo + attn_block], w_out_attn[attn_lo:attn_lo + attn_block], preferred_element_type=jnp.float32)
        term = term + jnp.dot(activated[:, mlp_lo:mlp_lo + mlp_block], w_out_mlp[mlp_lo:mlp_lo + mlp_block], preferred_element_type=jnp.float32)
        rounded = lax.optimization_barrier(term.astype(jnp.bfloat16))
        branch = branch + rounded.astype(jnp.float32)
    return step_sizes[t_index] * (gate_mod * branch)

def reference(trajectory, x_start, t_idx, mod_table, step_sizes, q_gain, k_gain, w_qkv, w_mlp_in, w_out_attn, w_out_mlp):

    def slot_drift(pair):
        return one_slot(pair[0], pair[1], mod_table, step_sizes, q_gain, k_gain, w_qkv, w_mlp_in, w_out_attn, w_out_mlp)
    drifts = lax.map(slot_drift, (trajectory, t_idx))
    return x_start[None] + jnp.cumsum(drifts, axis=0)
```

```python
import functools
import math

import jax
import jax.numpy as jnp
from jax import lax
from jax.experimental import pallas as pl
from jax.experimental.pallas import tpu as pltpu
from jax.sharding import PartitionSpec as P

eps = 1e-06
f32 = jnp.float32
bf16 = jnp.bfloat16
VM = pltpu.VMEM
VMEM_BYTES = 48 * 1024 * 1024


def params():
    return pltpu.CompilerParams(vmem_limit_bytes=VMEM_BYTES)


def norm_kernel(t_ref, x_ref, mod_ref, size_ref, m_ref, sg_ref):
    width = x_ref.shape[-1]
    row = lax.rem(t_ref[0], 8)
    shift = mod_ref[pl.ds(row, 1), :width]
    scale = mod_ref[pl.ds(row, 1), width : 2 * width]
    gate = mod_ref[pl.ds(row, 1), 2 * width :]
    sg_ref[...] = size_ref[t_ref[0]] * gate
    x = x_ref[0]
    center = x - jnp.mean(x, axis=-1, keepdims=True)
    spread = jnp.mean(center * center, axis=-1, keepdims=True)
    m_ref[...] = (center * lax.rsqrt(spread + eps) * (1.0 + scale) + shift).astype(bf16)


def norm_call(t_idx, trajectory, mod_table, step_sizes):
    _, rows, width = trajectory.shape
    block = 64
    return pl.pallas_call(
        norm_kernel,
        grid_spec=pltpu.PrefetchScalarGridSpec(
            num_scalar_prefetch=1,
            grid=(rows // block,),
            in_specs=[
                pl.BlockSpec((1, block, width), lambda i, t: (0, i, 0)),
                pl.BlockSpec((8, 3 * width), lambda i, t: (t[0] // 8, 0)),
                pl.BlockSpec(memory_space=pltpu.SMEM),
            ],
            out_specs=[
                pl.BlockSpec((block, width), lambda i, t: (i, 0)),
                pl.BlockSpec((1, width), lambda i, t: (0, 0)),
            ],
        ),
        out_shape=[
            jax.ShapeDtypeStruct((rows, width), bf16),
            jax.ShapeDtypeStruct((1, width), f32),
        ],
        compiler_params=params(),
        name="norm",
    )(t_idx, trajectory, mod_table, step_sizes)


def project_kernel(tile, m0, m1, qg, kg, wq_hbm, wm_hbm, q, k, v, act, rows, wq, wm, sem_q, sem_m):
    half = m0.shape[0]
    head = qg.shape[1]
    n_q = wq.shape[2] // tile
    n_m = wm.shape[1] // tile
    copies = []
    for which in range(3):
        for i in range(n_q):
            cols = pl.ds(i * tile, tile)
            copies.append(
                pltpu.make_async_copy(
                    wq_hbm.at[which, :, cols], wq.at[which, :, cols], sem_q.at[which * n_q + i]
                )
            )
    for i in range(n_m):
        cols = pl.ds(i * tile, tile)
        copies.append(pltpu.make_async_copy(wm_hbm.at[:, cols], wm.at[:, cols], sem_m.at[i]))
    for copy in copies:
        copy.start()
    rows[:half] = m0[...]
    rows[half:] = m1[...]
    x = rows[...]

    def normed(y, gain):
        parts = []
        for h in range(tile // head):
            one = y[:, h * head : (h + 1) * head]
            square = jnp.mean(one * one, axis=-1, keepdims=True)
            parts.append((one * lax.rsqrt(square + eps) * gain).astype(bf16))
        return jnp.concatenate(parts, axis=1)

    for which in range(3):
        for i in range(n_q):
            copies[which * n_q + i].wait()
            cols = slice(i * tile, (i + 1) * tile)
            y = jnp.dot(x, wq[which, :, cols], preferred_element_type=f32)
            if which == 0:
                q[:, cols] = normed(y, qg[...])
            elif which == 1:
                k[:, cols] = normed(y, kg[...])
            else:
                v[:, cols] = y.astype(bf16)
    for i in range(n_m):
        copies[3 * n_q + i].wait()
        cols = slice(i * tile, (i + 1) * tile)
        y = jnp.dot(x, wm[:, cols], preferred_element_type=f32)
        act[:, cols] = jax.nn.gelu(y, approximate=True).astype(bf16)


def project_call(m0, m1, q_gain, k_gain, w_qkv, w_mlp_in):
    half, width = m0.shape
    heads = w_qkv.shape[2]
    hidden = w_mlp_in.shape[1]
    tile = 256
    rows = 2 * half
    vm = pl.BlockSpec(memory_space=VM)
    hbm = pl.BlockSpec(memory_space=pl.ANY)
    return pl.pallas_call(
        functools.partial(project_kernel, tile),
        in_specs=[vm, vm, vm, vm, hbm, hbm],
        out_specs=[vm] * 4,
        out_shape=[jax.ShapeDtypeStruct((rows, heads), bf16)] * 3
        + [jax.ShapeDtypeStruct((rows, hidden), bf16)],
        scratch_shapes=[
            VM((rows, width), bf16),
            VM((3, width, heads), bf16),
            VM((width, hidden), bf16),
            pltpu.SemaphoreType.DMA((3 * heads // tile,)),
            pltpu.SemaphoreType.DMA((hidden // tile,)),
        ],
        compiler_params=params(),
        name="project",
    )(m0, m1, q_gain, k_gain, w_qkv, w_mlp_in)


def attend_kernel(pairs, head, *refs):
    q_ref = refs[0]
    k_refs = refs[1 : 1 + pairs]
    v_refs = refs[1 + pairs : 1 + 2 * pairs]
    out = refs[1 + 2 * pairs]
    scale = math.log2(math.e) / math.sqrt(head)
    for h in range(q_ref.shape[1] // head):
        cols = slice(h * head, (h + 1) * head)
        q = q_ref[:, cols]
        scores = [
            lax.dot_general(q, k[:, cols], (((1,), (1,)), ((), ())), preferred_element_type=f32)
            for k in k_refs
        ]
        top = functools.reduce(
            jnp.maximum, [jnp.max(s, axis=-1, keepdims=True) for s in scores]
        )
        weights = [jnp.exp2((s - top) * scale) for s in scores]
        total = sum(jnp.sum(w, axis=-1, keepdims=True) for w in weights)
        inverse = 1.0 / total
        mixed = sum(
            jnp.dot((w * inverse).astype(bf16), v[:, cols], preferred_element_type=f32)
            for w, v in zip(weights, v_refs)
        )
        out[:, cols] = mixed.astype(bf16)


def attend_call(q, ks, vs, head):
    vm = pl.BlockSpec(memory_space=VM)
    return pl.pallas_call(
        functools.partial(attend_kernel, len(ks), head),
        in_specs=[vm] * (1 + 2 * len(ks)),
        out_specs=vm,
        out_shape=jax.ShapeDtypeStruct(q.shape, bf16),
        compiler_params=params(),
        name="attend",
    )(q, *ks, *vs)


def out_kernel(tile, first, a, b, wa_hbm, wb_hbm, keep, send, wa, wb, sem_a, sem_b):
    half = keep.shape[0]
    n = keep.shape[1] // tile
    copies = []
    for i in range(n):
        here = pl.ds(i * tile, tile)
        there = pl.ds(first + i * tile, tile)
        copies.append(
            (
                pltpu.make_async_copy(wa_hbm.at[:, there], wa.at[:, here], sem_a.at[i]),
                pltpu.make_async_copy(wb_hbm.at[:, there], wb.at[:, here], sem_b.at[i]),
            )
        )
    for pair in copies:
        pair[0].start()
        pair[1].start()
    for i in range(n):
        cols = slice(i * tile, (i + 1) * tile)
        copies[i][0].wait()
        copies[i][1].wait()
        y = jnp.dot(a[...], wa[:, cols], preferred_element_type=f32)
        y = y + jnp.dot(b[...], wb[:, cols], preferred_element_type=f32)
        keep[:, cols] = y[:half]
        send[:, cols] = y[half:].astype(bf16)


def out_call(a, b, w_out_attn, w_out_mlp, first, count):
    half = a.shape[0] // 2
    tile = 256
    vm = pl.BlockSpec(memory_space=VM)
    hbm = pl.BlockSpec(memory_space=pl.ANY)
    return pl.pallas_call(
        functools.partial(out_kernel, tile, first),
        in_specs=[vm, vm, hbm, hbm],
        out_specs=[vm, vm],
        out_shape=[
            jax.ShapeDtypeStruct((half, count), f32),
            jax.ShapeDtypeStruct((half, count), bf16),
        ],
        scratch_shapes=[
            VM((a.shape[1], count), bf16),
            VM((b.shape[1], count), bf16),
            pltpu.SemaphoreType.DMA((count // tile,)),
            pltpu.SemaphoreType.DMA((count // tile,)),
        ],
        compiler_params=params(),
        name="project_out",
    )(a, b, w_out_attn, w_out_mlp)


def per_device(
    n_step,
    n_seq,
    trajectory,
    x_start,
    t_idx,
    mod_table,
    step_sizes,
    q_gain,
    k_gain,
    w_qkv,
    w_mlp_in,
    w_out_attn,
    w_out_mlp,
):
    head = q_gain.shape[0]
    rows, width = x_start.shape
    chips = n_seq // 2
    groups = n_step // 2
    chunks = 4
    count = width // chunks
    half = rows // 2
    qg, kg = q_gain[None, :], k_gain[None, :]

    def to_core(x):
        return lax.ppermute(x, "seq", [(i, i ^ 1) for i in range(n_seq)])

    def to_chip(x, offset):
        return lax.ppermute(x, "seq", [(i, (i + 2 * offset) % n_seq) for i in range(n_seq)])

    def to_pair(x):
        return lax.ppermute(x, "step", [(i, i ^ 1) for i in range(n_step)])

    mine, sg = norm_call(t_idx, trajectory, mod_table, step_sizes)
    blocks = [mine] + [to_chip(mine, j) for j in range(1, chips)]
    pairs = [(block, to_core(block)) for block in blocks]
    projected = [project_call(a, b, qg, kg, w_qkv, w_mlp_in) for a, b in pairs]
    ks = [p[1] for p in projected]
    vs = [p[2] for p in projected]

    parity = lax.rem(lax.axis_index("step"), 2)
    order = list(range(1, chips)) + [0]
    attended = {j: attend_call(projected[j][0], ks, vs, head) for j in order}

    results = []
    for c in range(chunks):
        first = c * count
        sums = {}
        for j in order:
            keep, send = out_call(attended[j], projected[j][3], w_out_attn, w_out_mlp, first, count)
            sums[j] = keep + to_core(send).astype(f32)
        branch = sums[0]
        for j in range(1, chips):
            branch = branch + to_chip(sums[j].astype(bf16), chips - j).astype(f32)
        drift = sg[:, first : first + count] * branch
        kept = lax.dynamic_slice_in_dim(drift, parity * half, half, 0)
        other = lax.dynamic_slice_in_dim(drift, (1 - parity) * half, half, 0)
        got = to_pair(other.astype(bf16)).astype(f32)
        total = kept + got
        earlier = jnp.zeros_like(total)
        for g in range(1, groups):
            moves = [(2 * (g - 1) + x, 2 * g + x) for x in range(2)]
            earlier = earlier + lax.ppermute((earlier + total).astype(bf16), "step", moves).astype(f32)
        even = (parity == 0).astype(f32)
        back = to_pair((earlier + even * kept).astype(bf16)).astype(f32)
        own = earlier + kept + (1.0 - even) * got
        rest = back + other
        low = jnp.where(parity == 0, own, rest)
        high = jnp.where(parity == 0, rest, own)
        results.append(x_start[:, first : first + count] + jnp.concatenate([low, high], axis=0))
    return jnp.concatenate(results, axis=1)[None]


def solution(mesh):
    placed = (
        P("step", "seq", None),
        P("seq", None),
        P("step"),
        P(),
        P(),
        P(),
        P(),
        P(None, None, "seq"),
        P(None, "seq"),
        P("seq", None),
        P("seq", None),
    )
    return jax.shard_map(
        functools.partial(per_device, mesh.shape["step"], mesh.shape["seq"]),
        mesh=mesh,
        in_specs=placed,
        out_specs=P("step", "seq", None),
        check_vma=False,
    )
```

```python
import functools
import math

import jax
import jax.numpy as jnp
from jax import lax
from jax.experimental import pallas as pl
from jax.experimental.pallas import tpu as pltpu
from jax.sharding import PartitionSpec as P

eps = 1e-06
f32 = jnp.float32
bf16 = jnp.bfloat16
VM = pltpu.VMEM
MIB = 1024 * 1024


def params(mib):
    return pltpu.CompilerParams(vmem_limit_bytes=mib * MIB)


def cost(flops, moved):
    return pl.CostEstimate(flops=flops, transcendentals=0, bytes_accessed=moved)


def norm_kernel(t_ref, x_hbm, mod_ref, size_ref, m_ref, sg_ref, x_ref, sem):
    width = x_hbm.shape[-1]
    pieces = sem.shape[0]
    block = x_hbm.shape[1] // pieces
    copies = []
    for i in range(pieces):
        here = pl.ds(i * block, block)
        copies.append(pltpu.make_async_copy(x_hbm.at[0, here, :], x_ref.at[here, :], sem.at[i]))
        copies[i].start()
    row = lax.rem(t_ref[0], 8)
    shift = mod_ref[pl.ds(row, 1), :width]
    scale = 1.0 + mod_ref[pl.ds(row, 1), width : 2 * width]
    gate = mod_ref[pl.ds(row, 1), 2 * width :]
    sg_ref[...] = size_ref[t_ref[0]] * gate
    for i in range(pieces):
        copies[i].wait()
        here = slice(i * block, (i + 1) * block)
        x = x_ref[here, :]
        center = x - jnp.mean(x, axis=-1, keepdims=True)
        spread = jnp.mean(center * center, axis=-1, keepdims=True)
        m_ref[here, :] = (center * lax.rsqrt(spread + eps) * scale + shift).astype(bf16)


def norm_call(t_idx, trajectory, mod_table, step_sizes):
    _, rows, width = trajectory.shape
    return pl.pallas_call(
        norm_kernel,
        grid_spec=pltpu.PrefetchScalarGridSpec(
            num_scalar_prefetch=1,
            grid=(1,),
            in_specs=[
                pl.BlockSpec(memory_space=pltpu.HBM),
                pl.BlockSpec((8, 3 * width), lambda i, t: (t[0] // 8, 0)),
                pl.BlockSpec(memory_space=pltpu.SMEM),
            ],
            out_specs=[
                pl.BlockSpec((rows, width), lambda i, t: (0, 0)),
                pl.BlockSpec((1, width), lambda i, t: (0, 0)),
            ],
            scratch_shapes=[VM((rows, width), f32), pltpu.SemaphoreType.DMA((4,))],
        ),
        out_shape=[
            jax.ShapeDtypeStruct((rows, width), bf16),
            jax.ShapeDtypeStruct((1, width), f32),
        ],
        compiler_params=params(60),
        cost_estimate=cost(10 * rows * width, 0),
        name="norm",
    )(t_idx, trajectory, mod_table, step_sizes)


def project_kernel(tile, m0, m1, qg, kg, wq_hbm, wm_hbm, q, k, v, act, rows, wq, wm, sem_q, sem_m):
    half = m0.shape[0]
    head = qg.shape[1]
    n_q = wq.shape[2] // tile
    n_m = wm.shape[1] // tile
    copies = []
    for which in range(3):
        for i in range(n_q):
            cols = pl.ds(i * tile, tile)
            copies.append(
                pltpu.make_async_copy(
                    wq_hbm.at[which, :, cols], wq.at[which, :, cols], sem_q.at[which * n_q + i]
                )
            )
    for i in range(n_m):
        cols = pl.ds(i * tile, tile)
        copies.append(pltpu.make_async_copy(wm_hbm.at[:, cols], wm.at[:, cols], sem_m.at[i]))
    for copy in copies:
        copy.start()
    rows[:half] = m0[...]
    rows[half:] = m1[...]

    def normed(y, gain):
        parts = []
        for h in range(tile // head):
            one = y[:, h * head : (h + 1) * head]
            square = jnp.mean(one * one, axis=-1, keepdims=True)
            parts.append((one * lax.rsqrt(square + eps) * gain).astype(bf16))
        return jnp.concatenate(parts, axis=1)

    for which in range(3):
        for i in range(n_q):
            copies[which * n_q + i].wait()
            cols = slice(i * tile, (i + 1) * tile)
            y = jnp.dot(rows[...], wq[which, :, cols], preferred_element_type=f32)
            if which == 0:
                q[:, cols] = normed(y, qg[...])
            elif which == 1:
                k[:, cols] = normed(y, kg[...])
            else:
                v[:, cols] = y.astype(bf16)
    for i in range(n_m):
        copies[3 * n_q + i].wait()
        cols = slice(i * tile, (i + 1) * tile)
        y = jnp.dot(rows[...], wm[:, cols], preferred_element_type=f32)
        act[:, cols] = jax.nn.gelu(y, approximate=True).astype(bf16)


def project_call(m0, m1, q_gain, k_gain, w_qkv, w_mlp_in):
    half, width = m0.shape
    heads = w_qkv.shape[2]
    hidden = w_mlp_in.shape[1]
    tile = min(512, heads)
    rows = 2 * half
    vm = pl.BlockSpec(memory_space=VM)
    hbm = pl.BlockSpec(memory_space=pltpu.HBM)
    return pl.pallas_call(
        functools.partial(project_kernel, tile),
        in_specs=[vm, vm, vm, vm, hbm, hbm],
        out_specs=[vm] * 4,
        out_shape=[jax.ShapeDtypeStruct((rows, heads), bf16)] * 3
        + [jax.ShapeDtypeStruct((rows, hidden), bf16)],
        scratch_shapes=[
            VM((rows, width), bf16),
            VM((3, width, heads), bf16),
            VM((width, hidden), bf16),
            pltpu.SemaphoreType.DMA((3 * heads // tile,)),
            pltpu.SemaphoreType.DMA((hidden // tile,)),
        ],
        compiler_params=params(46),
        cost_estimate=cost(2 * rows * width * (3 * heads + hidden), 0),
        name="project",
    )(m0, m1, q_gain, k_gain, w_qkv, w_mlp_in)


def attend_kernel(pairs, head, *refs):
    q_ref = refs[0]
    k_refs = refs[1 : 1 + pairs]
    v_refs = refs[1 + pairs : 1 + 2 * pairs]
    out = refs[1 + 2 * pairs]
    scale = math.log2(math.e) / math.sqrt(head)
    for h in range(q_ref.shape[1] // head):
        cols = slice(h * head, (h + 1) * head)
        q = q_ref[:, cols]
        scores = [
            lax.dot_general(q, k[:, cols], (((1,), (1,)), ((), ())), preferred_element_type=f32)
            for k in k_refs
        ]
        top = functools.reduce(
            jnp.maximum, [jnp.max(s, axis=-1, keepdims=True) for s in scores]
        )
        weights = [jnp.exp2((s - top) * scale) for s in scores]
        total = sum(jnp.sum(w, axis=-1, keepdims=True) for w in weights)
        inverse = 1.0 / total
        mixed = sum(
            jnp.dot((w * inverse).astype(bf16), v[:, cols], preferred_element_type=f32)
            for w, v in zip(weights, v_refs)
        )
        out[:, cols] = mixed.astype(bf16)


def attend_call(q, ks, vs, head):
    vm = pl.BlockSpec(memory_space=VM)
    return pl.pallas_call(
        functools.partial(attend_kernel, len(ks), head),
        in_specs=[vm] * (1 + 2 * len(ks)),
        out_specs=vm,
        out_shape=jax.ShapeDtypeStruct(q.shape, bf16),
        compiler_params=params(46),
        cost_estimate=cost(4 * len(ks) * q.shape[0] ** 2 * q.shape[1] * 3, 0),
        name="attend",
    )(q, *ks, *vs)


def out_kernel(first, parts, *refs):
    xs, ws, extra = refs[:parts], refs[parts : 2 * parts], refs[2 * parts : -3 - parts]
    keep, send = refs[-3 - parts], refs[-2 - parts]
    held, sem = refs[-1 - parts : -1], refs[-1]
    half, count = keep.shape
    piece = 512
    there = pl.ds(first, count)
    copies = []
    for w, to in zip(ws, held):
        for at in range(0, w.shape[0], piece):
            here = pl.ds(at, min(piece, w.shape[0] - at))
            copies.append(
                pltpu.make_async_copy(w.at[here, there], to.at[here, :], sem.at[len(copies)])
            )
            copies[-1].start()
    turn = 0
    y = None
    for x, to in zip(xs, held):
        for at in range(0, to.shape[0], piece):
            here = slice(at, min(at + piece, to.shape[0]))
            copies[turn].wait()
            turn += 1
            term = jnp.dot(x[:, here], to[here, :], preferred_element_type=f32)
            y = term if y is None else y + term
    low, high = y[:half], y[half:]
    if extra:
        low = low + extra[0][:, first : first + count]
        high = high + extra[1][:, first : first + count]
    keep[...] = low
    send[...] = high.astype(send.dtype)


def out_call(xs, ws, extra, first, count, kind):
    half = xs[0].shape[0] // 2
    depth = sum(x.shape[1] for x in xs)
    vm = pl.BlockSpec(memory_space=VM)
    hbm = pl.BlockSpec(memory_space=pltpu.HBM)
    return pl.pallas_call(
        functools.partial(out_kernel, first, len(xs)),
        in_specs=[vm] * len(xs) + [hbm] * len(ws) + [vm] * len(extra),
        out_specs=[vm, vm],
        out_shape=[
            jax.ShapeDtypeStruct((half, count), f32),
            jax.ShapeDtypeStruct((half, count), kind),
        ],
        scratch_shapes=[VM((x.shape[1], count), bf16) for x in xs]
        + [pltpu.SemaphoreType.DMA((sum(-(-x.shape[1] // 512) for x in xs),))],
        compiler_params=params(46),
        cost_estimate=cost(4 * half * count * depth, 0),
        name="project_out",
    )(*xs, *ws, *extra)


def per_device(
    n_step,
    n_seq,
    trajectory,
    x_start,
    t_idx,
    mod_table,
    step_sizes,
    q_gain,
    k_gain,
    w_qkv,
    w_mlp_in,
    w_out_attn,
    w_out_mlp,
):
    head = q_gain.shape[0]
    rows, width = x_start.shape
    chips = n_seq // 2
    groups = n_step // 2
    chunks = 4
    count = width // chunks
    half = rows // 2
    qg, kg = q_gain[None, :], k_gain[None, :]

    def to_core(x):
        return lax.ppermute(x, "seq", [(i, i ^ 1) for i in range(n_seq)])

    def to_chip(x, offset):
        return lax.ppermute(x, "seq", [(i, (i + 2 * offset) % n_seq) for i in range(n_seq)])

    def to_pair(x):
        return lax.ppermute(x, "step", [(i, i ^ 1) for i in range(n_step)])

    def tied(*values):
        return lax.optimization_barrier(values)

    parity = lax.rem(lax.axis_index("step"), 2)
    even = (parity == 0).astype(f32)
    offsets = range(1, chips)

    mine, sg = norm_call(t_idx, trajectory, mod_table, step_sizes)
    far = [to_chip(mine, j) for j in offsets]
    q0, k0, v0, act0 = project_call(mine, to_core(mine), qg, kg, w_qkv, w_mlp_in)
    low0, high0 = out_call([act0], [w_out_mlp], [], 0, width, f32)
    far, low0, high0 = tied(far, low0, high0)
    qs, ks, vs, acts = [], [k0], [v0], []
    for block in far:
        q, k, v, act = project_call(block, to_core(block), qg, kg, w_qkv, w_mlp_in)
        qs.append(q)
        ks.append(k)
        vs.append(v)
        acts.append(act)
    mixed = [attend_call(q, ks, vs, head) for q in qs]

    firsts = [c * count for c in range(chunks)]
    weights = [w_out_attn, w_out_mlp]
    sums = [[] for _ in offsets]
    ready = [[] for _ in offsets]
    gate = (mixed, acts)
    for c, first in enumerate(firsts):
        for j in range(chips - 1):
            keep, send = out_call([gate[0][j], gate[1][j]], weights, [], first, count, bf16)
            sums[j].append((keep, to_core(send)))
        if c >= 1:
            for j in range(chips - 1):
                keep, send = sums[j][c - 1]
                ready[j].append((keep + send.astype(f32)).astype(bf16))
            recent = [r[-1] for r in ready]
            now = [x[-1][0] for x in sums]
            gate, recent, now = tied(gate, recent, now)
            for j in range(chips - 1):
                ready[j][-1] = recent[j]
                sums[j][-1] = (now[j], sums[j][-1][1])
    for j in range(chips - 1):
        keep, send = sums[j][-1]
        ready[j].append((keep + send.astype(f32)).astype(bf16))
    q0, ready = tied(q0, ready)
    got = [[to_chip(r, chips - 1 - j) for r in ready[j]] for j in range(chips - 1)]
    mixed0 = attend_call(q0, ks, vs, head)
    early = [row[:2] for row in got]
    mixed0, early = tied(mixed0, early)
    got = [e + row[2:] for e, row in zip(early, got)]
    keep0, send0 = out_call([mixed0], [w_out_attn], [low0, high0], 0, width, bf16)
    own = keep0 + to_core(send0).astype(f32)

    def prefix_stages(c):
        first = firsts[c]
        held = {}

        def drift_of(fetched):
            branch = own[:, first : first + count]
            for one in fetched:
                branch = branch + one.astype(f32)
            drift = sg[:, first : first + count] * branch
            held["kept"] = lax.dynamic_slice_in_dim(drift, parity * half, half, 0)
            held["other"] = lax.dynamic_slice_in_dim(drift, (1 - parity) * half, half, 0)
            return held["other"].astype(bf16)

        def pair_sum(fetched):
            held["fetched"] = fetched.astype(f32)
            held["total"] = held["kept"] + held["fetched"]
            held["earlier"] = jnp.zeros_like(held["total"])
            if groups > 1:
                return held["total"].astype(bf16)
            return (even * held["kept"]).astype(bf16)

        def hop(g, fetched):
            held["earlier"] = held["earlier"] + fetched.astype(f32)
            if g < groups - 1:
                return (held["earlier"] + held["total"]).astype(bf16)
            return (held["earlier"] + even * held["kept"]).astype(bf16)

        def finish(fetched):
            mine_half = held["earlier"] + held["kept"] + (1.0 - even) * held["fetched"]
            rest = fetched.astype(f32) + held["other"]
            low = jnp.where(parity == 0, mine_half, rest)
            high = jnp.where(parity == 0, rest, mine_half)
            return x_start[:, first : first + count] + jnp.concatenate([low, high], axis=0)

        def along(g):
            moves = [(2 * (g - 1) + x, 2 * g + x) for x in range(2)]
            return lambda x: lax.ppermute(x, "step", moves)

        stages = [(drift_of, to_pair)]
        stages.append((pair_sum, along(1) if groups > 1 else to_pair))
        for g in range(1, groups):
            stages.append((functools.partial(hop, g), along(g + 1) if g < groups - 1 else to_pair))
        stages.append((finish, None))
        return stages

    plan = [prefix_stages(c) for c in range(chunks)]
    inbox = [[got[j][c] for j in range(chips - 1)] for c in range(chunks)]
    turns = sorted(
        (4 * c + 3 * i, i, c) for c in range(chunks) for i in range(len(plan[c]))
    )
    results = [None] * chunks
    last = None
    for _, i, c in turns:
        compute, move = plan[c][i]
        fetched = inbox[c]
        if last is not None:
            fetched, last = tied(fetched, last)
        out = compute(fetched)
        if move is None:
            results[c] = out
        else:
            inbox[c] = move(out)
            last = out
    return jnp.concatenate(results, axis=1)[None]


def solution(mesh):
    placed = (
        P("step", "seq", None),
        P("seq", None),
        P("step"),
        P(),
        P(),
        P(),
        P(),
        P(None, None, "seq"),
        P(None, "seq"),
        P("seq", None),
        P("seq", None),
    )
    return jax.shard_map(
        functools.partial(per_device, mesh.shape["step"], mesh.shape["seq"]),
        mesh=mesh,
        in_specs=placed,
        out_specs=P("step", "seq", None),
        check_vma=False,
    )
```

```python
import functools
import math

import jax
import jax.numpy as jnp
from jax import lax
from jax.experimental import pallas as pl
from jax.experimental.pallas import tpu as pltpu
from jax.sharding import PartitionSpec as P

eps = 1e-06
f32 = jnp.float32
bf16 = jnp.bfloat16
VM = pltpu.VMEM
MIB = 1024 * 1024


def params(mib):
    return pltpu.CompilerParams(vmem_limit_bytes=mib * MIB)


def cost(flops, moved):
    return pl.CostEstimate(flops=flops, transcendentals=0, bytes_accessed=moved)


def norm_kernel(t_ref, x_hbm, mod_ref, size_ref, m_ref, sg_ref, x_ref, sem):
    width = x_hbm.shape[-1]
    pieces = sem.shape[0]
    block = x_hbm.shape[1] // pieces
    copies = []
    for i in range(pieces):
        here = pl.ds(i * block, block)
        copies.append(pltpu.make_async_copy(x_hbm.at[0, here, :], x_ref.at[here, :], sem.at[i]))
        copies[i].start()
    row = lax.rem(t_ref[0], 8)
    shift = mod_ref[pl.ds(row, 1), :width]
    scale = 1.0 + mod_ref[pl.ds(row, 1), width : 2 * width]
    gate = mod_ref[pl.ds(row, 1), 2 * width :]
    sg_ref[...] = size_ref[t_ref[0]] * gate
    for i in range(pieces):
        copies[i].wait()
        here = slice(i * block, (i + 1) * block)
        x = x_ref[here, :]
        center = x - jnp.mean(x, axis=-1, keepdims=True)
        spread = jnp.mean(center * center, axis=-1, keepdims=True)
        m_ref[here, :] = (center * lax.rsqrt(spread + eps) * scale + shift).astype(bf16)


def norm_call(t_idx, trajectory, mod_table, step_sizes):
    _, rows, width = trajectory.shape
    return pl.pallas_call(
        norm_kernel,
        grid_spec=pltpu.PrefetchScalarGridSpec(
            num_scalar_prefetch=1,
            grid=(1,),
            in_specs=[
                pl.BlockSpec(memory_space=pltpu.HBM),
                pl.BlockSpec((8, 3 * width), lambda i, t: (t[0] // 8, 0)),
                pl.BlockSpec(memory_space=pltpu.SMEM),
            ],
            out_specs=[
                pl.BlockSpec((rows, width), lambda i, t: (0, 0)),
                pl.BlockSpec((1, width), lambda i, t: (0, 0)),
            ],
            scratch_shapes=[VM((rows, width), f32), pltpu.SemaphoreType.DMA((4,))],
        ),
        out_shape=[
            jax.ShapeDtypeStruct((rows, width), bf16),
            jax.ShapeDtypeStruct((1, width), f32),
        ],
        compiler_params=params(60),
        cost_estimate=cost(10 * rows * width, 0),
        name="norm",
    )(t_idx, trajectory, mod_table, step_sizes)


def project_kernel(tile, load, tiles, m0, m1, qg, kg, *refs):
    if load:
        wq_hbm, wm_hbm, q, k, v, act = refs[:6]
        held, rows, sem = refs[6:-2], refs[-2], refs[-1]
    else:
        held = refs[:tiles]
        q, k, v, act, rows = refs[tiles:]
    half = m0.shape[0]
    head = qg.shape[1]
    n_q = q.shape[1] // tile
    copies = []
    if load:
        for i in range(tiles):
            if i < 3 * n_q:
                source = wq_hbm.at[i // n_q, :, pl.ds(i % n_q * tile, tile)]
            else:
                source = wm_hbm.at[:, pl.ds((i - 3 * n_q) * tile, tile)]
            copies.append(pltpu.make_async_copy(source, held[i], sem.at[i]))
            copies[i].start()
    rows[:half] = m0[...]
    rows[half:] = m1[...]

    def normed(y, gain):
        parts = []
        for h in range(tile // head):
            one = y[:, h * head : (h + 1) * head]
            square = jnp.mean(one * one, axis=-1, keepdims=True)
            parts.append((one * lax.rsqrt(square + eps) * gain).astype(bf16))
        return jnp.concatenate(parts, axis=1)

    for i in range(tiles):
        if load:
            copies[i].wait()
        y = jnp.dot(rows[...], held[i][...], preferred_element_type=f32)
        cols = slice(i % n_q * tile, (i % n_q + 1) * tile)
        if i < n_q:
            q[:, cols] = normed(y, qg[...])
        elif i < 2 * n_q:
            k[:, cols] = normed(y, kg[...])
        elif i < 3 * n_q:
            v[:, cols] = y.astype(bf16)
        else:
            cols = slice((i - 3 * n_q) * tile, (i - 3 * n_q + 1) * tile)
            act[:, cols] = jax.nn.gelu(y, approximate=True).astype(bf16)


def project_call(m0, m1, q_gain, k_gain, w_qkv, w_mlp_in, held):
    half, width = m0.shape
    heads = w_qkv.shape[2]
    hidden = w_mlp_in.shape[1]
    tile = min(512, heads)
    tiles = (3 * heads + hidden) // tile
    rows = 2 * half
    load = held is None
    vm = pl.BlockSpec(memory_space=VM)
    hbm = pl.BlockSpec(memory_space=pltpu.HBM)
    shapes = [jax.ShapeDtypeStruct((rows, heads), bf16)] * 3
    shapes.append(jax.ShapeDtypeStruct((rows, hidden), bf16))
    scratch = [VM((rows, width), bf16)]
    if load:
        shapes += [jax.ShapeDtypeStruct((width, tile), bf16)] * tiles
        scratch.append(pltpu.SemaphoreType.DMA((tiles,)))
    return pl.pallas_call(
        functools.partial(project_kernel, tile, load, tiles),
        in_specs=[vm] * 4 + ([hbm] * 2 if load else [vm] * tiles),
        out_specs=[vm] * len(shapes),
        out_shape=shapes,
        scratch_shapes=scratch,
        compiler_params=params(26 if load else 9),
        cost_estimate=cost(2 * rows * width * (3 * heads + hidden), 0),
        name="project",
    )(m0, m1, q_gain, k_gain, *([w_qkv, w_mlp_in] if load else held))


def attend_kernel(pairs, head, *refs):
    q_ref = refs[0]
    k_refs = refs[1 : 1 + pairs]
    v_refs = refs[1 + pairs : 1 + 2 * pairs]
    out = refs[1 + 2 * pairs]
    scale = math.log2(math.e) / math.sqrt(head)
    for h in range(q_ref.shape[1] // head):
        cols = slice(h * head, (h + 1) * head)
        q = q_ref[:, cols]
        scores = [
            lax.dot_general(q, k[:, cols], (((1,), (1,)), ((), ())), preferred_element_type=f32)
            for k in k_refs
        ]
        top = functools.reduce(
            jnp.maximum, [jnp.max(s, axis=-1, keepdims=True) for s in scores]
        )
        weights = [jnp.exp2((s - top) * scale) for s in scores]
        total = sum(jnp.sum(w, axis=-1, keepdims=True) for w in weights)
        inverse = 1.0 / total
        mixed = sum(
            jnp.dot((w * inverse).astype(bf16), v[:, cols], preferred_element_type=f32)
            for w, v in zip(weights, v_refs)
        )
        out[:, cols] = mixed.astype(bf16)


def attend_call(q, ks, vs, head):
    vm = pl.BlockSpec(memory_space=VM)
    return pl.pallas_call(
        functools.partial(attend_kernel, len(ks), head),
        in_specs=[vm] * (1 + 2 * len(ks)),
        out_specs=vm,
        out_shape=jax.ShapeDtypeStruct(q.shape, bf16),
        compiler_params=params(9),
        cost_estimate=cost(4 * len(ks) * q.shape[0] ** 2 * q.shape[1] * 3, 0),
        name="attend",
    )(q, *ks, *vs)


def out_kernel(first, parts, *refs):
    xs, ws = refs[:parts], refs[parts : 2 * parts]
    keep, send = refs[-2:]
    half, count = keep.shape
    cols = slice(first, first + count)
    terms = [
        jnp.dot(x[...], w[:, cols], preferred_element_type=f32) for x, w in zip(xs, ws)
    ]
    y = functools.reduce(jnp.add, terms)
    keep[...] = y[:half]
    send[...] = y[half:].astype(bf16)


def out_call(xs, ws, first, count):
    half = xs[0].shape[0] // 2
    depth = sum(x.shape[1] for x in xs)
    vm = pl.BlockSpec(memory_space=VM)
    return pl.pallas_call(
        functools.partial(out_kernel, first, len(xs)),
        in_specs=[vm] * (2 * len(xs)),
        out_specs=[vm, vm],
        out_shape=[
            jax.ShapeDtypeStruct((half, count), f32),
            jax.ShapeDtypeStruct((half, count), bf16),
        ],
        compiler_params=params(9),
        cost_estimate=cost(4 * half * count * depth, 0),
        name="project_out",
    )(*xs, *ws)


def per_device(
    n_step,
    n_seq,
    trajectory,
    x_start,
    t_idx,
    mod_table,
    step_sizes,
    q_gain,
    k_gain,
    w_qkv,
    w_mlp_in,
    w_out_attn,
    w_out_mlp,
):
    head = q_gain.shape[0]
    rows, width = x_start.shape
    chips = n_seq // 2
    groups = n_step // 2
    chunks = 4
    count = width // chunks
    half = rows // 2
    qg, kg = q_gain[None, :], k_gain[None, :]

    def to_core(x):
        return lax.ppermute(x, "seq", [(i, i ^ 1) for i in range(n_seq)])

    def to_chip(x, offset):
        return lax.ppermute(x, "seq", [(i, (i + 2 * offset) % n_seq) for i in range(n_seq)])

    def to_pair(x):
        return lax.ppermute(x, "step", [(i, i ^ 1) for i in range(n_step)])

    def tied(*values):
        return lax.optimization_barrier(values)

    parity = lax.rem(lax.axis_index("step"), 2)
    even = (parity == 0).astype(f32)
    offsets = range(1, chips)

    mine, sg = norm_call(t_idx, trajectory, mod_table, step_sizes)
    far = [to_chip(mine, j) for j in offsets]
    q0, k0, v0, act0, *held = project_call(
        mine, to_core(mine), qg, kg, w_qkv, w_mlp_in, None
    )
    far, act0 = tied(far, act0)
    qs, ks, vs, acts = [], [k0], [v0], []
    for block in far:
        q, k, v, act = project_call(block, to_core(block), qg, kg, w_qkv, w_mlp_in, held)
        qs.append(q)
        ks.append(k)
        vs.append(v)
        acts.append(act)
    mixed = [attend_call(q, ks, vs, head) for q in qs]

    firsts = [c * count for c in range(chunks)]
    weights = [w_out_attn, w_out_mlp]
    sums = [[] for _ in offsets]
    ready = [[] for _ in offsets]
    gate = (mixed, acts)
    for c, first in enumerate(firsts):
        for j in range(chips - 1):
            keep, send = out_call([gate[0][j], gate[1][j]], weights, first, count)
            sums[j].append((keep, to_core(send)))
        if c >= 1:
            for j in range(chips - 1):
                keep, send = sums[j][c - 1]
                ready[j].append((keep + send.astype(f32)).astype(bf16))
            recent = [r[-1] for r in ready]
            now = [x[-1][0] for x in sums]
            gate, recent, now = tied(gate, recent, now)
            for j in range(chips - 1):
                ready[j][-1] = recent[j]
                sums[j][-1] = (now[j], sums[j][-1][1])
    for j in range(chips - 1):
        keep, send = sums[j][-1]
        ready[j].append((keep + send.astype(f32)).astype(bf16))
    q0, ready = tied(q0, ready)
    got = [[to_chip(r, chips - 1 - j) for r in ready[j]] for j in range(chips - 1)]
    mixed0 = attend_call(q0, ks, vs, head)
    early = [row[:2] for row in got]
    mixed0, early = tied(mixed0, early)
    got = [e + row[2:] for e, row in zip(early, got)]
    keep0, send0 = out_call([mixed0, act0], weights, 0, width)
    own = keep0 + to_core(send0).astype(f32)

    def prefix_stages(c):
        first = firsts[c]
        held = {}

        def drift_of(fetched):
            branch = own[:, first : first + count]
            for one in fetched:
                branch = branch + one.astype(f32)
            drift = sg[:, first : first + count] * branch
            held["kept"] = lax.dynamic_slice_in_dim(drift, parity * half, half, 0)
            held["other"] = lax.dynamic_slice_in_dim(drift, (1 - parity) * half, half, 0)
            return held["other"].astype(bf16)

        def pair_sum(fetched):
            held["fetched"] = fetched.astype(f32)
            held["total"] = held["kept"] + held["fetched"]
            held["earlier"] = jnp.zeros_like(held["total"])
            if groups > 1:
                return held["total"].astype(bf16)
            return (even * held["kept"]).astype(bf16)

        def hop(g, fetched):
            held["earlier"] = held["earlier"] + fetched.astype(f32)
            if g < groups - 1:
                return (held["earlier"] + held["total"]).astype(bf16)
            return (held["earlier"] + even * held["kept"]).astype(bf16)

        def finish(fetched):
            mine_half = held["earlier"] + held["kept"] + (1.0 - even) * held["fetched"]
            rest = fetched.astype(f32) + held["other"]
            low = jnp.where(parity == 0, mine_half, rest)
            high = jnp.where(parity == 0, rest, mine_half)
            return x_start[:, first : first + count] + jnp.concatenate([low, high], axis=0)

        def along(g):
            moves = [(2 * (g - 1) + x, 2 * g + x) for x in range(2)]
            return lambda x: lax.ppermute(x, "step", moves)

        stages = [(drift_of, to_pair)]
        stages.append((pair_sum, along(1) if groups > 1 else to_pair))
        for g in range(1, groups):
            stages.append((functools.partial(hop, g), along(g + 1) if g < groups - 1 else to_pair))
        stages.append((finish, None))
        return stages

    plan = [prefix_stages(c) for c in range(chunks)]
    inbox = [[got[j][c] for j in range(chips - 1)] for c in range(chunks)]
    turns = sorted(
        (4 * c + 3 * i, i, c) for c in range(chunks) for i in range(len(plan[c]))
    )
    results = [None] * chunks
    last = None
    for _, i, c in turns:
        compute, move = plan[c][i]
        fetched = inbox[c]
        if last is not None:
            fetched, last = tied(fetched, last)
        out = compute(fetched)
        if move is None:
            results[c] = out
        else:
            inbox[c] = move(out)
            last = out
    return jnp.concatenate(results, axis=1)[None]


def solution(mesh):
    placed = (
        P("step", "seq", None),
        P("seq", None),
        P("step"),
        P(),
        P(),
        P(),
        P(),
        P(None, None, "seq"),
        P(None, "seq"),
        P("seq", None),
        P("seq", None),
    )
    return jax.shard_map(
        functools.partial(per_device, mesh.shape["step"], mesh.shape["seq"]),
        mesh=mesh,
        in_specs=placed,
        out_specs=P("step", "seq", None),
        check_vma=False,
    )
```

```python
import functools
import math

import jax
import jax.numpy as jnp
from jax import lax
from jax.experimental import pallas as pl
from jax.experimental.pallas import tpu as pltpu
from jax.sharding import PartitionSpec as P

eps = 1e-06
f32 = jnp.float32
bf16 = jnp.bfloat16
VM = pltpu.VMEM
MIB = 1024 * 1024


def params(mib):
    return pltpu.CompilerParams(vmem_limit_bytes=mib * MIB)


def cost(flops, moved):
    return pl.CostEstimate(flops=flops, transcendentals=0, bytes_accessed=moved)


def norm_kernel(t_ref, x_hbm, mod_ref, size_ref, m_ref, sg_ref, x_ref, sem):
    width = x_hbm.shape[-1]
    pieces = sem.shape[0]
    block = x_hbm.shape[1] // pieces
    copies = []
    for i in range(pieces):
        here = pl.ds(i * block, block)
        copies.append(pltpu.make_async_copy(x_hbm.at[0, here, :], x_ref.at[here, :], sem.at[i]))
        copies[i].start()
    row = lax.rem(t_ref[0], 8)
    shift = mod_ref[pl.ds(row, 1), :width]
    scale = 1.0 + mod_ref[pl.ds(row, 1), width : 2 * width]
    gate = mod_ref[pl.ds(row, 1), 2 * width :]
    sg_ref[...] = size_ref[t_ref[0]] * gate
    for i in range(pieces):
        copies[i].wait()
        here = slice(i * block, (i + 1) * block)
        x = x_ref[here, :]
        center = x - jnp.mean(x, axis=-1, keepdims=True)
        spread = jnp.mean(center * center, axis=-1, keepdims=True)
        m_ref[here, :] = (center * lax.rsqrt(spread + eps) * scale + shift).astype(bf16)


def norm_call(t_idx, trajectory, mod_table, step_sizes):
    _, rows, width = trajectory.shape
    return pl.pallas_call(
        norm_kernel,
        grid_spec=pltpu.PrefetchScalarGridSpec(
            num_scalar_prefetch=1,
            grid=(1,),
            in_specs=[
                pl.BlockSpec(memory_space=pltpu.HBM),
                pl.BlockSpec((8, 3 * width), lambda i, t: (t[0] // 8, 0)),
                pl.BlockSpec(memory_space=pltpu.SMEM),
            ],
            out_specs=[
                pl.BlockSpec((rows, width), lambda i, t: (0, 0)),
                pl.BlockSpec((1, width), lambda i, t: (0, 0)),
            ],
            scratch_shapes=[VM((rows, width), f32), pltpu.SemaphoreType.DMA((4,))],
        ),
        out_shape=[
            jax.ShapeDtypeStruct((rows, width), bf16),
            jax.ShapeDtypeStruct((1, width), f32),
        ],
        compiler_params=params(60),
        cost_estimate=cost(10 * rows * width, 0),
        name="norm",
    )(t_idx, trajectory, mod_table, step_sizes)


def project_kernel(tile, load, tiles, m0, m1, qg, kg, *refs):
    if load:
        wq_hbm, wm_hbm, q, k, v, act = refs[:6]
        held, rows, sem = refs[6:-2], refs[-2], refs[-1]
    else:
        held = refs[:tiles]
        q, k, v, act, rows = refs[tiles:]
    half = m0.shape[0]
    head = qg.shape[1]
    n_q = q.shape[1] // tile
    copies = []
    if load:
        for i in range(tiles):
            if i < 3 * n_q:
                source = wq_hbm.at[i // n_q, :, pl.ds(i % n_q * tile, tile)]
            else:
                source = wm_hbm.at[:, pl.ds((i - 3 * n_q) * tile, tile)]
            copies.append(pltpu.make_async_copy(source, held[i], sem.at[i]))
            copies[i].start()
    rows[:half] = m0[...]
    rows[half:] = m1[...]

    def normed(y, gain):
        parts = []
        for h in range(tile // head):
            one = y[:, h * head : (h + 1) * head]
            square = jnp.mean(one * one, axis=-1, keepdims=True)
            parts.append((one * lax.rsqrt(square + eps) * gain).astype(bf16))
        return jnp.concatenate(parts, axis=1)

    for i in range(tiles):
        if load:
            copies[i].wait()
        y = jnp.dot(rows[...], held[i][...], preferred_element_type=f32)
        cols = slice(i % n_q * tile, (i % n_q + 1) * tile)
        if i < n_q:
            q[:, cols] = normed(y, qg[...])
        elif i < 2 * n_q:
            k[:, cols] = normed(y, kg[...])
        elif i < 3 * n_q:
            v[:, cols] = y.astype(bf16)
        else:
            cols = slice((i - 3 * n_q) * tile, (i - 3 * n_q + 1) * tile)
            act[:, cols] = jax.nn.gelu(y, approximate=True).astype(bf16)


def project_call(m0, m1, q_gain, k_gain, w_qkv, w_mlp_in, held):
    half, width = m0.shape
    heads = w_qkv.shape[2]
    hidden = w_mlp_in.shape[1]
    tile = min(512, heads)
    tiles = (3 * heads + hidden) // tile
    rows = 2 * half
    load = held is None
    vm = pl.BlockSpec(memory_space=VM)
    hbm = pl.BlockSpec(memory_space=pltpu.HBM)
    shapes = [jax.ShapeDtypeStruct((rows, heads), bf16)] * 3
    shapes.append(jax.ShapeDtypeStruct((rows, hidden), bf16))
    scratch = [VM((rows, width), bf16)]
    if load:
        shapes += [jax.ShapeDtypeStruct((width, tile), bf16)] * tiles
        scratch.append(pltpu.SemaphoreType.DMA((tiles,)))
    return pl.pallas_call(
        functools.partial(project_kernel, tile, load, tiles),
        in_specs=[vm] * 4 + ([hbm] * 2 if load else [vm] * tiles),
        out_specs=[vm] * len(shapes),
        out_shape=shapes,
        scratch_shapes=scratch,
        compiler_params=params(30 if load else 9),
        cost_estimate=cost(2 * rows * width * (3 * heads + hidden), 0),
        name="project",
    )(m0, m1, q_gain, k_gain, *([w_qkv, w_mlp_in] if load else held))


def attend_kernel(pairs, head, *refs):
    q_ref = refs[0]
    k_refs = refs[1 : 1 + pairs]
    v_refs = refs[1 + pairs : 1 + 2 * pairs]
    out = refs[1 + 2 * pairs]
    scale = math.log2(math.e) / math.sqrt(head)
    for h in range(q_ref.shape[1] // head):
        cols = slice(h * head, (h + 1) * head)
        q = q_ref[:, cols]
        scores = [
            lax.dot_general(q, k[:, cols], (((1,), (1,)), ((), ())), preferred_element_type=f32)
            for k in k_refs
        ]
        top = functools.reduce(
            jnp.maximum, [jnp.max(s, axis=-1, keepdims=True) for s in scores]
        )
        weights = [jnp.exp2((s - top) * scale) for s in scores]
        total = sum(jnp.sum(w, axis=-1, keepdims=True) for w in weights)
        inverse = 1.0 / total
        mixed = sum(
            jnp.dot((w * inverse).astype(bf16), v[:, cols], preferred_element_type=f32)
            for w, v in zip(weights, v_refs)
        )
        out[:, cols] = mixed.astype(bf16)


def attend_call(q, ks, vs, head):
    vm = pl.BlockSpec(memory_space=VM)
    return pl.pallas_call(
        functools.partial(attend_kernel, len(ks), head),
        in_specs=[vm] * (1 + 2 * len(ks)),
        out_specs=vm,
        out_shape=jax.ShapeDtypeStruct(q.shape, bf16),
        compiler_params=params(9),
        cost_estimate=cost(4 * len(ks) * q.shape[0] ** 2 * q.shape[1] * 3, 0),
        name="attend",
    )(q, *ks, *vs)


def out_kernel(first, parts, *refs):
    xs, ws, extra = refs[:parts], refs[parts : 2 * parts], refs[2 * parts : -2]
    keep, send = refs[-2:]
    half, count = keep.shape
    cols = slice(first, first + count)
    terms = [
        jnp.dot(x[...], w[:, cols], preferred_element_type=f32) for x, w in zip(xs, ws)
    ]
    y = functools.reduce(jnp.add, terms)
    low, high = y[:half], y[half:]
    if extra:
        low = low + extra[0][:, cols]
        high = high + extra[1][:, cols]
    keep[...] = low
    send[...] = high.astype(send.dtype)


def out_call(xs, ws, extra, first, count, kind=bf16):
    half = xs[0].shape[0] // 2
    depth = sum(x.shape[1] for x in xs)
    vm = pl.BlockSpec(memory_space=VM)
    return pl.pallas_call(
        functools.partial(out_kernel, first, len(xs)),
        in_specs=[vm] * (2 * len(xs) + len(extra)),
        out_specs=[vm, vm],
        out_shape=[
            jax.ShapeDtypeStruct((half, count), f32),
            jax.ShapeDtypeStruct((half, count), kind),
        ],
        compiler_params=params(9),
        cost_estimate=cost(4 * half * count * depth, 0),
        name="project_out",
    )(*xs, *ws, *extra)


def per_device(
    n_step,
    n_seq,
    trajectory,
    x_start,
    t_idx,
    mod_table,
    step_sizes,
    q_gain,
    k_gain,
    w_qkv,
    w_mlp_in,
    w_out_attn,
    w_out_mlp,
):
    head = q_gain.shape[0]
    rows, width = x_start.shape
    chips = n_seq // 2
    groups = n_step // 2
    half = rows // 2
    unit = width // 24
    counts = [4 * unit, 8 * unit, 8 * unit, 4 * unit]
    chunks = len(counts)
    firsts = [sum(counts[:c]) for c in range(chunks)]
    qg, kg = q_gain[None, :], k_gain[None, :]

    def to_core(x):
        return lax.ppermute(x, "seq", [(i, i ^ 1) for i in range(n_seq)])

    def to_chip(x, offset):
        return lax.ppermute(x, "seq", [(i, (i + 2 * offset) % n_seq) for i in range(n_seq)])

    def to_pair(x):
        return lax.ppermute(x, "step", [(i, i ^ 1) for i in range(n_step)])

    def tied(*values):
        return lax.optimization_barrier(values)

    parity = lax.rem(lax.axis_index("step"), 2)
    even = (parity == 0).astype(f32)
    offsets = range(1, chips)

    mine, sg = norm_call(t_idx, trajectory, mod_table, step_sizes)
    far = [to_chip(mine, j) for j in offsets]
    q0, k0, v0, act0, *held = project_call(
        mine, to_core(mine), qg, kg, w_qkv, w_mlp_in, None
    )
    low0, high0 = out_call([act0], [w_out_mlp], [], 0, width, f32)
    far, low0, high0 = tied(far, low0, high0)
    qs, ks, vs, acts = [], [k0], [v0], []
    for block in far:
        q, k, v, act = project_call(block, to_core(block), qg, kg, w_qkv, w_mlp_in, held)
        qs.append(q)
        ks.append(k)
        vs.append(v)
        acts.append(act)
    mixed = [attend_call(q, ks, vs, head) for q in qs]

    weights = [w_out_attn, w_out_mlp]
    sums = [[] for _ in offsets]
    ready = [[] for _ in offsets]
    gate = (mixed, acts)
    for c in range(chunks):
        for j in range(chips - 1):
            keep, send = out_call([gate[0][j], gate[1][j]], weights, [], firsts[c], counts[c])
            sums[j].append((keep, to_core(send)))
        if c >= 1:
            for j in range(chips - 1):
                keep, send = sums[j][c - 1]
                ready[j].append((keep + send.astype(f32)).astype(bf16))
            recent = [r[-1] for r in ready]
            now = [x[-1][0] for x in sums]
            gate, recent, now = tied(gate, recent, now)
            for j in range(chips - 1):
                ready[j][-1] = recent[j]
                sums[j][-1] = (now[j], sums[j][-1][1])
    for j in range(chips - 1):
        keep, send = sums[j][-1]
        ready[j].append((keep + send.astype(f32)).astype(bf16))
    q0, ready = tied(q0, ready)
    got = [[to_chip(r, chips - 1 - j) for r in ready[j]] for j in range(chips - 1)]
    mixed0 = attend_call(q0, ks, vs, head)
    early = [row[0] for row in got]
    mixed0, early = tied(mixed0, early)
    got = [[e] + row[1:] for e, row in zip(early, got)]
    keep, send = out_call([mixed0], [w_out_attn], [low0, high0], 0, width)
    own = keep + to_core(send).astype(f32)

    def along(pairs):
        return lambda x: lax.ppermute(x, "step", [(2 * a + i, 2 * b + i) for a, b in pairs for i in (0, 1)])

    rounds = []
    span = 1
    while span < groups:
        moves = []
        for t in range(span):
            pairs = [(b + span - 1, b + span + t) for b in range(0, groups, 2 * span)]
            moves.append(along([p for p in pairs if p[1] < groups]))
        rounds.append(moves)
        span *= 2

    def prefix_stages(c, split):
        first = firsts[c]
        cols = slice(first, first + counts[c])
        held = {}

        def drift_of(fetched):
            branch = own[:, cols]
            for one in fetched:
                branch = branch + one.astype(f32)
            drift = sg[:, cols] * branch
            if split:
                held["kept"] = lax.dynamic_slice_in_dim(drift, parity * half, half, 0)
                held["other"] = lax.dynamic_slice_in_dim(drift, (1 - parity) * half, half, 0)
                return held["other"].astype(bf16)
            held["kept"] = held["total"] = drift
            return held["total"].astype(bf16)

        def pair_sum(fetched):
            held["fetched"] = fetched[0].astype(f32)
            held["total"] = held["kept"] + held["fetched"]
            return held["total"].astype(bf16)

        def collect(final, fetched):
            for one in fetched:
                one = one.astype(f32)
                held["earlier"] = held["earlier"] + one if "earlier" in held else one
            if final:
                return (held["earlier"] + even * held["kept"]).astype(bf16)
            return (held["earlier"] + held["total"]).astype(bf16)

        def finish(fetched):
            back = fetched[0].astype(f32)
            if split:
                mine_half = held["earlier"] + held["kept"] + (1.0 - even) * held["fetched"]
                rest = back + held["other"]
                low = jnp.where(parity == 0, mine_half, rest)
                high = jnp.where(parity == 0, rest, mine_half)
                change = jnp.concatenate([low, high], axis=0)
            else:
                change = held["earlier"] + held["kept"] + back
            return x_start[:, cols] + change

        stages = [(drift_of, [to_pair] if split else rounds[0])]
        if split:
            stages.append((pair_sum, rounds[0]))
        for r in range(len(rounds)):
            final = r == len(rounds) - 1
            stages.append((functools.partial(collect, final), [to_pair] if final else rounds[r + 1]))
        stages.append((finish, None))
        return stages

    plan = [prefix_stages(c, c < chunks - 1) for c in range(chunks)]
    inbox = [[got[j][c] for j in range(chips - 1)] for c in range(chunks)]
    turns = []
    arrival = 2.0
    for c in range(chunks):
        share = 16.0 * counts[c] / width
        arrival += share
        when = arrival
        for i, (_, moves) in enumerate(plan[c]):
            turns.append((when, c, i))
            if moves is not None:
                full = 1.0 if c == chunks - 1 else 0.5
                when += 1.7 + share * full * len(moves)
    results = [None] * chunks
    last = None
    for _, c, i in sorted(turns):
        compute, moves = plan[c][i]
        fetched = inbox[c]
        if last is not None:
            fetched, last = tied(fetched, last)
        out = compute(fetched)
        if moves is None:
            results[c] = out
        else:
            inbox[c] = [move(out) for move in moves]
            last = out
    return jnp.concatenate(results, axis=1)[None]


def solution(mesh):
    placed = (
        P("step", "seq", None),
        P("seq", None),
        P("step"),
        P(),
        P(),
        P(),
        P(),
        P(None, None, "seq"),
        P(None, "seq"),
        P("seq", None),
        P("seq", None),
    )
    return jax.shard_map(
        functools.partial(per_device, mesh.shape["step"], mesh.shape["seq"]),
        mesh=mesh,
        in_specs=placed,
        out_specs=P("step", "seq", None),
        check_vma=False,
    )
```

```python
import functools
import math

import jax
import jax.numpy as jnp
from jax import lax
from jax.experimental import pallas as pl
from jax.experimental.pallas import tpu as pltpu
from jax.sharding import PartitionSpec as P

eps = 1e-06
f32 = jnp.float32
bf16 = jnp.bfloat16
VM = pltpu.VMEM
MIB = 1024 * 1024


def params(mib):
    return pltpu.CompilerParams(vmem_limit_bytes=mib * MIB)


def cost(flops, moved):
    return pl.CostEstimate(flops=flops, transcendentals=0, bytes_accessed=moved)


def norm_kernel(t_ref, x_hbm, mod_ref, size_ref, m_ref, sg_ref, x_ref, sem):
    width = x_hbm.shape[-1]
    pieces = sem.shape[0]
    block = x_hbm.shape[1] // pieces
    copies = []
    for i in range(pieces):
        here = pl.ds(i * block, block)
        copies.append(pltpu.make_async_copy(x_hbm.at[0, here, :], x_ref.at[here, :], sem.at[i]))
        copies[i].start()
    row = lax.rem(t_ref[0], 8)
    shift = mod_ref[pl.ds(row, 1), :width]
    scale = 1.0 + mod_ref[pl.ds(row, 1), width : 2 * width]
    gate = mod_ref[pl.ds(row, 1), 2 * width :]
    sg_ref[...] = size_ref[t_ref[0]] * gate
    for i in range(pieces):
        copies[i].wait()
        here = slice(i * block, (i + 1) * block)
        x = x_ref[here, :]
        center = x - jnp.mean(x, axis=-1, keepdims=True)
        spread = jnp.mean(center * center, axis=-1, keepdims=True)
        m_ref[here, :] = (center * lax.rsqrt(spread + eps) * scale + shift).astype(bf16)


def norm_call(t_idx, trajectory, mod_table, step_sizes):
    _, rows, width = trajectory.shape
    return pl.pallas_call(
        norm_kernel,
        grid_spec=pltpu.PrefetchScalarGridSpec(
            num_scalar_prefetch=1,
            grid=(1,),
            in_specs=[
                pl.BlockSpec(memory_space=pltpu.HBM),
                pl.BlockSpec((8, 3 * width), lambda i, t: (t[0] // 8, 0)),
                pl.BlockSpec(memory_space=pltpu.SMEM),
            ],
            out_specs=[
                pl.BlockSpec((rows, width), lambda i, t: (0, 0)),
                pl.BlockSpec((1, width), lambda i, t: (0, 0)),
            ],
            scratch_shapes=[VM((rows, width), f32), pltpu.SemaphoreType.DMA((4,))],
        ),
        out_shape=[
            jax.ShapeDtypeStruct((rows, width), bf16),
            jax.ShapeDtypeStruct((1, width), f32),
        ],
        compiler_params=params(60),
        cost_estimate=cost(10 * rows * width, 0),
        name="norm",
    )(t_idx, trajectory, mod_table, step_sizes)


def project_kernel(tile, load, tiles, m0, m1, qg, kg, *refs):
    if load:
        wq_hbm, wm_hbm, q, k, v, act = refs[:6]
        held, rows, sem = refs[6:-2], refs[-2], refs[-1]
    else:
        held = refs[:tiles]
        q, k, v, act, rows = refs[tiles:]
    half = m0.shape[0]
    head = qg.shape[1]
    n_q = q.shape[1] // tile
    copies = []
    if load:
        for i in range(tiles):
            if i < 3 * n_q:
                source = wq_hbm.at[i // n_q, :, pl.ds(i % n_q * tile, tile)]
            else:
                source = wm_hbm.at[:, pl.ds((i - 3 * n_q) * tile, tile)]
            copies.append(pltpu.make_async_copy(source, held[i], sem.at[i]))
            copies[i].start()
    rows[:half] = m0[...]
    rows[half:] = m1[...]

    def normed(y, gain):
        parts = []
        for h in range(tile // head):
            one = y[:, h * head : (h + 1) * head]
            square = jnp.mean(one * one, axis=-1, keepdims=True)
            parts.append((one * lax.rsqrt(square + eps) * gain).astype(bf16))
        return jnp.concatenate(parts, axis=1)

    for i in range(tiles):
        if load:
            copies[i].wait()
        y = jnp.dot(rows[...], held[i][...], preferred_element_type=f32)
        cols = slice(i % n_q * tile, (i % n_q + 1) * tile)
        if i < n_q:
            q[:, cols] = normed(y, qg[...])
        elif i < 2 * n_q:
            k[:, cols] = normed(y, kg[...])
        elif i < 3 * n_q:
            v[:, cols] = y.astype(bf16)
        else:
            cols = slice((i - 3 * n_q) * tile, (i - 3 * n_q + 1) * tile)
            act[:, cols] = jax.nn.gelu(y, approximate=True).astype(bf16)


def project_call(m0, m1, q_gain, k_gain, w_qkv, w_mlp_in, held):
    half, width = m0.shape
    heads = w_qkv.shape[2]
    hidden = w_mlp_in.shape[1]
    tile = min(512, heads)
    tiles = (3 * heads + hidden) // tile
    rows = 2 * half
    load = held is None
    vm = pl.BlockSpec(memory_space=VM)
    hbm = pl.BlockSpec(memory_space=pltpu.HBM)
    shapes = [jax.ShapeDtypeStruct((rows, heads), bf16)] * 3
    shapes.append(jax.ShapeDtypeStruct((rows, hidden), bf16))
    scratch = [VM((rows, width), bf16)]
    if load:
        shapes += [jax.ShapeDtypeStruct((width, tile), bf16)] * tiles
        scratch.append(pltpu.SemaphoreType.DMA((tiles,)))
    return pl.pallas_call(
        functools.partial(project_kernel, tile, load, tiles),
        in_specs=[vm] * 4 + ([hbm] * 2 if load else [vm] * tiles),
        out_specs=[vm] * len(shapes),
        out_shape=shapes,
        scratch_shapes=scratch,
        compiler_params=params(30 if load else 9),
        cost_estimate=cost(2 * rows * width * (3 * heads + hidden), 0),
        name="project",
    )(m0, m1, q_gain, k_gain, *([w_qkv, w_mlp_in] if load else held))


def attend_kernel(pairs, head, *refs):
    q_ref = refs[0]
    k_refs = refs[1 : 1 + pairs]
    v_refs = refs[1 + pairs : 1 + 2 * pairs]
    out = refs[1 + 2 * pairs]
    scale = math.log2(math.e) / math.sqrt(head)
    for h in range(q_ref.shape[1] // head):
        cols = slice(h * head, (h + 1) * head)
        q = q_ref[:, cols]
        scores = [
            lax.dot_general(q, k[:, cols], (((1,), (1,)), ((), ())), preferred_element_type=f32)
            for k in k_refs
        ]
        top = functools.reduce(
            jnp.maximum, [jnp.max(s, axis=-1, keepdims=True) for s in scores]
        )
        weights = [jnp.exp2((s - top) * scale) for s in scores]
        total = sum(jnp.sum(w, axis=-1, keepdims=True) for w in weights)
        inverse = 1.0 / total
        mixed = sum(
            jnp.dot((w * inverse).astype(bf16), v[:, cols], preferred_element_type=f32)
            for w, v in zip(weights, v_refs)
        )
        out[:, cols] = mixed.astype(bf16)


def attend_call(q, ks, vs, head):
    vm = pl.BlockSpec(memory_space=VM)
    return pl.pallas_call(
        functools.partial(attend_kernel, len(ks), head),
        in_specs=[vm] * (1 + 2 * len(ks)),
        out_specs=vm,
        out_shape=jax.ShapeDtypeStruct(q.shape, bf16),
        compiler_params=params(9),
        cost_estimate=cost(4 * len(ks) * q.shape[0] ** 2 * q.shape[1] * 3, 0),
        name="attend",
    )(q, *ks, *vs)


def out_kernel(first, parts, *refs):
    xs, ws, extra = refs[:parts], refs[parts : 2 * parts], refs[2 * parts : -2]
    keep, send = refs[-2:]
    half, count = keep.shape
    cols = slice(first, first + count)
    terms = [
        jnp.dot(x[...], w[:, cols], preferred_element_type=f32) for x, w in zip(xs, ws)
    ]
    y = functools.reduce(jnp.add, terms)
    low, high = y[:half], y[half:]
    if extra:
        low = low + extra[0][:, cols]
        high = high + extra[1][:, cols]
    keep[...] = low
    send[...] = high.astype(send.dtype)


def out_call(xs, ws, extra, first, count, kind=bf16):
    half = xs[0].shape[0] // 2
    depth = sum(x.shape[1] for x in xs)
    vm = pl.BlockSpec(memory_space=VM)
    return pl.pallas_call(
        functools.partial(out_kernel, first, len(xs)),
        in_specs=[vm] * (2 * len(xs) + len(extra)),
        out_specs=[vm, vm],
        out_shape=[
            jax.ShapeDtypeStruct((half, count), f32),
            jax.ShapeDtypeStruct((half, count), kind),
        ],
        compiler_params=params(9),
        cost_estimate=cost(4 * half * count * depth, 0),
        name="project_out",
    )(*xs, *ws, *extra)


def per_device(
    n_step,
    n_seq,
    trajectory,
    x_start,
    t_idx,
    mod_table,
    step_sizes,
    q_gain,
    k_gain,
    w_qkv,
    w_mlp_in,
    w_out_attn,
    w_out_mlp,
):
    head = q_gain.shape[0]
    rows, width = x_start.shape
    chips = n_seq // 2
    groups = n_step // 2
    half = rows // 2
    unit = width // 24
    counts = [6 * unit, 10 * unit, 8 * unit]
    chunks = len(counts)
    firsts = [sum(counts[:c]) for c in range(chunks)]
    qg, kg = q_gain[None, :], k_gain[None, :]

    def to_core(x):
        return lax.ppermute(x, "seq", [(i, i ^ 1) for i in range(n_seq)])

    def to_chip(x, offset):
        return lax.ppermute(x, "seq", [(i, (i + 2 * offset) % n_seq) for i in range(n_seq)])

    def to_pair(x):
        return lax.ppermute(x, "step", [(i, i ^ 1) for i in range(n_step)])

    def tied(*values):
        return lax.optimization_barrier(values)

    parity = lax.rem(lax.axis_index("step"), 2)
    even = (parity == 0).astype(f32)
    offsets = range(1, chips)

    mine, sg = norm_call(t_idx, trajectory, mod_table, step_sizes)
    far = [to_chip(mine, j) for j in offsets]
    q0, k0, v0, act0, *held = project_call(
        mine, to_core(mine), qg, kg, w_qkv, w_mlp_in, None
    )
    low0, high0 = out_call([act0], [w_out_mlp], [], 0, width, f32)
    far, low0, high0 = tied(far, low0, high0)
    qs, ks, vs, acts = [], [k0], [v0], []
    for block in far:
        q, k, v, act = project_call(block, to_core(block), qg, kg, w_qkv, w_mlp_in, held)
        qs.append(q)
        ks.append(k)
        vs.append(v)
        acts.append(act)
    mixed = [attend_call(q, ks, vs, head) for q in qs]

    weights = [w_out_attn, w_out_mlp]
    got = [[] for _ in offsets]

    def rows_out(c):
        return [
            out_call([a, b], weights, [], firsts[c], counts[c]) for a, b in zip(mixed, acts)
        ]

    def joined(parts, sent):
        return [(keep + s.astype(f32)).astype(bf16) for (keep, _), s in zip(parts, sent)]

    def to_chips(ready):
        for j, one in enumerate(ready):
            got[j].append(to_chip(one, chips - 1 - j))

    parts = rows_out(0)
    sent = [to_core(send) for _, send in parts]
    q0, parts = tied(q0, parts)
    mixed0 = attend_call(q0, ks, vs, head)
    mixed0, sent = tied(mixed0, sent)
    ready = joined(parts, sent)
    mixed, acts, mixed0, ready = tied(mixed, acts, mixed0, ready)
    to_chips(ready)
    waiting = []
    for c in range(1, chunks):
        parts = rows_out(c)
        waiting.append((parts, [to_core(send) for _, send in parts]))
        mixed, acts, mixed0, parts = tied(mixed, acts, mixed0, parts)
        waiting[-1] = (parts, waiting[-1][1])
    mixed0, first = tied(mixed0, [row[0] for row in got])
    for row, one in zip(got, first):
        row[0] = one
    keep, send = out_call([mixed0], [w_out_attn], [low0, high0], 0, width)
    keep, waiting[0] = tied(keep, waiting[0])
    for parts, sent in waiting:
        to_chips(joined(parts, sent))
    own = keep + to_core(send).astype(f32)

    def along(pairs):
        return lambda x: lax.ppermute(x, "step", [(2 * a + i, 2 * b + i) for a, b in pairs for i in (0, 1)])

    group = lax.div(lax.axis_index("step"), 2)
    rounds = []
    span = 1
    while span < groups:
        pairs = [(b, b ^ span) for b in range(groups) if b ^ span < groups]
        if 2 * span >= groups:
            pairs = [p for p in pairs if p[0] < p[1]]
        rounds.append((span, along(pairs)))
        span *= 2

    def prefix_stages(c, split):
        cols = slice(firsts[c], firsts[c] + counts[c])
        held = {}

        def drift_of(fetched):
            branch = own[:, cols]
            for one in fetched:
                branch = branch + one.astype(f32)
            drift = sg[:, cols] * branch
            if split:
                held["kept"] = lax.dynamic_slice_in_dim(drift, parity * half, half, 0)
                held["other"] = lax.dynamic_slice_in_dim(drift, (1 - parity) * half, half, 0)
                return held["other"].astype(bf16)
            held["kept"] = held["total"] = drift
            return held["total"].astype(bf16)

        def pair_sum(fetched):
            held["fetched"] = fetched[0].astype(f32)
            held["total"] = held["kept"] + held["fetched"]
            return held["total"].astype(bf16)

        def collect(r, fetched):
            one = fetched[0].astype(f32)
            upper = (lax.rem(lax.div(group, rounds[r][0]), 2) == 1).astype(f32)
            held["earlier"] = held["earlier"] + upper * one if r else upper * one
            if r == len(rounds) - 1:
                return (held["earlier"] + even * held["kept"]).astype(bf16)
            held["total"] = held["total"] + one
            return held["total"].astype(bf16)

        def finish(fetched):
            back = fetched[0].astype(f32)
            if split:
                mine_half = held["earlier"] + held["kept"] + (1.0 - even) * held["fetched"]
                rest = back + held["other"]
                low = jnp.where(parity == 0, mine_half, rest)
                high = jnp.where(parity == 0, rest, mine_half)
                change = jnp.concatenate([low, high], axis=0)
            else:
                change = held["earlier"] + held["kept"] + back
            return x_start[:, cols] + change

        stages = [(drift_of, to_pair if split else rounds[0][1])]
        if split:
            stages.append((pair_sum, rounds[0][1]))
        for r in range(len(rounds)):
            move = to_pair if r == len(rounds) - 1 else rounds[r + 1][1]
            stages.append((functools.partial(collect, r), move))
        stages.append((finish, None))
        return stages

    plan = [prefix_stages(c, True) for c in range(chunks)]
    inbox = [[got[j][c] for j in range(chips - 1)] for c in range(chunks)]
    turns = []
    arrival = 2.0
    for c in range(chunks):
        share = 16.0 * counts[c] / width
        arrival += share
        when = arrival
        for i in range(len(plan[c])):
            turns.append((when, c, i))
            when += 2.2 + share * (1.0 if i == len(plan[c]) - 3 else 0.5)
    results = [None] * chunks
    last = None
    for _, c, i in sorted(turns):
        compute, move = plan[c][i]
        fetched = inbox[c]
        if last is not None:
            fetched, last = tied(fetched, last)
        out = compute(fetched)
        if move is None:
            results[c] = out
        else:
            inbox[c] = [move(out)]
            last = out
    return jnp.concatenate(results, axis=1)[None]


def solution(mesh):
    placed = (
        P("step", "seq", None),
        P("seq", None),
        P("step"),
        P(),
        P(),
        P(),
        P(),
        P(None, None, "seq"),
        P(None, "seq"),
        P("seq", None),
        P("seq", None),
    )
    return jax.shard_map(
        functools.partial(per_device, mesh.shape["step"], mesh.shape["seq"]),
        mesh=mesh,
        in_specs=placed,
        out_specs=P("step", "seq", None),
        check_vma=False,
    )
```

```python
import functools
import math

import jax
import jax.numpy as jnp
from jax import lax
from jax.experimental import pallas as pl
from jax.experimental.pallas import tpu as pltpu
from jax.sharding import PartitionSpec as P

eps = 1e-06
f32 = jnp.float32
bf16 = jnp.bfloat16
VM = pltpu.VMEM
MIB = 1024 * 1024


def params(mib):
    return pltpu.CompilerParams(vmem_limit_bytes=mib * MIB)


def cost(flops, moved):
    return pl.CostEstimate(flops=flops, transcendentals=0, bytes_accessed=moved)


def norm_kernel(t_ref, size_ref, x_hbm, mod_hbm, m_ref, sg_ref, x_ref, mod_ref, sem):
    width = x_hbm.shape[-1]
    pieces = sem.shape[0] - 1
    block = x_hbm.shape[1] // pieces
    t = t_ref[0]
    mod_copy = pltpu.make_async_copy(mod_hbm.at[pl.ds(t, 1), :], mod_ref, sem.at[pieces])
    mod_copy.start()
    copies = []
    for i in range(pieces):
        here = pl.ds(i * block, block)
        copies.append(pltpu.make_async_copy(x_hbm.at[0, here, :], x_ref.at[here, :], sem.at[i]))
        copies[i].start()
    mod_copy.wait()
    shift = mod_ref[:, :width]
    scale = 1.0 + mod_ref[:, width : 2 * width]
    sg_ref[...] = size_ref[t] * mod_ref[:, 2 * width :]
    for i in range(pieces):
        copies[i].wait()
        here = slice(i * block, (i + 1) * block)
        x = x_ref[here, :]
        center = x - jnp.mean(x, axis=-1, keepdims=True)
        spread = jnp.mean(center * center, axis=-1, keepdims=True)
        m_ref[here, :] = (center * lax.rsqrt(spread + eps) * scale + shift).astype(bf16)


def norm_call(t_idx, trajectory, mod_table, step_sizes):
    _, rows, width = trajectory.shape
    smem = pl.BlockSpec(memory_space=pltpu.SMEM)
    hbm = pl.BlockSpec(memory_space=pltpu.HBM)
    vm = pl.BlockSpec(memory_space=VM)
    return pl.pallas_call(
        norm_kernel,
        in_specs=[smem, smem, hbm, hbm],
        out_specs=[vm, vm],
        out_shape=[
            jax.ShapeDtypeStruct((rows, width), bf16),
            jax.ShapeDtypeStruct((1, width), f32),
        ],
        scratch_shapes=[
            VM((rows, width), f32),
            VM((1, 3 * width), f32),
            pltpu.SemaphoreType.DMA((5,)),
        ],
        compiler_params=params(60),
        cost_estimate=cost(10 * rows * width, 0),
        name="norm",
    )(t_idx, step_sizes, trajectory, mod_table)


def project_kernel(tile, load, tiles, m0, m1, qg, kg, *refs):
    if load:
        wq_hbm, wm_hbm, wb_hbm, q, k, v, act, low, high = refs[:9]
        held, rows, wb, sem = refs[9:-3], refs[-3], refs[-2], refs[-1]
    else:
        held = refs[:tiles]
        q, k, v, act, rows = refs[tiles:]
    half = m0.shape[0]
    head = qg.shape[1]
    n_q = q.shape[1] // tile
    copies = []
    if load:
        for i in range(tiles):
            if i < 3 * n_q:
                source = wq_hbm.at[i // n_q, :, pl.ds(i % n_q * tile, tile)]
            else:
                source = wm_hbm.at[:, pl.ds((i - 3 * n_q) * tile, tile)]
            copies.append(pltpu.make_async_copy(source, held[i], sem.at[i]))
            copies[i].start()
        span = low.shape[1] // (sem.shape[0] - tiles)
        for at in range(0, low.shape[1], span):
            here = (slice(None), pl.ds(at, span))
            copies.append(pltpu.make_async_copy(wb_hbm.at[here], wb.at[here], sem.at[len(copies)]))
            copies[-1].start()
    rows[:half] = m0[...]
    rows[half:] = m1[...]

    def normed(y, gain):
        parts = []
        for h in range(tile // head):
            one = y[:, h * head : (h + 1) * head]
            square = jnp.mean(one * one, axis=-1, keepdims=True)
            parts.append((one * lax.rsqrt(square + eps) * gain).astype(bf16))
        return jnp.concatenate(parts, axis=1)

    for i in range(tiles):
        if load:
            copies[i].wait()
        y = jnp.dot(rows[...], held[i][...], preferred_element_type=f32)
        cols = slice(i % n_q * tile, (i % n_q + 1) * tile)
        if i < n_q:
            q[:, cols] = normed(y, qg[...])
        elif i < 2 * n_q:
            k[:, cols] = normed(y, kg[...])
        elif i < 3 * n_q:
            v[:, cols] = y.astype(bf16)
        else:
            cols = slice((i - 3 * n_q) * tile, (i - 3 * n_q + 1) * tile)
            act[:, cols] = jax.nn.gelu(y, approximate=True).astype(bf16)
    if load:
        for i, copy in enumerate(copies[tiles:]):
            copy.wait()
            cols = slice(i * span, (i + 1) * span)
            y = jnp.dot(act[...], wb[:, cols], preferred_element_type=f32)
            low[:, cols] = y[:half]
            high[:, cols] = y[half:]


def project_call(m0, m1, q_gain, k_gain, w_qkv, w_mlp_in, w_out_mlp, held):
    half, width = m0.shape
    heads = w_qkv.shape[2]
    hidden = w_mlp_in.shape[1]
    tile = min(512, heads)
    tiles = (3 * heads + hidden) // tile
    rows = 2 * half
    load = held is None
    vm = pl.BlockSpec(memory_space=VM)
    hbm = pl.BlockSpec(memory_space=pltpu.HBM)
    shapes = [jax.ShapeDtypeStruct((rows, heads), bf16)] * 3
    shapes.append(jax.ShapeDtypeStruct((rows, hidden), bf16))
    scratch = [VM((rows, width), bf16)]
    if load:
        shapes += [jax.ShapeDtypeStruct((half, width), f32)] * 2
        shapes += [jax.ShapeDtypeStruct((width, tile), bf16)] * tiles
        scratch.append(VM(w_out_mlp.shape, bf16))
        scratch.append(pltpu.SemaphoreType.DMA((tiles + 4,)))
    return pl.pallas_call(
        functools.partial(project_kernel, tile, load, tiles),
        in_specs=[vm] * 4 + ([hbm] * 3 if load else [vm] * tiles),
        out_specs=[vm] * len(shapes),
        out_shape=shapes,
        scratch_shapes=scratch,
        compiler_params=params(27 if load else 9),
        cost_estimate=cost(2 * rows * width * (3 * heads + hidden), 0),
        name="project",
    )(m0, m1, q_gain, k_gain, *([w_qkv, w_mlp_in, w_out_mlp] if load else held))


def attend_kernel(pairs, head, *refs):
    q_ref = refs[0]
    k_refs = refs[1 : 1 + pairs]
    v_refs = refs[1 + pairs : 1 + 2 * pairs]
    out = refs[1 + 2 * pairs]
    scale = math.log2(math.e) / math.sqrt(head)
    for h in range(q_ref.shape[1] // head):
        cols = slice(h * head, (h + 1) * head)
        q = q_ref[:, cols]
        scores = [
            lax.dot_general(q, k[:, cols], (((1,), (1,)), ((), ())), preferred_element_type=f32)
            for k in k_refs
        ]
        top = functools.reduce(
            jnp.maximum, [jnp.max(s, axis=-1, keepdims=True) for s in scores]
        )
        weights = [jnp.exp2((s - top) * scale) for s in scores]
        total = sum(jnp.sum(w, axis=-1, keepdims=True) for w in weights)
        inverse = 1.0 / total
        mixed = sum(
            jnp.dot((w * inverse).astype(bf16), v[:, cols], preferred_element_type=f32)
            for w, v in zip(weights, v_refs)
        )
        out[:, cols] = mixed.astype(bf16)


def attend_call(q, ks, vs, head):
    vm = pl.BlockSpec(memory_space=VM)
    return pl.pallas_call(
        functools.partial(attend_kernel, len(ks), head),
        in_specs=[vm] * (1 + 2 * len(ks)),
        out_specs=vm,
        out_shape=jax.ShapeDtypeStruct(q.shape, bf16),
        compiler_params=params(9),
        cost_estimate=cost(4 * len(ks) * q.shape[0] ** 2 * q.shape[1] * 3, 0),
        name="attend",
    )(q, *ks, *vs)


def out_kernel(jobs, *refs):
    outs = refs[len(refs) - 2 * len(jobs) :]
    at = 0
    for turn, (parts, extras, first, count) in enumerate(jobs):
        xs = refs[at : at + parts]
        ws = refs[at + parts : at + 2 * parts]
        extra = refs[at + 2 * parts : at + 2 * parts + extras]
        at += 2 * parts + extras
        keep, send = outs[2 * turn : 2 * turn + 2]
        half = keep.shape[0]
        cols = slice(first, first + count)
        terms = [
            jnp.dot(x[...], w[:, cols], preferred_element_type=f32) for x, w in zip(xs, ws)
        ]
        y = functools.reduce(jnp.add, terms)
        low, high = y[:half], y[half:]
        if extra:
            low = low + extra[0][:, cols]
            high = high + extra[1][:, cols]
        keep[...] = low
        send[...] = high.astype(bf16)


def out_call(jobs):
    vm = pl.BlockSpec(memory_space=VM)
    given, plan, shapes, flops = [], [], [], 0
    for xs, ws, extra, first, count in jobs:
        given += [*xs, *ws, *extra]
        plan.append((len(xs), len(extra), first, count))
        half = xs[0].shape[0] // 2
        shapes.append(jax.ShapeDtypeStruct((half, count), f32))
        shapes.append(jax.ShapeDtypeStruct((half, count), bf16))
        flops += 4 * half * count * sum(x.shape[1] for x in xs)
    outs = pl.pallas_call(
        functools.partial(out_kernel, plan),
        in_specs=[vm] * len(given),
        out_specs=[vm] * len(shapes),
        out_shape=shapes,
        compiler_params=params(9),
        cost_estimate=cost(flops, 0),
        name="project_out",
    )(*given)
    return [tuple(outs[i : i + 2]) for i in range(0, len(outs), 2)]


def join_kernel(keep, sent, out):
    out[...] = (keep[...] + sent[...].astype(f32)).astype(bf16)


def join_call(keep, sent):
    vm = pl.BlockSpec(memory_space=VM)
    return pl.pallas_call(
        join_kernel,
        in_specs=[vm, vm],
        out_specs=vm,
        out_shape=jax.ShapeDtypeStruct(keep.shape, bf16),
        compiler_params=params(6),
        name="join",
    )(keep, sent)


def drift_kernel(first, parity, keep, sent, sg, *refs):
    fetched, (kept, other, send) = refs[:-3], refs[-3:]
    half, count = kept.shape
    p = parity[0]

    def part(which):
        rows = pl.ds(pl.multiple_of(which * half, half), half)
        branch = keep[rows, :] + sent[rows, :].astype(f32)
        for one in fetched:
            branch = branch + one[rows, :].astype(f32)
        return sg[:, first : first + count] * branch

    kept[...] = part(p)
    passed = part(1 - p)
    other[...] = passed
    send[...] = passed.astype(bf16)


def drift_call(parity, keep, sent, sg, fetched, first):
    rows, count = fetched[0].shape
    vm = pl.BlockSpec(memory_space=VM)
    smem = pl.BlockSpec(memory_space=pltpu.SMEM)
    shape = (rows // 2, count)
    return pl.pallas_call(
        functools.partial(drift_kernel, first),
        in_specs=[smem] + [vm] * (3 + len(fetched)),
        out_specs=[vm] * 3,
        out_shape=[
            jax.ShapeDtypeStruct(shape, f32),
            jax.ShapeDtypeStruct(shape, f32),
            jax.ShapeDtypeStruct(shape, bf16),
        ],
        compiler_params=params(6),
        name="drift",
    )(parity, keep, sent, sg, *fetched)


def finish_kernel(first, parity, x_start, earlier, kept, fetched, other, back, *refs):
    out, result, sem = refs[-3:]
    half, count = kept.shape
    cols = slice(first, first + count)
    p = parity[0]
    mine = pl.ds(pl.multiple_of(p * half, half), half)
    rest = pl.ds(pl.multiple_of((1 - p) * half, half), half)
    odd = p.astype(f32)
    result[mine, :] = x_start[mine, cols] + earlier[...] + kept[...] + odd * fetched[...].astype(f32)
    result[rest, :] = x_start[rest, cols] + other[...] + back[...].astype(f32)
    copy = pltpu.make_async_copy(result, out.at[0, :, pl.ds(first, count)], sem)
    copy.start()
    copy.wait()


def finish_call(parity, x_start, earlier, kept, fetched, other, back, into, first):
    rows, width = x_start.shape
    vm = pl.BlockSpec(memory_space=VM)
    smem = pl.BlockSpec(memory_space=pltpu.SMEM)
    hbm = pl.BlockSpec(memory_space=pltpu.HBM)
    given = [parity, x_start, earlier, kept, fetched, other, back]
    return pl.pallas_call(
        functools.partial(finish_kernel, first),
        in_specs=[smem] + [vm] * 6 + [hbm] * len(into),
        out_specs=hbm,
        out_shape=jax.ShapeDtypeStruct((1, rows, width), f32),
        scratch_shapes=[VM((rows, kept.shape[1]), f32), pltpu.SemaphoreType.DMA],
        input_output_aliases={len(given): 0} if into else {},
        compiler_params=params(6),
        name="finish",
    )(*given, *into)


def per_device(
    n_step,
    n_seq,
    trajectory,
    x_start,
    t_idx,
    mod_table,
    step_sizes,
    q_gain,
    k_gain,
    w_qkv,
    w_mlp_in,
    w_out_attn,
    w_out_mlp,
):
    head = q_gain.shape[0]
    rows, width = x_start.shape
    chips = n_seq // 2
    groups = n_step // 2
    half = rows // 2
    unit = width // 24
    counts = [10 * unit, 8 * unit, 6 * unit]
    chunks = len(counts)
    firsts = [sum(counts[:c]) for c in range(chunks)]
    qg, kg = q_gain[None, :], k_gain[None, :]

    def to_core(x):
        return lax.ppermute(x, "seq", [(i, i ^ 1) for i in range(n_seq)])

    def to_chip(x, offset):
        return lax.ppermute(x, "seq", [(i, (i + 2 * offset) % n_seq) for i in range(n_seq)])

    def to_pair(x):
        return lax.ppermute(x, "step", [(i, i ^ 1) for i in range(n_step)])

    def tied(*values):
        return lax.optimization_barrier(values)

    parity = lax.rem(lax.axis_index("step"), 2)
    even = (parity == 0).astype(f32)
    which = parity[None]
    offsets = range(1, chips)

    mine, sg = norm_call(t_idx, trajectory, mod_table, step_sizes)
    far = [to_chip(mine, j) for j in offsets]
    q0, k0, v0, act0, low0, high0, *held = project_call(
        mine, to_core(mine), qg, kg, w_qkv, w_mlp_in, w_out_mlp, None
    )
    far, low0, high0 = tied(far, low0, high0)
    qs, ks, vs, acts = [], [k0], [v0], []
    for block in far:
        q, k, v, act = project_call(block, to_core(block), qg, kg, w_qkv, w_mlp_in, w_out_mlp, held)
        qs.append(q)
        ks.append(k)
        vs.append(v)
        acts.append(act)
    mixed = [attend_call(q, ks, vs, head) for q in qs]

    weights = [w_out_attn, w_out_mlp]
    got = [[] for _ in offsets]

    def jobs_of(c):
        return [([a, b], weights, [], firsts[c], counts[c]) for a, b in zip(mixed, acts)]

    def joined(parts, sent):
        return [join_call(keep, s) for (keep, _), s in zip(parts, sent)]

    def to_chips(ready):
        for j, one in enumerate(ready):
            got[j].append(to_chip(one, chips - 1 - j))

    parts = out_call(jobs_of(0))
    sent = [to_core(send) for _, send in parts]
    q0, parts = tied(q0, parts)
    mixed0 = attend_call(q0, ks, vs, head)
    mixed0, sent = tied(mixed0, sent)
    ready = joined(parts, sent)
    mixed, acts, mixed0, ready = tied(mixed, acts, mixed0, ready)
    to_chips(ready)
    jobs = [job for c in range(1, chunks) for job in jobs_of(c)]
    for c in range(chunks):
        jobs.append(([mixed0], [w_out_attn], [low0, high0], firsts[c], counts[c]))
    parts = out_call(jobs)
    sent = [to_core(send) for _, send in parts]
    keep = [part[0] for part in parts[-chunks:]]
    sent0 = sent[-chunks:]
    others = chips - 1
    first, keep, sent[:others] = tied([row[0] for row in got], keep, sent[:others])
    for row, one in zip(got, first):
        row[0] = one
    ready = joined(parts[:others], sent[:others])
    keep, ready = tied(keep, ready)
    to_chips(ready)
    for c in range(2, chunks):
        here = slice((c - 1) * others, c * others)
        to_chips(joined(parts[here], sent[here]))

    def along(pairs):
        return lambda x: lax.ppermute(x, "step", [(2 * a + i, 2 * b + i) for a, b in pairs for i in (0, 1)])

    group = lax.div(lax.axis_index("step"), 2)
    rounds = []
    span = 1
    while span < groups:
        pairs = [(b, b ^ span) for b in range(groups) if b ^ span < groups]
        rounds.append((span, along(pairs)))
        span *= 2

    def prefix_stages(c):
        held = {}

        def drift_of(fetched):
            drift = drift_call(which, keep[c], sent0[c], sg, fetched, firsts[c])
            held["kept"], held["other"], send = drift
            return send

        def pair_sum(fetched):
            held["fetched"] = fetched[0]
            held["total"] = held["kept"] + fetched[0].astype(f32)
            return held["total"].astype(bf16)

        def collect(r, fetched):
            one = fetched[0].astype(f32)
            upper = (lax.rem(lax.div(group, rounds[r][0]), 2) == 1).astype(f32)
            held["earlier"] = held["earlier"] + upper * one if r else upper * one
            if r == len(rounds) - 1:
                return (held["earlier"] + even * held["kept"]).astype(bf16)
            held["total"] = held["total"] + one
            return held["total"].astype(bf16)

        def finish(fetched):
            given = [held[name] for name in ("earlier", "kept", "fetched", "other")]
            into = list(written)
            written[:] = [finish_call(which, x_start, *given, fetched[0], into, firsts[c])]

        stages = [(drift_of, to_pair), (pair_sum, rounds[0][1])]
        for r in range(len(rounds)):
            move = to_pair if r == len(rounds) - 1 else rounds[r + 1][1]
            stages.append((functools.partial(collect, r), move))
        stages.append((finish, None))
        return stages

    plan = [prefix_stages(c) for c in range(chunks)]
    inbox = [[got[j][c] for j in range(chips - 1)] for c in range(chunks)]
    turns = []
    arrival = 2.0
    for c in range(chunks):
        share = 16.0 * counts[c] / width
        arrival += share
        when = arrival
        for i in range(len(plan[c])):
            turns.append((when, c, i))
            when += 2.2 + share * (1.0 if i == len(plan[c]) - 3 else 0.5)
    written = []
    last = None
    for _, c, i in sorted(turns):
        compute, move = plan[c][i]
        fetched = inbox[c]
        if last is not None:
            fetched, last = tied(fetched, last)
        out = compute(fetched)
        if move is not None:
            inbox[c] = [move(out)]
            last = out
    return written[0]


def solution(mesh):
    placed = (
        P("step", "seq", None),
        P("seq", None),
        P("step"),
        P(),
        P(),
        P(),
        P(),
        P(None, None, "seq"),
        P(None, "seq"),
        P("seq", None),
        P("seq", None),
    )
    return jax.shard_map(
        functools.partial(per_device, mesh.shape["step"], mesh.shape["seq"]),
        mesh=mesh,
        in_specs=placed,
        out_specs=P("step", "seq", None),
        check_vma=False,
    )
```

```python
import functools
import math

import jax
import jax.numpy as jnp
from jax import lax
from jax.experimental import pallas as pl
from jax.experimental.pallas import tpu as pltpu
from jax.sharding import PartitionSpec as P

eps = 1e-06
f32 = jnp.float32
bf16 = jnp.bfloat16
VM = pltpu.VMEM
MIB = 1024 * 1024


def params(mib):
    return pltpu.CompilerParams(vmem_limit_bytes=mib * MIB)


def cost(flops, moved):
    return pl.CostEstimate(flops=flops, transcendentals=0, bytes_accessed=moved)


def norm_kernel(t_ref, size_ref, x_hbm, mod_hbm, m_ref, sg_ref, x_ref, mod_ref, sem):
    width = x_hbm.shape[-1]
    pieces = sem.shape[0] - 1
    block = x_hbm.shape[1] // pieces
    t = t_ref[0]
    mod_copy = pltpu.make_async_copy(mod_hbm.at[pl.ds(t, 1), :], mod_ref, sem.at[pieces])
    mod_copy.start()
    copies = []
    for i in range(pieces):
        here = pl.ds(i * block, block)
        copies.append(pltpu.make_async_copy(x_hbm.at[0, here, :], x_ref.at[here, :], sem.at[i]))
        copies[i].start()
    mod_copy.wait()
    shift = mod_ref[:, :width]
    scale = 1.0 + mod_ref[:, width : 2 * width]
    sg_ref[...] = size_ref[t] * mod_ref[:, 2 * width :]
    for i in range(pieces):
        copies[i].wait()
        here = slice(i * block, (i + 1) * block)
        x = x_ref[here, :]
        center = x - jnp.mean(x, axis=-1, keepdims=True)
        spread = jnp.mean(center * center, axis=-1, keepdims=True)
        m_ref[here, :] = (center * lax.rsqrt(spread + eps) * scale + shift).astype(bf16)


def norm_call(t_idx, trajectory, mod_table, step_sizes):
    _, rows, width = trajectory.shape
    smem = pl.BlockSpec(memory_space=pltpu.SMEM)
    hbm = pl.BlockSpec(memory_space=pltpu.HBM)
    vm = pl.BlockSpec(memory_space=VM)
    return pl.pallas_call(
        norm_kernel,
        in_specs=[smem, smem, hbm, hbm],
        out_specs=[vm, vm],
        out_shape=[
            jax.ShapeDtypeStruct((rows, width), bf16),
            jax.ShapeDtypeStruct((1, width), f32),
        ],
        scratch_shapes=[
            VM((rows, width), f32),
            VM((1, 3 * width), f32),
            pltpu.SemaphoreType.DMA((5,)),
        ],
        compiler_params=params(60),
        cost_estimate=cost(10 * rows * width, 0),
        name="norm",
    )(t_idx, step_sizes, trajectory, mod_table)


def project_kernel(tile, load, tiles, m0, m1, qg, kg, *refs):
    if load:
        wq_hbm, wm_hbm, wb_hbm, q, k, v, act, low, high = refs[:9]
        held, rows, wb, sem = refs[9:-3], refs[-3], refs[-2], refs[-1]
    else:
        held = refs[:tiles]
        q, k, v, act, rows = refs[tiles:]
    half = m0.shape[0]
    head = qg.shape[1]
    n_q = q.shape[1] // tile
    copies = []
    if load:
        for i in range(tiles):
            if i < 3 * n_q:
                source = wq_hbm.at[i // n_q, :, pl.ds(i % n_q * tile, tile)]
            else:
                source = wm_hbm.at[:, pl.ds((i - 3 * n_q) * tile, tile)]
            copies.append(pltpu.make_async_copy(source, held[i], sem.at[i]))
            copies[i].start()
        span = low.shape[1] // (sem.shape[0] - tiles)
        for at in range(0, low.shape[1], span):
            here = (slice(None), pl.ds(at, span))
            copies.append(pltpu.make_async_copy(wb_hbm.at[here], wb.at[here], sem.at[len(copies)]))
            copies[-1].start()
    rows[:half] = m0[...]
    rows[half:] = m1[...]

    def normed(y, gain):
        parts = []
        for h in range(tile // head):
            one = y[:, h * head : (h + 1) * head]
            square = jnp.mean(one * one, axis=-1, keepdims=True)
            parts.append((one * lax.rsqrt(square + eps) * gain).astype(bf16))
        return jnp.concatenate(parts, axis=1)

    for i in range(tiles):
        if load:
            copies[i].wait()
        y = jnp.dot(rows[...], held[i][...], preferred_element_type=f32)
        cols = slice(i % n_q * tile, (i % n_q + 1) * tile)
        if i < n_q:
            q[:, cols] = normed(y, qg[...])
        elif i < 2 * n_q:
            k[:, cols] = normed(y, kg[...])
        elif i < 3 * n_q:
            v[:, cols] = y.astype(bf16)
        else:
            cols = slice((i - 3 * n_q) * tile, (i - 3 * n_q + 1) * tile)
            act[:, cols] = jax.nn.gelu(y, approximate=True).astype(bf16)
    if load:
        for i, copy in enumerate(copies[tiles:]):
            copy.wait()
            cols = slice(i * span, (i + 1) * span)
            y = jnp.dot(act[...], wb[:, cols], preferred_element_type=f32)
            low[:, cols] = y[:half]
            high[:, cols] = y[half:]


def project_call(m0, m1, q_gain, k_gain, w_qkv, w_mlp_in, w_out_mlp, held):
    half, width = m0.shape
    heads = w_qkv.shape[2]
    hidden = w_mlp_in.shape[1]
    tile = min(512, heads)
    tiles = (3 * heads + hidden) // tile
    rows = 2 * half
    load = held is None
    vm = pl.BlockSpec(memory_space=VM)
    hbm = pl.BlockSpec(memory_space=pltpu.HBM)
    shapes = [jax.ShapeDtypeStruct((rows, heads), bf16)] * 3
    shapes.append(jax.ShapeDtypeStruct((rows, hidden), bf16))
    scratch = [VM((rows, width), bf16)]
    if load:
        shapes += [jax.ShapeDtypeStruct((half, width), f32)] * 2
        shapes += [jax.ShapeDtypeStruct((width, tile), bf16)] * tiles
        scratch.append(VM(w_out_mlp.shape, bf16))
        scratch.append(pltpu.SemaphoreType.DMA((tiles + 4,)))
    return pl.pallas_call(
        functools.partial(project_kernel, tile, load, tiles),
        in_specs=[vm] * 4 + ([hbm] * 3 if load else [vm] * tiles),
        out_specs=[vm] * len(shapes),
        out_shape=shapes,
        scratch_shapes=scratch,
        compiler_params=params(27 if load else 9),
        cost_estimate=cost(2 * rows * width * (3 * heads + hidden), 0),
        name="project",
    )(m0, m1, q_gain, k_gain, *([w_qkv, w_mlp_in, w_out_mlp] if load else held))


def attend_kernel(pairs, head, *refs):
    q_ref = refs[0]
    k_refs = refs[1 : 1 + pairs]
    v_refs = refs[1 + pairs : 1 + 2 * pairs]
    out = refs[1 + 2 * pairs]
    scale = math.log2(math.e) / math.sqrt(head)
    for h in range(q_ref.shape[1] // head):
        cols = slice(h * head, (h + 1) * head)
        q = q_ref[:, cols]
        scores = [
            lax.dot_general(q, k[:, cols], (((1,), (1,)), ((), ())), preferred_element_type=f32)
            for k in k_refs
        ]
        top = functools.reduce(
            jnp.maximum, [jnp.max(s, axis=-1, keepdims=True) for s in scores]
        )
        weights = [jnp.exp2((s - top) * scale) for s in scores]
        total = sum(jnp.sum(w, axis=-1, keepdims=True) for w in weights)
        inverse = 1.0 / total
        mixed = sum(
            jnp.dot((w * inverse).astype(bf16), v[:, cols], preferred_element_type=f32)
            for w, v in zip(weights, v_refs)
        )
        out[:, cols] = mixed.astype(bf16)


def attend_call(q, ks, vs, head):
    vm = pl.BlockSpec(memory_space=VM)
    return pl.pallas_call(
        functools.partial(attend_kernel, len(ks), head),
        in_specs=[vm] * (1 + 2 * len(ks)),
        out_specs=vm,
        out_shape=jax.ShapeDtypeStruct(q.shape, bf16),
        compiler_params=params(9),
        cost_estimate=cost(4 * len(ks) * q.shape[0] ** 2 * q.shape[1] * 3, 0),
        name="attend",
    )(q, *ks, *vs)


def out_kernel(jobs, *refs):
    outs = refs[len(refs) - 2 * len(jobs) :]
    at = 0
    for turn, (parts, extras, first, count) in enumerate(jobs):
        xs = refs[at : at + parts]
        ws = refs[at + parts : at + 2 * parts]
        extra = refs[at + 2 * parts : at + 2 * parts + extras]
        at += 2 * parts + extras
        keep, send = outs[2 * turn : 2 * turn + 2]
        half = keep.shape[0]
        cols = slice(first, first + count)
        terms = [
            jnp.dot(x[...], w[:, cols], preferred_element_type=f32) for x, w in zip(xs, ws)
        ]
        y = functools.reduce(jnp.add, terms)
        low, high = y[:half], y[half:]
        if extra:
            low = low + extra[0][:, cols]
            high = high + extra[1][:, cols]
        keep[...] = low
        send[...] = high.astype(bf16)


def out_call(jobs):
    vm = pl.BlockSpec(memory_space=VM)
    given, plan, shapes, flops = [], [], [], 0
    for xs, ws, extra, first, count in jobs:
        given += [*xs, *ws, *extra]
        plan.append((len(xs), len(extra), first, count))
        half = xs[0].shape[0] // 2
        shapes.append(jax.ShapeDtypeStruct((half, count), f32))
        shapes.append(jax.ShapeDtypeStruct((half, count), bf16))
        flops += 4 * half * count * sum(x.shape[1] for x in xs)
    outs = pl.pallas_call(
        functools.partial(out_kernel, plan),
        in_specs=[vm] * len(given),
        out_specs=[vm] * len(shapes),
        out_shape=shapes,
        compiler_params=params(9),
        cost_estimate=cost(flops, 0),
        name="project_out",
    )(*given)
    return [tuple(outs[i : i + 2]) for i in range(0, len(outs), 2)]


def join_kernel(keep, sent, out):
    out[...] = (keep[...] + sent[...].astype(f32)).astype(bf16)


def join_call(keep, sent):
    vm = pl.BlockSpec(memory_space=VM)
    return pl.pallas_call(
        join_kernel,
        in_specs=[vm, vm],
        out_specs=vm,
        out_shape=jax.ShapeDtypeStruct(keep.shape, bf16),
        compiler_params=params(6),
        name="join",
    )(keep, sent)


def drift_kernel(first, parity, keep, sent, sg, *refs):
    fetched, (kept, other, send) = refs[:-3], refs[-3:]
    half, count = kept.shape
    p = parity[0]

    def part(which):
        rows = pl.ds(pl.multiple_of(which * half, half), half)
        branch = keep[rows, :] + sent[rows, :].astype(f32)
        for one in fetched:
            branch = branch + one[rows, :].astype(f32)
        return sg[:, first : first + count] * branch

    kept[...] = part(p)
    passed = part(1 - p)
    other[...] = passed
    send[...] = passed.astype(bf16)


def drift_call(parity, keep, sent, sg, fetched, first):
    rows, count = fetched[0].shape
    vm = pl.BlockSpec(memory_space=VM)
    smem = pl.BlockSpec(memory_space=pltpu.SMEM)
    shape = (rows // 2, count)
    return pl.pallas_call(
        functools.partial(drift_kernel, first),
        in_specs=[smem] + [vm] * (3 + len(fetched)),
        out_specs=[vm] * 3,
        out_shape=[
            jax.ShapeDtypeStruct(shape, f32),
            jax.ShapeDtypeStruct(shape, f32),
            jax.ShapeDtypeStruct(shape, bf16),
        ],
        compiler_params=params(6),
        name="drift",
    )(parity, keep, sent, sg, *fetched)


def finish_kernel(first, parity, x_start, earlier, kept, fetched, other, back, *refs):
    out, result, sem = refs[-3:]
    half, count = kept.shape
    cols = slice(first, first + count)
    p = parity[0]
    mine = pl.ds(pl.multiple_of(p * half, half), half)
    rest = pl.ds(pl.multiple_of((1 - p) * half, half), half)
    odd = p.astype(f32)
    result[mine, :] = x_start[mine, cols] + earlier[...] + kept[...] + odd * fetched[...].astype(f32)
    result[rest, :] = x_start[rest, cols] + other[...] + back[...].astype(f32)
    copy = pltpu.make_async_copy(result, out.at[0, :, pl.ds(first, count)], sem)
    copy.start()
    copy.wait()


def finish_call(parity, x_start, earlier, kept, fetched, other, back, into, first):
    rows, width = x_start.shape
    vm = pl.BlockSpec(memory_space=VM)
    smem = pl.BlockSpec(memory_space=pltpu.SMEM)
    hbm = pl.BlockSpec(memory_space=pltpu.HBM)
    given = [parity, x_start, earlier, kept, fetched, other, back]
    return pl.pallas_call(
        functools.partial(finish_kernel, first),
        in_specs=[smem] + [vm] * 6 + [hbm] * len(into),
        out_specs=hbm,
        out_shape=jax.ShapeDtypeStruct((1, rows, width), f32),
        scratch_shapes=[VM((rows, kept.shape[1]), f32), pltpu.SemaphoreType.DMA],
        input_output_aliases={len(given): 0} if into else {},
        compiler_params=params(6),
        name="finish",
    )(*given, *into)


def per_device(
    n_step,
    n_seq,
    trajectory,
    x_start,
    t_idx,
    mod_table,
    step_sizes,
    q_gain,
    k_gain,
    w_qkv,
    w_mlp_in,
    w_out_attn,
    w_out_mlp,
):
    head = q_gain.shape[0]
    rows, width = x_start.shape
    chips = n_seq // 2
    groups = n_step // 2
    half = rows // 2
    unit = width // 24
    counts = [10 * unit, 8 * unit, 6 * unit]
    chunks = len(counts)
    firsts = [sum(counts[:c]) for c in range(chunks)]
    qg, kg = q_gain[None, :], k_gain[None, :]

    def to_core(x):
        return lax.ppermute(x, "seq", [(i, i ^ 1) for i in range(n_seq)])

    def to_chip(x, offset):
        return lax.ppermute(x, "seq", [(i, (i + 2 * offset) % n_seq) for i in range(n_seq)])

    def to_pair(x):
        return lax.ppermute(x, "step", [(i, i ^ 1) for i in range(n_step)])

    def tied(*values):
        return lax.optimization_barrier(values)

    parity = lax.rem(lax.axis_index("step"), 2)
    even = (parity == 0).astype(f32)
    which = parity[None]
    offsets = range(1, chips)

    mine, sg = norm_call(t_idx, trajectory, mod_table, step_sizes)
    far = [to_chip(mine, j) for j in offsets]
    q0, k0, v0, act0, low0, high0, *held = project_call(
        mine, to_core(mine), qg, kg, w_qkv, w_mlp_in, w_out_mlp, None
    )
    far, low0, high0 = tied(far, low0, high0)
    qs, ks, vs, acts = [], [k0], [v0], []
    for block in far:
        q, k, v, act = project_call(block, to_core(block), qg, kg, w_qkv, w_mlp_in, w_out_mlp, held)
        qs.append(q)
        ks.append(k)
        vs.append(v)
        acts.append(act)
    mixed = [attend_call(q, ks, vs, head) for q in qs]

    weights = [w_out_attn, w_out_mlp]
    got = [[] for _ in offsets]

    def jobs_of(c):
        return [([a, b], weights, [], firsts[c], counts[c]) for a, b in zip(mixed, acts)]

    def joined(parts, sent):
        return [join_call(keep, s) for (keep, _), s in zip(parts, sent)]

    def to_chips(ready):
        for j, one in enumerate(ready):
            got[j].append(to_chip(one, chips - 1 - j))

    parts = out_call(jobs_of(0))
    sent = [to_core(send) for _, send in parts]
    q0, parts = tied(q0, parts)
    mixed0 = attend_call(q0, ks, vs, head)
    mixed0, sent = tied(mixed0, sent)
    ready = joined(parts, sent)
    mixed, acts, mixed0, ready = tied(mixed, acts, mixed0, ready)
    to_chips(ready)
    jobs = [job for c in range(1, chunks) for job in jobs_of(c)]
    for c in range(chunks):
        jobs.append(([mixed0], [w_out_attn], [low0, high0], firsts[c], counts[c]))
    parts = out_call(jobs)
    sent = [to_core(send) for _, send in parts]
    keep = [part[0] for part in parts[-chunks:]]
    sent0 = sent[-chunks:]
    others = chips - 1
    first, keep, sent[:others] = tied([row[0] for row in got], keep, sent[:others])
    for row, one in zip(got, first):
        row[0] = one
    ready = joined(parts[:others], sent[:others])
    keep, ready = tied(keep, ready)
    to_chips(ready)
    for c in range(2, chunks):
        here = slice((c - 1) * others, c * others)
        to_chips(joined(parts[here], sent[here]))

    def along(pairs):
        return lambda x: lax.ppermute(x, "step", [(2 * a + i, 2 * b + i) for a, b in pairs for i in (0, 1)])

    group = lax.div(lax.axis_index("step"), 2)
    spans = []
    while 2 ** len(spans) < groups:
        spans.append(2 ** len(spans))

    def swap(span):
        return along([(b, b ^ span) for b in range(groups) if b ^ span < groups])

    def prefix_stages(c, halves):
        held = {}
        quarter = half // 2
        bit = lax.rem(group, 2)

        def drift_of(fetched):
            drift = drift_call(which, keep[c], sent0[c], sg, fetched, firsts[c])
            held["kept"], held["other"], send = drift
            return send

        def pair_sum(fetched):
            held["fetched"] = fetched[0]
            held["total"] = held["kept"] + fetched[0].astype(f32)
            return held["total"].astype(bf16)

        def collect(r, fetched):
            one = fetched[0]
            if halves and spans[r] == 2:
                both = [held["piece"], one]
                one = jnp.where(
                    bit == 0, jnp.concatenate(both, axis=0), jnp.concatenate(both[::-1], axis=0)
                )
            one = one.astype(f32)
            upper = (lax.rem(lax.div(group, spans[r]), 2) == 1).astype(f32)
            held["earlier"] = held["earlier"] + upper * one if r else upper * one
            if r == len(spans) - 1:
                return (held["earlier"] + even * held["kept"]).astype(bf16)
            held["total"] = held["total"] + one
            total = held["total"].astype(bf16)
            if halves and spans[r + 1] == 2:
                return lax.dynamic_slice_in_dim(total, bit * quarter, quarter, 0)
            return total

        def pass_on(fetched):
            held["piece"] = fetched[0]
            return fetched[0]

        def finish(fetched):
            given = [held[name] for name in ("earlier", "kept", "fetched", "other")]
            into = list(written)
            written[:] = [finish_call(which, x_start, *given, fetched[0], into, firsts[c])]

        stages = [(drift_of, to_pair, "x", 0.5), (pair_sum, swap(1), "z1", 0.5)]
        for r in range(len(spans)):
            take = functools.partial(collect, r)
            if r == len(spans) - 1:
                stages.append((take, to_pair, "x", 0.5))
            elif halves and spans[r + 1] == 2:
                stages.append((take, swap(2), "z2", 0.5))
                stages.append((pass_on, swap(1), "z1", 0.25))
            else:
                stages.append((take, swap(spans[r + 1]), "z2", 1.0))
        stages.append((finish, None, "", 0.0))
        return stages

    plan = [prefix_stages(c, c < chunks - 1) for c in range(chunks)]
    inbox = [[got[j][c] for j in range(chips - 1)] for c in range(chunks)]
    shares = [18.5 * n / width for n in counts]
    ends = [2.0 + sum(shares[: c + 1]) for c in range(chunks)]
    waits = [(end, c, 0) for c, end in enumerate(ends)]
    free = {"x": 0.0, "z1": 0.0, "z2": 0.0, "": 0.0}
    turns = []
    while waits:
        when, c, i = min(waits)
        waits.remove((when, c, i))
        turns.append((c, i))
        if i + 1 < len(plan[c]):
            link, load = plan[c][i][2:]
            begin = max(when + 2.0, free[link])
            free[link] = begin + load * shares[c]
            waits.append((free[link] + 0.7, c, i + 1))
    written = []
    last = None
    for c, i in turns:
        compute, move = plan[c][i][:2]
        fetched = inbox[c]
        if last is not None:
            fetched, last = tied(fetched, last)
        out = compute(fetched)
        if move is not None:
            inbox[c] = [move(out)]
            last = out
    return written[0]


def solution(mesh):
    placed = (
        P("step", "seq", None),
        P("seq", None),
        P("step"),
        P(),
        P(),
        P(),
        P(),
        P(None, None, "seq"),
        P(None, "seq"),
        P("seq", None),
        P("seq", None),
    )
    return jax.shard_map(
        functools.partial(per_device, mesh.shape["step"], mesh.shape["seq"]),
        mesh=mesh,
        in_specs=placed,
        out_specs=P("step", "seq", None),
        check_vma=False,
    )
```

```python
import functools
import math

import jax
import jax.numpy as jnp
from jax import lax
from jax.experimental import pallas as pl
from jax.experimental.pallas import tpu as pltpu
from jax.sharding import PartitionSpec as P

eps = 1e-06
f32 = jnp.float32
bf16 = jnp.bfloat16
VM = pltpu.VMEM
MIB = 1024 * 1024


def params(mib):
    return pltpu.CompilerParams(vmem_limit_bytes=mib * MIB)


def cost(flops, moved):
    return pl.CostEstimate(flops=flops, transcendentals=0, bytes_accessed=moved)


def norm_kernel(t_ref, size_ref, x_hbm, mod_hbm, m_ref, sg_ref, x_ref, mod_ref, sem):
    width = x_hbm.shape[-1]
    pieces = sem.shape[0] - 1
    block = x_hbm.shape[1] // pieces
    t = t_ref[0]
    mod_copy = pltpu.make_async_copy(mod_hbm.at[pl.ds(t, 1), :], mod_ref, sem.at[pieces])
    mod_copy.start()
    copies = []
    for i in range(pieces):
        here = pl.ds(i * block, block)
        copies.append(pltpu.make_async_copy(x_hbm.at[0, here, :], x_ref.at[here, :], sem.at[i]))
        copies[i].start()
    mod_copy.wait()
    shift = mod_ref[:, :width]
    scale = 1.0 + mod_ref[:, width : 2 * width]
    sg_ref[...] = size_ref[t] * mod_ref[:, 2 * width :]
    for i in range(pieces):
        copies[i].wait()
        here = slice(i * block, (i + 1) * block)
        x = x_ref[here, :]
        center = x - jnp.mean(x, axis=-1, keepdims=True)
        spread = jnp.mean(center * center, axis=-1, keepdims=True)
        m_ref[here, :] = (center * lax.rsqrt(spread + eps) * scale + shift).astype(bf16)


def norm_call(t_idx, trajectory, mod_table, step_sizes):
    _, rows, width = trajectory.shape
    smem = pl.BlockSpec(memory_space=pltpu.SMEM)
    hbm = pl.BlockSpec(memory_space=pltpu.HBM)
    vm = pl.BlockSpec(memory_space=VM)
    return pl.pallas_call(
        norm_kernel,
        in_specs=[smem, smem, hbm, hbm],
        out_specs=[vm, vm],
        out_shape=[
            jax.ShapeDtypeStruct((rows, width), bf16),
            jax.ShapeDtypeStruct((1, width), f32),
        ],
        scratch_shapes=[
            VM((rows, width), f32),
            VM((1, 3 * width), f32),
            pltpu.SemaphoreType.DMA((5,)),
        ],
        compiler_params=params(60),
        cost_estimate=cost(10 * rows * width, 0),
        name="norm",
    )(t_idx, step_sizes, trajectory, mod_table)


def project_kernel(tile, load, tiles, m0, m1, qg, kg, *refs):
    if load:
        wq_hbm, wm_hbm, wb_hbm, q, k, v, act, low, high = refs[:9]
        held, rows, wb, sem = refs[9:-3], refs[-3], refs[-2], refs[-1]
    else:
        held = refs[:tiles]
        q, k, v, act, rows = refs[tiles:]
    half = m0.shape[0]
    head = qg.shape[1]
    n_q = q.shape[1] // tile
    copies = []
    if load:
        for i in range(tiles):
            if i < 3 * n_q:
                source = wq_hbm.at[i // n_q, :, pl.ds(i % n_q * tile, tile)]
            else:
                source = wm_hbm.at[:, pl.ds((i - 3 * n_q) * tile, tile)]
            copies.append(pltpu.make_async_copy(source, held[i], sem.at[i]))
            copies[i].start()
        span = low.shape[1] // (sem.shape[0] - tiles)
        for at in range(0, low.shape[1], span):
            here = (slice(None), pl.ds(at, span))
            copies.append(pltpu.make_async_copy(wb_hbm.at[here], wb.at[here], sem.at[len(copies)]))
            copies[-1].start()
    rows[:half] = m0[...]
    rows[half:] = m1[...]

    def normed(y, gain):
        parts = []
        for h in range(tile // head):
            one = y[:, h * head : (h + 1) * head]
            square = jnp.mean(one * one, axis=-1, keepdims=True)
            parts.append((one * lax.rsqrt(square + eps) * gain).astype(bf16))
        return jnp.concatenate(parts, axis=1)

    for i in range(tiles):
        if load:
            copies[i].wait()
        y = jnp.dot(rows[...], held[i][...], preferred_element_type=f32)
        cols = slice(i % n_q * tile, (i % n_q + 1) * tile)
        if i < n_q:
            q[:, cols] = normed(y, qg[...])
        elif i < 2 * n_q:
            k[:, cols] = normed(y, kg[...])
        elif i < 3 * n_q:
            v[:, cols] = y.astype(bf16)
        else:
            cols = slice((i - 3 * n_q) * tile, (i - 3 * n_q + 1) * tile)
            act[:, cols] = jax.nn.gelu(y, approximate=True).astype(bf16)
    if load:
        for i, copy in enumerate(copies[tiles:]):
            copy.wait()
            cols = slice(i * span, (i + 1) * span)
            y = jnp.dot(act[...], wb[:, cols], preferred_element_type=f32)
            low[:, cols] = y[:half]
            high[:, cols] = y[half:]


def project_call(m0, m1, q_gain, k_gain, w_qkv, w_mlp_in, w_out_mlp, held):
    half, width = m0.shape
    heads = w_qkv.shape[2]
    hidden = w_mlp_in.shape[1]
    tile = min(512, heads)
    tiles = (3 * heads + hidden) // tile
    rows = 2 * half
    load = held is None
    vm = pl.BlockSpec(memory_space=VM)
    hbm = pl.BlockSpec(memory_space=pltpu.HBM)
    shapes = [jax.ShapeDtypeStruct((rows, heads), bf16)] * 3
    shapes.append(jax.ShapeDtypeStruct((rows, hidden), bf16))
    scratch = [VM((rows, width), bf16)]
    if load:
        shapes += [jax.ShapeDtypeStruct((half, width), f32)] * 2
        shapes += [jax.ShapeDtypeStruct((width, tile), bf16)] * tiles
        scratch.append(VM(w_out_mlp.shape, bf16))
        scratch.append(pltpu.SemaphoreType.DMA((tiles + 4,)))
    return pl.pallas_call(
        functools.partial(project_kernel, tile, load, tiles),
        in_specs=[vm] * 4 + ([hbm] * 3 if load else [vm] * tiles),
        out_specs=[vm] * len(shapes),
        out_shape=shapes,
        scratch_shapes=scratch,
        compiler_params=params(27 if load else 9),
        cost_estimate=cost(2 * rows * width * (3 * heads + hidden), 0),
        name="project",
    )(m0, m1, q_gain, k_gain, *([w_qkv, w_mlp_in, w_out_mlp] if load else held))


def attend_kernel(pairs, head, *refs):
    q_ref = refs[0]
    k_refs = refs[1 : 1 + pairs]
    v_refs = refs[1 + pairs : 1 + 2 * pairs]
    out = refs[1 + 2 * pairs]
    scale = math.log2(math.e) / math.sqrt(head)
    for h in range(q_ref.shape[1] // head):
        cols = slice(h * head, (h + 1) * head)
        q = q_ref[:, cols]
        scores = [
            lax.dot_general(q, k[:, cols], (((1,), (1,)), ((), ())), preferred_element_type=f32)
            for k in k_refs
        ]
        top = functools.reduce(
            jnp.maximum, [jnp.max(s, axis=-1, keepdims=True) for s in scores]
        )
        weights = [jnp.exp2((s - top) * scale) for s in scores]
        total = sum(jnp.sum(w, axis=-1, keepdims=True) for w in weights)
        inverse = 1.0 / total
        mixed = sum(
            jnp.dot((w * inverse).astype(bf16), v[:, cols], preferred_element_type=f32)
            for w, v in zip(weights, v_refs)
        )
        out[:, cols] = mixed.astype(bf16)


def attend_call(q, ks, vs, head):
    vm = pl.BlockSpec(memory_space=VM)
    return pl.pallas_call(
        functools.partial(attend_kernel, len(ks), head),
        in_specs=[vm] * (1 + 2 * len(ks)),
        out_specs=vm,
        out_shape=jax.ShapeDtypeStruct(q.shape, bf16),
        compiler_params=params(9),
        cost_estimate=cost(4 * len(ks) * q.shape[0] ** 2 * q.shape[1] * 3, 0),
        name="attend",
    )(q, *ks, *vs)


def out_kernel(jobs, *refs):
    outs = refs[len(refs) - 2 * len(jobs) :]
    at = 0
    for turn, (parts, extras, first, count) in enumerate(jobs):
        xs = refs[at : at + parts]
        ws = refs[at + parts : at + 2 * parts]
        extra = refs[at + 2 * parts : at + 2 * parts + extras]
        at += 2 * parts + extras
        keep, send = outs[2 * turn : 2 * turn + 2]
        half = keep.shape[0]
        cols = slice(first, first + count)
        terms = [
            jnp.dot(x[...], w[:, cols], preferred_element_type=f32) for x, w in zip(xs, ws)
        ]
        y = functools.reduce(jnp.add, terms)
        low, high = y[:half], y[half:]
        if extra:
            low = low + extra[0][:, cols]
            high = high + extra[1][:, cols]
        keep[...] = low
        send[...] = high.astype(bf16)


def out_call(jobs):
    vm = pl.BlockSpec(memory_space=VM)
    given, plan, shapes, flops = [], [], [], 0
    for xs, ws, extra, first, count in jobs:
        given += [*xs, *ws, *extra]
        plan.append((len(xs), len(extra), first, count))
        half = xs[0].shape[0] // 2
        shapes.append(jax.ShapeDtypeStruct((half, count), f32))
        shapes.append(jax.ShapeDtypeStruct((half, count), bf16))
        flops += 4 * half * count * sum(x.shape[1] for x in xs)
    outs = pl.pallas_call(
        functools.partial(out_kernel, plan),
        in_specs=[vm] * len(given),
        out_specs=[vm] * len(shapes),
        out_shape=shapes,
        compiler_params=params(9),
        cost_estimate=cost(flops, 0),
        name="project_out",
    )(*given)
    return [tuple(outs[i : i + 2]) for i in range(0, len(outs), 2)]


def join_kernel(keep, sent, out):
    out[...] = (keep[...] + sent[...].astype(f32)).astype(bf16)


def join_call(keep, sent):
    vm = pl.BlockSpec(memory_space=VM)
    return pl.pallas_call(
        join_kernel,
        in_specs=[vm, vm],
        out_specs=vm,
        out_shape=jax.ShapeDtypeStruct(keep.shape, bf16),
        compiler_params=params(6),
        name="join",
    )(keep, sent)


def drift_kernel(first, parity, keep, sent, sg, *refs):
    fetched, (kept, other, send) = refs[:-3], refs[-3:]
    half, count = kept.shape
    p = parity[0]

    def part(which):
        rows = pl.ds(pl.multiple_of(which * half, half), half)
        branch = keep[rows, :] + sent[rows, :].astype(f32)
        for one in fetched:
            branch = branch + one[rows, :].astype(f32)
        return sg[:, first : first + count] * branch

    kept[...] = part(p)
    passed = part(1 - p)
    other[...] = passed
    send[...] = passed.astype(bf16)


def drift_call(parity, keep, sent, sg, fetched, first):
    rows, count = fetched[0].shape
    vm = pl.BlockSpec(memory_space=VM)
    smem = pl.BlockSpec(memory_space=pltpu.SMEM)
    shape = (rows // 2, count)
    return pl.pallas_call(
        functools.partial(drift_kernel, first),
        in_specs=[smem] + [vm] * (3 + len(fetched)),
        out_specs=[vm] * 3,
        out_shape=[
            jax.ShapeDtypeStruct(shape, f32),
            jax.ShapeDtypeStruct(shape, f32),
            jax.ShapeDtypeStruct(shape, bf16),
        ],
        compiler_params=params(6),
        name="drift",
    )(parity, keep, sent, sg, *fetched)


def finish_kernel(first, parity, x_start, earlier, kept, fetched, other, back, *refs):
    out, result, sem = refs[-3:]
    half, count = kept.shape
    cols = slice(first, first + count)
    p = parity[0]
    mine = pl.ds(pl.multiple_of(p * half, half), half)
    rest = pl.ds(pl.multiple_of((1 - p) * half, half), half)
    odd = p.astype(f32)
    result[mine, :] = x_start[mine, cols] + earlier[...] + kept[...] + odd * fetched[...].astype(f32)
    result[rest, :] = x_start[rest, cols] + other[...] + back[...].astype(f32)
    copy = pltpu.make_async_copy(result, out.at[0, :, pl.ds(first, count)], sem)
    copy.start()
    copy.wait()


def finish_call(parity, x_start, earlier, kept, fetched, other, back, into, first):
    rows, width = x_start.shape
    vm = pl.BlockSpec(memory_space=VM)
    smem = pl.BlockSpec(memory_space=pltpu.SMEM)
    hbm = pl.BlockSpec(memory_space=pltpu.HBM)
    given = [parity, x_start, earlier, kept, fetched, other, back]
    return pl.pallas_call(
        functools.partial(finish_kernel, first),
        in_specs=[smem] + [vm] * 6 + [hbm] * len(into),
        out_specs=hbm,
        out_shape=jax.ShapeDtypeStruct((1, rows, width), f32),
        scratch_shapes=[VM((rows, kept.shape[1]), f32), pltpu.SemaphoreType.DMA],
        input_output_aliases={len(given): 0} if into else {},
        compiler_params=params(6),
        name="finish",
    )(*given, *into)


def per_device(
    n_step,
    n_seq,
    trajectory,
    x_start,
    t_idx,
    mod_table,
    step_sizes,
    q_gain,
    k_gain,
    w_qkv,
    w_mlp_in,
    w_out_attn,
    w_out_mlp,
):
    head = q_gain.shape[0]
    rows, width = x_start.shape
    chips = n_seq // 2
    groups = n_step // 2
    half = rows // 2
    unit = width // 24
    counts = [10 * unit, 8 * unit, 6 * unit]
    chunks = len(counts)
    firsts = [sum(counts[:c]) for c in range(chunks)]
    qg, kg = q_gain[None, :], k_gain[None, :]

    def to_core(x):
        return lax.ppermute(x, "seq", [(i, i ^ 1) for i in range(n_seq)])

    def to_chip(x, offset):
        return lax.ppermute(x, "seq", [(i, (i + 2 * offset) % n_seq) for i in range(n_seq)])

    def to_pair(x):
        return lax.ppermute(x, "step", [(i, i ^ 1) for i in range(n_step)])

    def tied(*values):
        return lax.optimization_barrier(values)

    parity = lax.rem(lax.axis_index("step"), 2)
    even = (parity == 0).astype(f32)
    which = parity[None]
    offsets = range(1, chips)

    mine, sg = norm_call(t_idx, trajectory, mod_table, step_sizes)
    far = [to_chip(mine, j) for j in offsets]
    q0, k0, v0, act0, low0, high0, *held = project_call(
        mine, to_core(mine), qg, kg, w_qkv, w_mlp_in, w_out_mlp, None
    )
    far, low0, high0 = tied(far, low0, high0)
    qs, ks, vs, acts = [], [k0], [v0], []
    for block in far:
        q, k, v, act = project_call(block, to_core(block), qg, kg, w_qkv, w_mlp_in, w_out_mlp, held)
        qs.append(q)
        ks.append(k)
        vs.append(v)
        acts.append(act)
    mixed = [attend_call(q, ks, vs, head) for q in qs]

    weights = [w_out_attn, w_out_mlp]
    got = [[] for _ in offsets]

    def jobs_of(c):
        return [([a, b], weights, [], firsts[c], counts[c]) for a, b in zip(mixed, acts)]

    def joined(parts, sent):
        return [join_call(keep, s) for (keep, _), s in zip(parts, sent)]

    def to_chips(ready):
        for j, one in enumerate(ready):
            got[j].append(to_chip(one, chips - 1 - j))

    parts = out_call(jobs_of(0))
    sent = [to_core(send) for _, send in parts]
    q0, parts = tied(q0, parts)
    mixed0 = attend_call(q0, ks, vs, head)
    mixed0, sent = tied(mixed0, sent)
    ready = joined(parts, sent)
    mixed, acts, mixed0, ready = tied(mixed, acts, mixed0, ready)
    to_chips(ready)
    jobs = [job for c in range(1, chunks) for job in jobs_of(c)]
    for c in range(chunks):
        jobs.append(([mixed0], [w_out_attn], [low0, high0], firsts[c], counts[c]))
    parts = out_call(jobs)
    sent = [to_core(send) for _, send in parts]
    keep = [part[0] for part in parts[-chunks:]]
    sent0 = sent[-chunks:]
    others = chips - 1
    later = []
    for c in range(1, chunks):
        here = slice((c - 1) * others, c * others)
        later.append(joined(parts[here], sent[here]))
    first, keep, later = tied([row[0] for row in got], keep, later)
    for row, one in zip(got, first):
        row[0] = one
    for ready in later:
        to_chips(ready)

    def along(pairs):
        return lambda x: lax.ppermute(x, "step", [(2 * a + i, 2 * b + i) for a, b in pairs for i in (0, 1)])

    group = lax.div(lax.axis_index("step"), 2)
    spans = []
    while 2 ** len(spans) < groups:
        spans.append(2 ** len(spans))

    def swap(span):
        return along([(b, b ^ span) for b in range(groups) if b ^ span < groups])

    def prefix_stages(c, halves):
        held = {}
        quarter = half // 2
        bit = lax.rem(group, 2)

        def drift_of(fetched):
            drift = drift_call(which, keep[c], sent0[c], sg, fetched, firsts[c])
            held["kept"], held["other"], send = drift
            return send

        def pair_sum(fetched):
            held["fetched"] = fetched[0]
            held["total"] = held["kept"] + fetched[0].astype(f32)
            return held["total"].astype(bf16)

        def collect(r, fetched):
            one = fetched[0]
            if halves and spans[r] == 2:
                both = [held["piece"], one]
                one = jnp.where(
                    bit == 0, jnp.concatenate(both, axis=0), jnp.concatenate(both[::-1], axis=0)
                )
            one = one.astype(f32)
            upper = (lax.rem(lax.div(group, spans[r]), 2) == 1).astype(f32)
            held["earlier"] = held["earlier"] + upper * one if r else upper * one
            if r == len(spans) - 1:
                return (held["earlier"] + even * held["kept"]).astype(bf16)
            held["total"] = held["total"] + one
            total = held["total"].astype(bf16)
            if halves and spans[r + 1] == 2:
                return lax.dynamic_slice_in_dim(total, bit * quarter, quarter, 0)
            return total

        def pass_on(fetched):
            held["piece"] = fetched[0]
            return fetched[0]

        def finish(fetched):
            given = [held[name] for name in ("earlier", "kept", "fetched", "other")]
            fetched, into = tied(fetched, list(written))
            written[:] = [finish_call(which, x_start, *given, fetched[0], into, firsts[c])]

        stages = [(drift_of, to_pair, "x", 0.5), (pair_sum, swap(1), "z1", 0.5)]
        for r in range(len(spans)):
            take = functools.partial(collect, r)
            if r == len(spans) - 1:
                stages.append((take, to_pair, "x", 0.5))
            elif halves and spans[r + 1] == 2:
                stages.append((take, swap(2), "z2", 0.5))
                stages.append((pass_on, swap(1), "z1", 0.25))
            else:
                stages.append((take, swap(spans[r + 1]), "z2", 1.0))
        stages.append((finish, None, "", 0.0))
        return stages

    plan = [prefix_stages(c, c == 0) for c in range(chunks)]
    inbox = [[got[j][c] for j in range(chips - 1)] for c in range(chunks)]
    shares = [18.5 * n / width for n in counts]
    ends = [2.0 * c + sum(shares[: c + 1]) for c in range(chunks)]
    waits = [(end, c, 0) for c, end in enumerate(ends)]
    free = {"x": 0.0, "z1": 0.0, "z2": 0.0, "": 0.0}
    turns = []
    while waits:
        when, c, i = min(waits)
        waits.remove((when, c, i))
        turns.append((c, i))
        if i + 1 < len(plan[c]):
            link, load = plan[c][i][2:]
            begin = max(when + 1.5, free[link])
            free[link] = begin + load * shares[c]
            waits.append((free[link] + 0.7, c, i + 1))
    written = []
    last = None
    for c, i in turns:
        compute, move = plan[c][i][:2]
        fetched = inbox[c]
        if last is not None:
            fetched, last = tied(fetched, last)
        out = compute(fetched)
        if move is not None:
            inbox[c] = [move(out)]
            last = out
    return written[0]


def solution(mesh):
    placed = (
        P("step", "seq", None),
        P("seq", None),
        P("step"),
        P(),
        P(),
        P(),
        P(),
        P(None, None, "seq"),
        P(None, "seq"),
        P("seq", None),
        P("seq", None),
    )
    return jax.shard_map(
        functools.partial(per_device, mesh.shape["step"], mesh.shape["seq"]),
        mesh=mesh,
        in_specs=placed,
        out_specs=P("step", "seq", None),
        check_vma=False,
    )
```

```python
import functools
import math

import jax
import jax.numpy as jnp
from jax import lax
from jax.experimental import pallas as pl
from jax.experimental.pallas import tpu as pltpu
from jax.sharding import PartitionSpec as P

eps = 1e-06
f32 = jnp.float32
bf16 = jnp.bfloat16
VM = pltpu.VMEM
MIB = 1024 * 1024


def params(mib):
    return pltpu.CompilerParams(vmem_limit_bytes=mib * MIB)


def cost(flops, moved):
    return pl.CostEstimate(flops=flops, transcendentals=0, bytes_accessed=moved)


def norm_kernel(t_ref, size_ref, x_hbm, mod_hbm, m_ref, sg_ref, x_ref, mod_ref, sem):
    width = x_hbm.shape[-1]
    pieces = sem.shape[0] - 1
    block = x_hbm.shape[1] // pieces
    t = t_ref[0]
    mod_copy = pltpu.make_async_copy(mod_hbm.at[pl.ds(t, 1), :], mod_ref, sem.at[pieces])
    mod_copy.start()
    copies = []
    for i in range(pieces):
        here = pl.ds(i * block, block)
        copies.append(pltpu.make_async_copy(x_hbm.at[0, here, :], x_ref.at[here, :], sem.at[i]))
        copies[i].start()
    mod_copy.wait()
    shift = mod_ref[:, :width]
    scale = 1.0 + mod_ref[:, width : 2 * width]
    sg_ref[...] = size_ref[t] * mod_ref[:, 2 * width :]
    for i in range(pieces):
        copies[i].wait()
        here = slice(i * block, (i + 1) * block)
        x = x_ref[here, :]
        center = x - jnp.mean(x, axis=-1, keepdims=True)
        spread = jnp.mean(center * center, axis=-1, keepdims=True)
        m_ref[here, :] = (center * lax.rsqrt(spread + eps) * scale + shift).astype(bf16)


def norm_call(t_idx, trajectory, mod_table, step_sizes):
    _, rows, width = trajectory.shape
    smem = pl.BlockSpec(memory_space=pltpu.SMEM)
    hbm = pl.BlockSpec(memory_space=pltpu.HBM)
    vm = pl.BlockSpec(memory_space=VM)
    return pl.pallas_call(
        norm_kernel,
        in_specs=[smem, smem, hbm, hbm],
        out_specs=[vm, vm],
        out_shape=[
            jax.ShapeDtypeStruct((rows, width), bf16),
            jax.ShapeDtypeStruct((1, width), f32),
        ],
        scratch_shapes=[
            VM((rows, width), f32),
            VM((1, 3 * width), f32),
            pltpu.SemaphoreType.DMA((5,)),
        ],
        compiler_params=params(60),
        cost_estimate=cost(10 * rows * width, 0),
        name="norm",
    )(t_idx, step_sizes, trajectory, mod_table)


def project_kernel(tile, load, tiles, m0, m1, qg, kg, *refs):
    if load:
        wq_hbm, wm_hbm, wb_hbm, q, k, v, act, low, high = refs[:9]
        held, rows, wb, sem = refs[9:-3], refs[-3], refs[-2], refs[-1]
    else:
        held = refs[:tiles]
        q, k, v, act, rows = refs[tiles:]
    half = m0.shape[0]
    head = qg.shape[1]
    n_q = q.shape[1] // tile
    copies = []
    if load:
        for i in range(tiles):
            if i < 3 * n_q:
                source = wq_hbm.at[i // n_q, :, pl.ds(i % n_q * tile, tile)]
            else:
                source = wm_hbm.at[:, pl.ds((i - 3 * n_q) * tile, tile)]
            copies.append(pltpu.make_async_copy(source, held[i], sem.at[i]))
            copies[i].start()
        span = low.shape[1] // (sem.shape[0] - tiles)
        for at in range(0, low.shape[1], span):
            here = (slice(None), pl.ds(at, span))
            copies.append(pltpu.make_async_copy(wb_hbm.at[here], wb.at[here], sem.at[len(copies)]))
            copies[-1].start()
    rows[:half] = m0[...]
    rows[half:] = m1[...]

    def normed(y, gain):
        parts = []
        for h in range(tile // head):
            one = y[:, h * head : (h + 1) * head]
            square = jnp.mean(one * one, axis=-1, keepdims=True)
            parts.append((one * lax.rsqrt(square + eps) * gain).astype(bf16))
        return jnp.concatenate(parts, axis=1)

    for i in range(tiles):
        if load:
            copies[i].wait()
        y = jnp.dot(rows[...], held[i][...], preferred_element_type=f32)
        cols = slice(i % n_q * tile, (i % n_q + 1) * tile)
        if i < n_q:
            q[:, cols] = normed(y, qg[...])
        elif i < 2 * n_q:
            k[:, cols] = normed(y, kg[...])
        elif i < 3 * n_q:
            v[:, cols] = y.astype(bf16)
        else:
            cols = slice((i - 3 * n_q) * tile, (i - 3 * n_q + 1) * tile)
            act[:, cols] = jax.nn.gelu(y, approximate=True).astype(bf16)
    if load:
        for i, copy in enumerate(copies[tiles:]):
            copy.wait()
            cols = slice(i * span, (i + 1) * span)
            y = jnp.dot(act[...], wb[:, cols], preferred_element_type=f32)
            low[:, cols] = y[:half]
            high[:, cols] = y[half:]


def project_call(m0, m1, q_gain, k_gain, w_qkv, w_mlp_in, w_out_mlp, held):
    half, width = m0.shape
    heads = w_qkv.shape[2]
    hidden = w_mlp_in.shape[1]
    tile = min(512, heads)
    tiles = (3 * heads + hidden) // tile
    rows = 2 * half
    load = held is None
    vm = pl.BlockSpec(memory_space=VM)
    hbm = pl.BlockSpec(memory_space=pltpu.HBM)
    shapes = [jax.ShapeDtypeStruct((rows, heads), bf16)] * 3
    shapes.append(jax.ShapeDtypeStruct((rows, hidden), bf16))
    scratch = [VM((rows, width), bf16)]
    if load:
        shapes += [jax.ShapeDtypeStruct((half, width), f32)] * 2
        shapes += [jax.ShapeDtypeStruct((width, tile), bf16)] * tiles
        scratch.append(VM(w_out_mlp.shape, bf16))
        scratch.append(pltpu.SemaphoreType.DMA((tiles + 4,)))
    return pl.pallas_call(
        functools.partial(project_kernel, tile, load, tiles),
        in_specs=[vm] * 4 + ([hbm] * 3 if load else [vm] * tiles),
        out_specs=[vm] * len(shapes),
        out_shape=shapes,
        scratch_shapes=scratch,
        compiler_params=params(27 if load else 9),
        cost_estimate=cost(2 * rows * width * (3 * heads + hidden), 0),
        name="project",
    )(m0, m1, q_gain, k_gain, *([w_qkv, w_mlp_in, w_out_mlp] if load else held))


def attend_kernel(pairs, head, *refs):
    q_ref = refs[0]
    k_refs = refs[1 : 1 + pairs]
    v_refs = refs[1 + pairs : 1 + 2 * pairs]
    out = refs[1 + 2 * pairs]
    scale = math.log2(math.e) / math.sqrt(head)
    for h in range(q_ref.shape[1] // head):
        cols = slice(h * head, (h + 1) * head)
        q = q_ref[:, cols]
        scores = [
            lax.dot_general(q, k[:, cols], (((1,), (1,)), ((), ())), preferred_element_type=f32)
            for k in k_refs
        ]
        top = functools.reduce(
            jnp.maximum, [jnp.max(s, axis=-1, keepdims=True) for s in scores]
        )
        weights = [jnp.exp2((s - top) * scale) for s in scores]
        total = sum(jnp.sum(w, axis=-1, keepdims=True) for w in weights)
        inverse = 1.0 / total
        mixed = sum(
            jnp.dot((w * inverse).astype(bf16), v[:, cols], preferred_element_type=f32)
            for w, v in zip(weights, v_refs)
        )
        out[:, cols] = mixed.astype(bf16)


def attend_call(q, ks, vs, head):
    vm = pl.BlockSpec(memory_space=VM)
    return pl.pallas_call(
        functools.partial(attend_kernel, len(ks), head),
        in_specs=[vm] * (1 + 2 * len(ks)),
        out_specs=vm,
        out_shape=jax.ShapeDtypeStruct(q.shape, bf16),
        compiler_params=params(9),
        cost_estimate=cost(4 * len(ks) * q.shape[0] ** 2 * q.shape[1] * 3, 0),
        name="attend",
    )(q, *ks, *vs)


def out_kernel(jobs, *refs):
    outs = refs[len(refs) - 2 * len(jobs) :]
    at = 0
    for turn, (parts, extras, first, count) in enumerate(jobs):
        xs = refs[at : at + parts]
        ws = refs[at + parts : at + 2 * parts]
        extra = refs[at + 2 * parts : at + 2 * parts + extras]
        at += 2 * parts + extras
        keep, send = outs[2 * turn : 2 * turn + 2]
        half = keep.shape[0]
        cols = slice(first, first + count)
        terms = [
            jnp.dot(x[...], w[:, cols], preferred_element_type=f32) for x, w in zip(xs, ws)
        ]
        y = functools.reduce(jnp.add, terms)
        low, high = y[:half], y[half:]
        if extra:
            low = low + extra[0][:, cols]
            high = high + extra[1][:, cols]
        keep[...] = low
        send[...] = high.astype(bf16)


def out_call(jobs):
    vm = pl.BlockSpec(memory_space=VM)
    given, plan, shapes, flops = [], [], [], 0
    for xs, ws, extra, first, count in jobs:
        given += [*xs, *ws, *extra]
        plan.append((len(xs), len(extra), first, count))
        half = xs[0].shape[0] // 2
        shapes.append(jax.ShapeDtypeStruct((half, count), f32))
        shapes.append(jax.ShapeDtypeStruct((half, count), bf16))
        flops += 4 * half * count * sum(x.shape[1] for x in xs)
    outs = pl.pallas_call(
        functools.partial(out_kernel, plan),
        in_specs=[vm] * len(given),
        out_specs=[vm] * len(shapes),
        out_shape=shapes,
        compiler_params=params(9),
        cost_estimate=cost(flops, 0),
        name="project_out",
    )(*given)
    return [tuple(outs[i : i + 2]) for i in range(0, len(outs), 2)]


def join_kernel(keep, sent, out):
    out[...] = (keep[...] + sent[...].astype(f32)).astype(bf16)


def join_call(keep, sent):
    vm = pl.BlockSpec(memory_space=VM)
    return pl.pallas_call(
        join_kernel,
        in_specs=[vm, vm],
        out_specs=vm,
        out_shape=jax.ShapeDtypeStruct(keep.shape, bf16),
        compiler_params=params(6),
        name="join",
    )(keep, sent)


def drift_kernel(first, parity, keep, sent, sg, *refs):
    fetched, (kept, other, send) = refs[:-3], refs[-3:]
    half, count = kept.shape
    p = parity[0]

    def part(which):
        rows = pl.ds(pl.multiple_of(which * half, half), half)
        branch = keep[rows, :] + sent[rows, :].astype(f32)
        for one in fetched:
            branch = branch + one[rows, :].astype(f32)
        return sg[:, first : first + count] * branch

    kept[...] = part(p)
    passed = part(1 - p)
    other[...] = passed
    send[...] = passed.astype(bf16)


def drift_call(parity, keep, sent, sg, fetched, first):
    rows, count = fetched[0].shape
    vm = pl.BlockSpec(memory_space=VM)
    smem = pl.BlockSpec(memory_space=pltpu.SMEM)
    shape = (rows // 2, count)
    return pl.pallas_call(
        functools.partial(drift_kernel, first),
        in_specs=[smem] + [vm] * (3 + len(fetched)),
        out_specs=[vm] * 3,
        out_shape=[
            jax.ShapeDtypeStruct(shape, f32),
            jax.ShapeDtypeStruct(shape, f32),
            jax.ShapeDtypeStruct(shape, bf16),
        ],
        compiler_params=params(6),
        name="drift",
    )(parity, keep, sent, sg, *fetched)


def finish_kernel(first, parity, x_start, earlier, kept, fetched, other, back, *refs):
    out, result, sem = refs[-3:]
    half, count = kept.shape
    cols = slice(first, first + count)
    p = parity[0]
    mine = pl.ds(pl.multiple_of(p * half, half), half)
    rest = pl.ds(pl.multiple_of((1 - p) * half, half), half)
    odd = p.astype(f32)
    result[mine, :] = x_start[mine, cols] + earlier[...] + kept[...] + odd * fetched[...].astype(f32)
    result[rest, :] = x_start[rest, cols] + other[...] + back[...].astype(f32)
    copy = pltpu.make_async_copy(result, out.at[0, :, pl.ds(first, count)], sem)
    copy.start()
    copy.wait()


def finish_call(parity, x_start, earlier, kept, fetched, other, back, into, first):
    rows, width = x_start.shape
    vm = pl.BlockSpec(memory_space=VM)
    smem = pl.BlockSpec(memory_space=pltpu.SMEM)
    hbm = pl.BlockSpec(memory_space=pltpu.HBM)
    given = [parity, x_start, earlier, kept, fetched, other, back]
    return pl.pallas_call(
        functools.partial(finish_kernel, first),
        in_specs=[smem] + [vm] * 6 + [hbm] * len(into),
        out_specs=hbm,
        out_shape=jax.ShapeDtypeStruct((1, rows, width), f32),
        scratch_shapes=[VM((rows, kept.shape[1]), f32), pltpu.SemaphoreType.DMA],
        input_output_aliases={len(given): 0} if into else {},
        compiler_params=params(6),
        name="finish",
    )(*given, *into)


def per_device(
    n_step,
    n_seq,
    trajectory,
    x_start,
    t_idx,
    mod_table,
    step_sizes,
    q_gain,
    k_gain,
    w_qkv,
    w_mlp_in,
    w_out_attn,
    w_out_mlp,
):
    head = q_gain.shape[0]
    rows, width = x_start.shape
    chips = n_seq // 2
    groups = n_step // 2
    half = rows // 2
    unit = width // 24
    counts = [10 * unit, 8 * unit, 6 * unit]
    chunks = len(counts)
    firsts = [sum(counts[:c]) for c in range(chunks)]
    qg, kg = q_gain[None, :], k_gain[None, :]

    def to_core(x):
        return lax.ppermute(x, "seq", [(i, i ^ 1) for i in range(n_seq)])

    def to_chip(x, offset):
        return lax.ppermute(x, "seq", [(i, (i + 2 * offset) % n_seq) for i in range(n_seq)])

    def to_pair(x):
        return lax.ppermute(x, "step", [(i, i ^ 1) for i in range(n_step)])

    def tied(*values):
        return lax.optimization_barrier(values)

    parity = lax.rem(lax.axis_index("step"), 2)
    even = (parity == 0).astype(f32)
    which = parity[None]
    offsets = range(1, chips)

    mine, sg = norm_call(t_idx, trajectory, mod_table, step_sizes)
    far = [to_chip(mine, j) for j in offsets]
    q0, k0, v0, act0, low0, high0, *held = project_call(
        mine, to_core(mine), qg, kg, w_qkv, w_mlp_in, w_out_mlp, None
    )
    far, low0, high0 = tied(far, low0, high0)
    qs, ks, vs, acts = [], [k0], [v0], []
    for block in far:
        q, k, v, act = project_call(block, to_core(block), qg, kg, w_qkv, w_mlp_in, w_out_mlp, held)
        qs.append(q)
        ks.append(k)
        vs.append(v)
        acts.append(act)
    mixed = [attend_call(q, ks, vs, head) for q in qs]

    weights = [w_out_attn, w_out_mlp]
    got = [[] for _ in offsets]

    def jobs_of(c):
        return [([a, b], weights, [], firsts[c], counts[c]) for a, b in zip(mixed, acts)]

    def joined(parts, sent):
        return [join_call(keep, s) for (keep, _), s in zip(parts, sent)]

    def to_chips(ready):
        for j, one in enumerate(ready):
            got[j].append(to_chip(one, chips - 1 - j))

    parts = out_call(jobs_of(0))
    sent = [to_core(send) for _, send in parts]
    q0, parts = tied(q0, parts)
    mixed0 = attend_call(q0, ks, vs, head)
    mixed0, sent = tied(mixed0, sent)
    ready = joined(parts, sent)
    mixed, acts, mixed0, ready = tied(mixed, acts, mixed0, ready)
    to_chips(ready)
    jobs = [job for c in range(1, chunks) for job in jobs_of(c)]
    for c in range(chunks):
        jobs.append(([mixed0], [w_out_attn], [low0, high0], firsts[c], counts[c]))
    parts = out_call(jobs)
    sent = [to_core(send) for _, send in parts]
    keep = [part[0] for part in parts[-chunks:]]
    sent0 = sent[-chunks:]
    others = chips - 1
    later = []
    for c in range(1, chunks):
        here = slice((c - 1) * others, c * others)
        later.append(joined(parts[here], sent[here]))
    first, later = tied([row[0] for row in got], later)
    for row, one in zip(got, first):
        row[0] = one
    for ready in later:
        to_chips(ready)

    def along(pairs):
        return lambda x: lax.ppermute(x, "step", [(2 * a + i, 2 * b + i) for a, b in pairs for i in (0, 1)])

    group = lax.div(lax.axis_index("step"), 2)
    spans = []
    while 2 ** len(spans) < groups:
        spans.append(2 ** len(spans))

    def swap(span):
        return along([(b, b ^ span) for b in range(groups) if b ^ span < groups])

    def prefix_stages(c, halves):
        held = {}
        quarter = half // 2
        bit = lax.rem(group, 2)

        def drift_of(fetched):
            drift = drift_call(which, keep[c], sent0[c], sg, fetched, firsts[c])
            held["kept"], held["other"], send = drift
            return send

        def pair_sum(fetched):
            held["fetched"] = fetched[0]
            held["total"] = held["kept"] + fetched[0].astype(f32)
            return held["total"].astype(bf16)

        def collect(r, fetched):
            one = fetched[0]
            if halves and spans[r] == 2:
                both = [held["piece"], one]
                one = jnp.where(
                    bit == 0, jnp.concatenate(both, axis=0), jnp.concatenate(both[::-1], axis=0)
                )
            one = one.astype(f32)
            upper = (lax.rem(lax.div(group, spans[r]), 2) == 1).astype(f32)
            held["earlier"] = held["earlier"] + upper * one if r else upper * one
            if r == len(spans) - 1:
                return (held["earlier"] + even * held["kept"]).astype(bf16)
            held["total"] = held["total"] + one
            total = held["total"].astype(bf16)
            if halves and spans[r + 1] == 2:
                return lax.dynamic_slice_in_dim(total, bit * quarter, quarter, 0)
            return total

        def pass_on(fetched):
            held["piece"] = fetched[0]
            return fetched[0]

        def finish(fetched):
            given = [held[name] for name in ("earlier", "kept", "fetched", "other")]
            into = list(written)
            written[:] = [finish_call(which, x_start, *given, fetched[0], into, firsts[c])]

        stages = [(drift_of, to_pair, "x", 0.5), (pair_sum, swap(1), "z1", 0.5)]
        for r in range(len(spans)):
            take = functools.partial(collect, r)
            if r == len(spans) - 1:
                stages.append((take, to_pair, "x", 0.5))
            elif halves and spans[r + 1] == 2:
                stages.append((take, swap(2), "z2", 0.5))
                stages.append((pass_on, swap(1), "z1", 0.25))
            else:
                stages.append((take, swap(spans[r + 1]), "z2", 1.0))
        stages.append((finish, None, "", 0.0))
        return stages

    plan = [prefix_stages(c, c == 0) for c in range(chunks)]
    inbox = [[got[j][c] for j in range(chips - 1)] for c in range(chunks)]
    shares = [18.5 * n / width for n in counts]
    ends = [2.0 * c + sum(shares[: c + 1]) for c in range(chunks)]
    waits = [(end, c, 0) for c, end in enumerate(ends)]
    free = {"x": 0.0, "z1": 0.0, "z2": 0.0, "": 0.0}
    turns = []
    while waits:
        when, c, i = min(waits)
        waits.remove((when, c, i))
        turns.append((c, i))
        if i + 1 < len(plan[c]):
            link, load = plan[c][i][2:]
            begin = max(when + 1.5, free[link])
            free[link] = begin + load * shares[c]
            waits.append((free[link] + 0.7, c, i + 1))
    written = []
    last = None
    for c, i in turns:
        compute, move = plan[c][i][:2]
        fetched = inbox[c]
        if last is not None:
            fetched, last = tied(fetched, last)
        out = compute(fetched)
        if move is not None:
            inbox[c] = [move(out)]
            last = out
    return written[0]


def solution(mesh):
    placed = (
        P("step", "seq", None),
        P("seq", None),
        P("step"),
        P(),
        P(),
        P(),
        P(),
        P(None, None, "seq"),
        P(None, "seq"),
        P("seq", None),
        P("seq", None),
    )
    return jax.shard_map(
        functools.partial(per_device, mesh.shape["step"], mesh.shape["seq"]),
        mesh=mesh,
        in_specs=placed,
        out_specs=P("step", "seq", None),
        check_vma=False,
    )
```

```python
import functools
import math

import jax
import jax.numpy as jnp
from jax import lax
from jax.experimental import pallas as pl
from jax.experimental.pallas import tpu as pltpu
from jax.sharding import PartitionSpec as P

eps = 1e-06
f32 = jnp.float32
bf16 = jnp.bfloat16
VM = pltpu.VMEM
MIB = 1024 * 1024


def params(mib):
    return pltpu.CompilerParams(vmem_limit_bytes=mib * MIB)


def cost(flops, moved):
    return pl.CostEstimate(flops=flops, transcendentals=0, bytes_accessed=moved)


def norm_kernel(t_ref, size_ref, x_hbm, mod_hbm, m_ref, sg_ref, x_ref, mod_ref, sem):
    width = x_hbm.shape[-1]
    pieces = sem.shape[0] - 1
    block = x_hbm.shape[1] // pieces
    t = t_ref[0]
    mod_copy = pltpu.make_async_copy(mod_hbm.at[pl.ds(t, 1), :], mod_ref, sem.at[pieces])
    mod_copy.start()
    copies = []
    for i in range(pieces):
        here = pl.ds(i * block, block)
        copies.append(pltpu.make_async_copy(x_hbm.at[0, here, :], x_ref.at[here, :], sem.at[i]))
        copies[i].start()
    mod_copy.wait()
    shift = mod_ref[:, :width]
    scale = 1.0 + mod_ref[:, width : 2 * width]
    sg_ref[...] = size_ref[t] * mod_ref[:, 2 * width :]
    for i in range(pieces):
        copies[i].wait()
        here = slice(i * block, (i + 1) * block)
        x = x_ref[here, :]
        center = x - jnp.mean(x, axis=-1, keepdims=True)
        spread = jnp.mean(center * center, axis=-1, keepdims=True)
        m_ref[here, :] = (center * lax.rsqrt(spread + eps) * scale + shift).astype(bf16)


def norm_call(t_idx, trajectory, mod_table, step_sizes):
    _, rows, width = trajectory.shape
    smem = pl.BlockSpec(memory_space=pltpu.SMEM)
    hbm = pl.BlockSpec(memory_space=pltpu.HBM)
    vm = pl.BlockSpec(memory_space=VM)
    return pl.pallas_call(
        norm_kernel,
        in_specs=[smem, smem, hbm, hbm],
        out_specs=[vm, vm],
        out_shape=[
            jax.ShapeDtypeStruct((rows, width), bf16),
            jax.ShapeDtypeStruct((1, width), f32),
        ],
        scratch_shapes=[
            VM((rows, width), f32),
            VM((1, 3 * width), f32),
            pltpu.SemaphoreType.DMA((5,)),
        ],
        compiler_params=params(60),
        cost_estimate=cost(10 * rows * width, 0),
        name="norm",
    )(t_idx, step_sizes, trajectory, mod_table)


def project_kernel(tile, load, tiles, m0, m1, qg, kg, *refs):
    if load:
        wq_hbm, wm_hbm, q, k, v, act = refs[:6]
        held, rows, sem = refs[6:-2], refs[-2], refs[-1]
    else:
        held = refs[:tiles]
        q, k, v, act, rows = refs[tiles:]
    half = m0.shape[0]
    head = qg.shape[1]
    n_q = q.shape[1] // tile
    copies = []
    if load:
        for i in range(tiles):
            if i < 3 * n_q:
                source = wq_hbm.at[i // n_q, :, pl.ds(i % n_q * tile, tile)]
            else:
                source = wm_hbm.at[:, pl.ds((i - 3 * n_q) * tile, tile)]
            copies.append(pltpu.make_async_copy(source, held[i], sem.at[i]))
            copies[i].start()
    rows[:half] = m0[...]
    rows[half:] = m1[...]

    def normed(y, gain):
        parts = []
        for h in range(tile // head):
            one = y[:, h * head : (h + 1) * head]
            square = jnp.mean(one * one, axis=-1, keepdims=True)
            parts.append((one * lax.rsqrt(square + eps) * gain).astype(bf16))
        return jnp.concatenate(parts, axis=1)

    for i in range(tiles):
        if load:
            copies[i].wait()
        y = jnp.dot(rows[...], held[i][...], preferred_element_type=f32)
        cols = slice(i % n_q * tile, (i % n_q + 1) * tile)
        if i < n_q:
            q[:, cols] = normed(y, qg[...])
        elif i < 2 * n_q:
            k[:, cols] = normed(y, kg[...])
        elif i < 3 * n_q:
            v[:, cols] = y.astype(bf16)
        else:
            cols = slice((i - 3 * n_q) * tile, (i - 3 * n_q + 1) * tile)
            act[:, cols] = jax.nn.gelu(y, approximate=True).astype(bf16)


def project_call(m0, m1, q_gain, k_gain, w_qkv, w_mlp_in, held):
    half, width = m0.shape
    heads = w_qkv.shape[2]
    hidden = w_mlp_in.shape[1]
    tile = min(512, heads)
    tiles = (3 * heads + hidden) // tile
    rows = 2 * half
    load = held is None
    vm = pl.BlockSpec(memory_space=VM)
    hbm = pl.BlockSpec(memory_space=pltpu.HBM)
    shapes = [jax.ShapeDtypeStruct((rows, heads), bf16)] * 3
    shapes.append(jax.ShapeDtypeStruct((rows, hidden), bf16))
    scratch = [VM((rows, width), bf16)]
    if load:
        shapes += [jax.ShapeDtypeStruct((width, tile), bf16)] * tiles
        scratch.append(pltpu.SemaphoreType.DMA((tiles,)))
    return pl.pallas_call(
        functools.partial(project_kernel, tile, load, tiles),
        in_specs=[vm] * 4 + ([hbm] * 2 if load else [vm] * tiles),
        out_specs=[vm] * len(shapes),
        out_shape=shapes,
        scratch_shapes=scratch,
        compiler_params=params(27 if load else 9),
        cost_estimate=cost(2 * rows * width * (3 * heads + hidden), 0),
        name="project",
    )(m0, m1, q_gain, k_gain, *([w_qkv, w_mlp_in] if load else held))


def attend(head, q_ref, k_refs, v_refs, out):
    scale = math.log2(math.e) / math.sqrt(head)
    for h in range(q_ref.shape[1] // head):
        cols = slice(h * head, (h + 1) * head)
        q = q_ref[:, cols]
        scores = [
            lax.dot_general(q, k[:, cols], (((1,), (1,)), ((), ())), preferred_element_type=f32)
            for k in k_refs
        ]
        top = functools.reduce(
            jnp.maximum, [jnp.max(s, axis=-1, keepdims=True) for s in scores]
        )
        weights = [jnp.exp2((s - top) * scale) for s in scores]
        total = sum(jnp.sum(w, axis=-1, keepdims=True) for w in weights)
        inverse = 1.0 / total
        mixed = sum(
            jnp.dot((w * inverse).astype(bf16), v[:, cols], preferred_element_type=f32)
            for w, v in zip(weights, v_refs)
        )
        out[:, cols] = mixed.astype(bf16)


def out_kernel(head, pairs, n_q, shown, jobs, *refs):
    queries, k_refs = refs[:n_q], refs[n_q : n_q + pairs]
    v_refs = refs[n_q + pairs : n_q + 2 * pairs]
    at = n_q + 2 * pairs
    outs = refs[at + sum(job[0] for job in jobs) :]
    if shown:
        mixed, outs = outs[:n_q], outs[n_q:]
    else:
        mixed = outs[len(outs) - n_q :]
    for q, out in zip(queries, mixed):
        attend(head, q, k_refs, v_refs, out)
    for turn, (given, which, parts, first, count) in enumerate(jobs):
        refs_in = list(refs[at : at + given])
        at += given
        xs = ([] if which is None else [mixed[which]]) + refs_in[: given - parts]
        ws = refs_in[given - parts :]
        keep, send = outs[2 * turn : 2 * turn + 2]
        half = keep.shape[0]
        cols = slice(first, first + count)
        terms = [
            jnp.dot(x[...], w[:, cols], preferred_element_type=f32) for x, w in zip(xs, ws)
        ]
        y = functools.reduce(jnp.add, terms)
        keep[...] = y[:half]
        send[...] = y[half:].astype(bf16)


def out_call(head, queries, ks, vs, shown, jobs):
    vm = pl.BlockSpec(memory_space=VM)
    given, plan, shapes, flops, moved = [*queries, *ks, *vs], [], [], 0, 0
    mixed = [jax.ShapeDtypeStruct(q.shape, bf16) for q in queries]
    if shown:
        shapes += mixed
    for which, xs, ws, first, count in jobs:
        plan.append((len(xs) + len(ws), which, len(ws), first, count))
        given += [*xs, *ws]
        half = queries[0].shape[0] // 2
        shapes.append(jax.ShapeDtypeStruct((half, count), f32))
        shapes.append(jax.ShapeDtypeStruct((half, count), bf16))
        depth = sum(w.shape[0] for w in ws)
        flops += 4 * half * count * depth
        moved += 2 * count * depth + 6 * half * count + 4 * half * depth
    outs = pl.pallas_call(
        functools.partial(out_kernel, head, len(ks), len(queries), shown, plan),
        in_specs=[vm] * len(given),
        out_specs=[vm] * len(shapes),
        out_shape=shapes,
        scratch_shapes=[] if shown else [VM(m.shape, bf16) for m in mixed],
        compiler_params=params(9),
        cost_estimate=cost(flops, moved),
        name="attend_out",
    )(*given)
    skip = len(queries) if shown else 0
    return list(outs[:skip]), [tuple(outs[i : i + 2]) for i in range(skip, len(outs), 2)]


def join_kernel(keep, sent, out):
    out[...] = (keep[...] + sent[...].astype(f32)).astype(bf16)


def join_call(keep, sent):
    vm = pl.BlockSpec(memory_space=VM)
    return pl.pallas_call(
        join_kernel,
        in_specs=[vm, vm],
        out_specs=vm,
        out_shape=jax.ShapeDtypeStruct(keep.shape, bf16),
        compiler_params=params(6),
        cost_estimate=cost(keep.size, 8 * keep.size),
        name="join",
    )(keep, sent)


def drift_kernel(first, parity, keep, sent, sg, *refs):
    fetched, (kept, other, send) = refs[:-3], refs[-3:]
    half, count = kept.shape
    p = parity[0]

    def part(which):
        rows = pl.ds(pl.multiple_of(which * half, half), half)
        branch = keep[rows, :] + sent[rows, :].astype(f32)
        for one in fetched:
            branch = branch + one[rows, :].astype(f32)
        return sg[:, first : first + count] * branch

    kept[...] = part(p)
    passed = part(1 - p)
    other[...] = passed
    send[...] = passed.astype(bf16)


def drift_call(parity, keep, sent, sg, fetched, first):
    rows, count = fetched[0].shape
    vm = pl.BlockSpec(memory_space=VM)
    smem = pl.BlockSpec(memory_space=pltpu.SMEM)
    shape = (rows // 2, count)
    return pl.pallas_call(
        functools.partial(drift_kernel, first),
        in_specs=[smem] + [vm] * (3 + len(fetched)),
        out_specs=[vm] * 3,
        out_shape=[
            jax.ShapeDtypeStruct(shape, f32),
            jax.ShapeDtypeStruct(shape, f32),
            jax.ShapeDtypeStruct(shape, bf16),
        ],
        compiler_params=params(6),
        cost_estimate=cost(4 * rows * count, 13 * rows * count),
        name="drift",
    )(parity, keep, sent, sg, *fetched)


def finish_kernel(first, parity, x_start, earlier, kept, fetched, other, back, *refs):
    out, result, sem = refs[-3:]
    half, count = kept.shape
    cols = slice(first, first + count)
    p = parity[0]
    mine = pl.ds(pl.multiple_of(p * half, half), half)
    rest = pl.ds(pl.multiple_of((1 - p) * half, half), half)
    odd = p.astype(f32)
    result[mine, :] = x_start[mine, cols] + earlier[...] + kept[...] + odd * fetched[...].astype(f32)
    result[rest, :] = x_start[rest, cols] + other[...] + back[...].astype(f32)
    copy = pltpu.make_async_copy(result, out.at[0, :, pl.ds(first, count)], sem)
    copy.start()
    copy.wait()


def finish_call(parity, x_start, earlier, kept, fetched, other, back, into, first):
    rows, width = x_start.shape
    vm = pl.BlockSpec(memory_space=VM)
    smem = pl.BlockSpec(memory_space=pltpu.SMEM)
    hbm = pl.BlockSpec(memory_space=pltpu.HBM)
    given = [parity, x_start, earlier, kept, fetched, other, back]
    return pl.pallas_call(
        functools.partial(finish_kernel, first),
        in_specs=[smem] + [vm] * 6 + [hbm] * len(into),
        out_specs=hbm,
        out_shape=jax.ShapeDtypeStruct((1, rows, width), f32),
        scratch_shapes=[VM((rows, kept.shape[1]), f32), pltpu.SemaphoreType.DMA],
        input_output_aliases={len(given): 0} if into else {},
        compiler_params=params(6),
        cost_estimate=cost(5 * kept.size, 24 * kept.size),
        name="finish",
    )(*given, *into)


def per_device(
    n_step,
    n_seq,
    trajectory,
    x_start,
    t_idx,
    mod_table,
    step_sizes,
    q_gain,
    k_gain,
    w_qkv,
    w_mlp_in,
    w_out_attn,
    w_out_mlp,
):
    head = q_gain.shape[0]
    rows, width = x_start.shape
    chips = n_seq // 2
    groups = n_step // 2
    half = rows // 2
    unit = width // 24
    counts = [10 * unit, 8 * unit, 6 * unit]
    chunks = len(counts)
    firsts = [sum(counts[:c]) for c in range(chunks)]
    qg, kg = q_gain[None, :], k_gain[None, :]

    def to_core(x):
        return lax.ppermute(x, "seq", [(i, i ^ 1) for i in range(n_seq)])

    def to_chip(x, offset):
        return lax.ppermute(x, "seq", [(i, (i + 2 * offset) % n_seq) for i in range(n_seq)])

    def to_pair(x):
        return lax.ppermute(x, "step", [(i, i ^ 1) for i in range(n_step)])

    def tied(*values):
        return lax.optimization_barrier(values)

    parity = lax.rem(lax.axis_index("step"), 2)
    even = (parity == 0).astype(f32)
    which = parity[None]
    offsets = range(1, chips)

    mine, sg = norm_call(t_idx, trajectory, mod_table, step_sizes)
    far = [to_chip(mine, j) for j in offsets]
    q0, k0, v0, act0, *held = project_call(
        mine, to_core(mine), qg, kg, w_qkv, w_mlp_in, None
    )
    far, q0 = tied(far, q0)
    qs, ks, vs, acts = [], [k0], [v0], []
    for block in far:
        q, k, v, act = project_call(block, to_core(block), qg, kg, w_qkv, w_mlp_in, held)
        qs.append(q)
        ks.append(k)
        vs.append(v)
        acts.append(act)
    weights = [w_out_attn, w_out_mlp]
    got = [[] for _ in offsets]

    def joined(parts, sent):
        return [join_call(keep, s) for (keep, _), s in zip(parts, sent)]

    def to_chips(ready):
        for j, one in enumerate(ready):
            got[j].append(to_chip(one, chips - 1 - j))

    others = chips - 1
    jobs = [(j, [acts[j]], weights, firsts[0], counts[0]) for j in range(others)]
    mixed, parts = out_call(head, qs, ks, vs, True, jobs)
    sent = [to_core(send) for _, send in parts]
    ready = joined(parts, sent)
    q0, ready = tied(q0, ready)
    to_chips(ready)
    jobs = []
    for c in range(1, chunks):
        for j in range(others):
            jobs.append((None, [mixed[j], acts[j]], weights, firsts[c], counts[c]))
    for c in range(chunks):
        jobs.append((0, [act0], weights, firsts[c], counts[c]))
    _, parts = out_call(head, [q0], ks, vs, False, jobs)
    sent = [to_core(send) for _, send in parts]
    keep = [part[0] for part in parts[-chunks:]]
    sent0 = sent[-chunks:]
    later = []
    for c in range(1, chunks):
        here = slice((c - 1) * others, c * others)
        later.append(joined(parts[here], sent[here]))
    first, later = tied([row[0] for row in got], later)
    for row, one in zip(got, first):
        row[0] = one
    for ready in later:
        to_chips(ready)

    def along(pairs):
        return lambda x: lax.ppermute(x, "step", [(2 * a + i, 2 * b + i) for a, b in pairs for i in (0, 1)])

    group = lax.div(lax.axis_index("step"), 2)
    spans = []
    while 2 ** len(spans) < groups:
        spans.append(2 ** len(spans))

    def swap(span):
        return along([(b, b ^ span) for b in range(groups) if b ^ span < groups])

    def prefix_stages(c, halves):
        held = {}
        quarter = half // 2
        bit = lax.rem(group, 2)

        def drift_of(fetched):
            drift = drift_call(which, keep[c], sent0[c], sg, fetched, firsts[c])
            held["kept"], held["other"], send = drift
            return send

        def pair_sum(fetched):
            held["fetched"] = fetched[0]
            held["total"] = held["kept"] + fetched[0].astype(f32)
            return held["total"].astype(bf16)

        def collect(r, fetched):
            one = fetched[0]
            if halves and spans[r] == 2:
                both = [held["piece"], one]
                one = jnp.where(
                    bit == 0, jnp.concatenate(both, axis=0), jnp.concatenate(both[::-1], axis=0)
                )
            one = one.astype(f32)
            upper = (lax.rem(lax.div(group, spans[r]), 2) == 1).astype(f32)
            held["earlier"] = held["earlier"] + upper * one if r else upper * one
            if r == len(spans) - 1:
                return (held["earlier"] + even * held["kept"]).astype(bf16)
            held["total"] = held["total"] + one
            total = held["total"].astype(bf16)
            if halves and spans[r + 1] == 2:
                return lax.dynamic_slice_in_dim(total, bit * quarter, quarter, 0)
            return total

        def pass_on(fetched):
            held["piece"] = fetched[0]
            return fetched[0]

        def finish(fetched):
            given = [held[name] for name in ("earlier", "kept", "fetched", "other")]
            into = list(written)
            written[:] = [finish_call(which, x_start, *given, fetched[0], into, firsts[c])]

        stages = [(drift_of, to_pair, "x", 0.5), (pair_sum, swap(1), "z1", 0.5)]
        for r in range(len(spans)):
            take = functools.partial(collect, r)
            if r == len(spans) - 1:
                stages.append((take, to_pair, "x", 0.5))
            elif halves and spans[r + 1] == 2:
                stages.append((take, swap(2), "z2", 0.5))
                stages.append((pass_on, swap(1), "z1", 0.25))
            else:
                stages.append((take, swap(spans[r + 1]), "z2", 1.0))
        stages.append((finish, None, "", 0.0))
        return stages

    plan = [prefix_stages(c, c == 0) for c in range(chunks)]
    inbox = [[got[j][c] for j in range(chips - 1)] for c in range(chunks)]
    shares = [18.5 * n / width for n in counts]
    ends = [2.0 * c + sum(shares[: c + 1]) for c in range(chunks)]
    waits = [(end, c, 0) for c, end in enumerate(ends)]
    free = {"x": 0.0, "z1": 0.0, "z2": 0.0, "": 0.0}
    turns = []
    while waits:
        when, c, i = min(waits)
        waits.remove((when, c, i))
        turns.append((c, i))
        if i + 1 < len(plan[c]):
            link, load = plan[c][i][2:]
            begin = max(when + 1.5, free[link])
            free[link] = begin + load * shares[c]
            waits.append((free[link] + 0.7, c, i + 1))
    written = []
    last = None
    for c, i in turns:
        compute, move = plan[c][i][:2]
        fetched = inbox[c]
        if last is not None:
            fetched, last = tied(fetched, last)
        out = compute(fetched)
        if move is not None:
            inbox[c] = [move(out)]
            last = out
    return written[0]


def solution(mesh):
    placed = (
        P("step", "seq", None),
        P("seq", None),
        P("step"),
        P(),
        P(),
        P(),
        P(),
        P(None, None, "seq"),
        P(None, "seq"),
        P("seq", None),
        P("seq", None),
    )
    return jax.shard_map(
        functools.partial(per_device, mesh.shape["step"], mesh.shape["seq"]),
        mesh=mesh,
        in_specs=placed,
        out_specs=P("step", "seq", None),
        check_vma=False,
    )
```

```python
import functools
import math

import jax
import jax.numpy as jnp
from jax import lax
from jax.experimental import pallas as pl
from jax.experimental.pallas import tpu as pltpu
from jax.sharding import PartitionSpec as P

eps = 1e-06
f32 = jnp.float32
bf16 = jnp.bfloat16
VM = pltpu.VMEM
MIB = 1024 * 1024


def params(mib):
    return pltpu.CompilerParams(vmem_limit_bytes=mib * MIB)


def cost(flops, moved):
    return pl.CostEstimate(flops=flops, transcendentals=0, bytes_accessed=moved)


def norm_kernel(t_ref, size_ref, x_hbm, mod_hbm, m_ref, sg_ref, x_ref, mod_ref, sem):
    width = x_hbm.shape[-1]
    pieces = sem.shape[0] - 1
    block = x_hbm.shape[1] // pieces
    t = t_ref[0]
    mod_copy = pltpu.make_async_copy(mod_hbm.at[pl.ds(t, 1), :], mod_ref, sem.at[pieces])
    mod_copy.start()
    copies = []
    for i in range(pieces):
        here = pl.ds(i * block, block)
        copies.append(pltpu.make_async_copy(x_hbm.at[0, here, :], x_ref.at[here, :], sem.at[i]))
        copies[i].start()
    mod_copy.wait()
    shift = mod_ref[:, :width]
    scale = 1.0 + mod_ref[:, width : 2 * width]
    sg_ref[...] = size_ref[t] * mod_ref[:, 2 * width :]
    for i in range(pieces):
        copies[i].wait()
        here = slice(i * block, (i + 1) * block)
        x = x_ref[here, :]
        center = x - jnp.mean(x, axis=-1, keepdims=True)
        spread = jnp.mean(center * center, axis=-1, keepdims=True)
        m_ref[here, :] = (center * lax.rsqrt(spread + eps) * scale + shift).astype(bf16)


def norm_call(t_idx, trajectory, mod_table, step_sizes):
    _, rows, width = trajectory.shape
    smem = pl.BlockSpec(memory_space=pltpu.SMEM)
    hbm = pl.BlockSpec(memory_space=pltpu.HBM)
    vm = pl.BlockSpec(memory_space=VM)
    return pl.pallas_call(
        norm_kernel,
        in_specs=[smem, smem, hbm, hbm],
        out_specs=[vm, vm],
        out_shape=[
            jax.ShapeDtypeStruct((rows, width), bf16),
            jax.ShapeDtypeStruct((1, width), f32),
        ],
        scratch_shapes=[
            VM((rows, width), f32),
            VM((1, 3 * width), f32),
            pltpu.SemaphoreType.DMA((5,)),
        ],
        compiler_params=params(60),
        cost_estimate=cost(10 * rows * width, 0),
        name="norm",
    )(t_idx, step_sizes, trajectory, mod_table)


def project_kernel(tile, load, tiles, m0, m1, qg, kg, *refs):
    if load:
        wq_hbm, wm_hbm, wb_hbm, q, k, v, act, low, high = refs[:9]
        held, rows, wb, sem = refs[9:-3], refs[-3], refs[-2], refs[-1]
    else:
        held = refs[:tiles]
        q, k, v, act, rows = refs[tiles:]
    half = m0.shape[0]
    head = qg.shape[1]
    n_q = q.shape[1] // tile
    copies = []
    if load:
        for i in range(tiles):
            if i < 3 * n_q:
                source = wq_hbm.at[i // n_q, :, pl.ds(i % n_q * tile, tile)]
            else:
                source = wm_hbm.at[:, pl.ds((i - 3 * n_q) * tile, tile)]
            copies.append(pltpu.make_async_copy(source, held[i], sem.at[i]))
            copies[i].start()
        span = low.shape[1] // (sem.shape[0] - tiles)
        for at in range(0, low.shape[1], span):
            here = (slice(None), pl.ds(at, span))
            copies.append(pltpu.make_async_copy(wb_hbm.at[here], wb.at[here], sem.at[len(copies)]))
            copies[-1].start()
    rows[:half] = m0[...]
    rows[half:] = m1[...]

    def normed(y, gain):
        parts = []
        for h in range(tile // head):
            one = y[:, h * head : (h + 1) * head]
            square = jnp.mean(one * one, axis=-1, keepdims=True)
            parts.append((one * lax.rsqrt(square + eps) * gain).astype(bf16))
        return jnp.concatenate(parts, axis=1)

    for i in range(tiles):
        if load:
            copies[i].wait()
        y = jnp.dot(rows[...], held[i][...], preferred_element_type=f32)
        cols = slice(i % n_q * tile, (i % n_q + 1) * tile)
        if i < n_q:
            q[:, cols] = normed(y, qg[...])
        elif i < 2 * n_q:
            k[:, cols] = normed(y, kg[...])
        elif i < 3 * n_q:
            v[:, cols] = y.astype(bf16)
        else:
            cols = slice((i - 3 * n_q) * tile, (i - 3 * n_q + 1) * tile)
            act[:, cols] = jax.nn.gelu(y, approximate=True).astype(bf16)
    if load:
        for i, copy in enumerate(copies[tiles:]):
            copy.wait()
            cols = slice(i * span, (i + 1) * span)
            y = jnp.dot(act[...], wb[:, cols], preferred_element_type=f32)
            low[:, cols] = y[:half]
            high[:, cols] = y[half:]


def project_call(m0, m1, q_gain, k_gain, w_qkv, w_mlp_in, w_out_mlp, held):
    half, width = m0.shape
    heads = w_qkv.shape[2]
    hidden = w_mlp_in.shape[1]
    tile = min(512, heads)
    tiles = (3 * heads + hidden) // tile
    rows = 2 * half
    load = held is None
    vm = pl.BlockSpec(memory_space=VM)
    hbm = pl.BlockSpec(memory_space=pltpu.HBM)
    shapes = [jax.ShapeDtypeStruct((rows, heads), bf16)] * 3
    shapes.append(jax.ShapeDtypeStruct((rows, hidden), bf16))
    scratch = [VM((rows, width), bf16)]
    if load:
        shapes += [jax.ShapeDtypeStruct((half, width), f32)] * 2
        shapes += [jax.ShapeDtypeStruct((width, tile), bf16)] * tiles
        scratch.append(VM(w_out_mlp.shape, bf16))
        scratch.append(pltpu.SemaphoreType.DMA((tiles + 4,)))
    return pl.pallas_call(
        functools.partial(project_kernel, tile, load, tiles),
        in_specs=[vm] * 4 + ([hbm] * 3 if load else [vm] * tiles),
        out_specs=[vm] * len(shapes),
        out_shape=shapes,
        scratch_shapes=scratch,
        compiler_params=params(27 if load else 9),
        cost_estimate=cost(2 * rows * width * (3 * heads + hidden), 0),
        name="project",
    )(m0, m1, q_gain, k_gain, *([w_qkv, w_mlp_in, w_out_mlp] if load else held))


def attend_kernel(pairs, head, *refs):
    q_ref = refs[0]
    k_refs = refs[1 : 1 + pairs]
    v_refs = refs[1 + pairs : 1 + 2 * pairs]
    out = refs[1 + 2 * pairs]
    scale = math.log2(math.e) / math.sqrt(head)
    for h in range(q_ref.shape[1] // head):
        cols = slice(h * head, (h + 1) * head)
        q = q_ref[:, cols]
        scores = [
            lax.dot_general(q, k[:, cols], (((1,), (1,)), ((), ())), preferred_element_type=f32)
            for k in k_refs
        ]
        top = functools.reduce(
            jnp.maximum, [jnp.max(s, axis=-1, keepdims=True) for s in scores]
        )
        weights = [jnp.exp2((s - top) * scale) for s in scores]
        total = sum(jnp.sum(w, axis=-1, keepdims=True) for w in weights)
        inverse = 1.0 / total
        mixed = sum(
            jnp.dot((w * inverse).astype(bf16), v[:, cols], preferred_element_type=f32)
            for w, v in zip(weights, v_refs)
        )
        out[:, cols] = mixed.astype(bf16)


def attend_call(q, ks, vs, head):
    vm = pl.BlockSpec(memory_space=VM)
    return pl.pallas_call(
        functools.partial(attend_kernel, len(ks), head),
        in_specs=[vm] * (1 + 2 * len(ks)),
        out_specs=vm,
        out_shape=jax.ShapeDtypeStruct(q.shape, bf16),
        compiler_params=params(9),
        cost_estimate=cost(4 * len(ks) * q.shape[0] ** 2 * q.shape[1] * 3, 0),
        name="attend",
    )(q, *ks, *vs)


def out_kernel(jobs, *refs):
    outs = refs[len(refs) - 2 * len(jobs) :]
    at = 0
    for turn, (parts, extras, first, count) in enumerate(jobs):
        xs = refs[at : at + parts]
        ws = refs[at + parts : at + 2 * parts]
        extra = refs[at + 2 * parts : at + 2 * parts + extras]
        at += 2 * parts + extras
        keep, send = outs[2 * turn : 2 * turn + 2]
        half = keep.shape[0]
        cols = slice(first, first + count)
        terms = [
            jnp.dot(x[...], w[:, cols], preferred_element_type=f32) for x, w in zip(xs, ws)
        ]
        y = functools.reduce(jnp.add, terms)
        low, high = y[:half], y[half:]
        if extra:
            low = low + extra[0][:, cols]
            high = high + extra[1][:, cols]
        keep[...] = low
        send[...] = high.astype(bf16)


def out_call(jobs):
    vm = pl.BlockSpec(memory_space=VM)
    given, plan, shapes, flops = [], [], [], 0
    for xs, ws, extra, first, count in jobs:
        given += [*xs, *ws, *extra]
        plan.append((len(xs), len(extra), first, count))
        half = xs[0].shape[0] // 2
        shapes.append(jax.ShapeDtypeStruct((half, count), f32))
        shapes.append(jax.ShapeDtypeStruct((half, count), bf16))
        flops += 4 * half * count * sum(x.shape[1] for x in xs)
    outs = pl.pallas_call(
        functools.partial(out_kernel, plan),
        in_specs=[vm] * len(given),
        out_specs=[vm] * len(shapes),
        out_shape=shapes,
        compiler_params=params(9),
        cost_estimate=cost(flops, 0),
        name="project_out",
    )(*given)
    return [tuple(outs[i : i + 2]) for i in range(0, len(outs), 2)]


def join_kernel(keep, sent, out):
    out[...] = (keep[...] + sent[...].astype(f32)).astype(bf16)


def join_call(keep, sent):
    vm = pl.BlockSpec(memory_space=VM)
    return pl.pallas_call(
        join_kernel,
        in_specs=[vm, vm],
        out_specs=vm,
        out_shape=jax.ShapeDtypeStruct(keep.shape, bf16),
        compiler_params=params(6),
        name="join",
    )(keep, sent)


def drift_kernel(first, parity, keep, sent, sg, *refs):
    fetched, (kept, other, send) = refs[:-3], refs[-3:]
    half, count = kept.shape
    p = parity[0]

    def part(which):
        rows = pl.ds(pl.multiple_of(which * half, half), half)
        branch = keep[rows, :] + sent[rows, :].astype(f32)
        for one in fetched:
            branch = branch + one[rows, :].astype(f32)
        return sg[:, first : first + count] * branch

    kept[...] = part(p)
    passed = part(1 - p)
    other[...] = passed
    send[...] = passed.astype(bf16)


def drift_call(parity, keep, sent, sg, fetched, first):
    rows, count = fetched[0].shape
    vm = pl.BlockSpec(memory_space=VM)
    smem = pl.BlockSpec(memory_space=pltpu.SMEM)
    shape = (rows // 2, count)
    return pl.pallas_call(
        functools.partial(drift_kernel, first),
        in_specs=[smem] + [vm] * (3 + len(fetched)),
        out_specs=[vm] * 3,
        out_shape=[
            jax.ShapeDtypeStruct(shape, f32),
            jax.ShapeDtypeStruct(shape, f32),
            jax.ShapeDtypeStruct(shape, bf16),
        ],
        compiler_params=params(6),
        name="drift",
    )(parity, keep, sent, sg, *fetched)


def finish_kernel(firsts, parity, x_start, *refs):
    n = len(firsts)
    given, rest = refs[: 5 * n], refs[-2 - n :]
    out, results, sem = rest[0], rest[1 : 1 + n], rest[1 + n]
    p = parity[0]
    odd = p.astype(f32)
    copies = []
    for i, first in enumerate(firsts):
        earlier, kept, fetched, other, back = given[5 * i : 5 * i + 5]
        half, count = kept.shape
        cols = slice(first, first + count)
        mine = pl.ds(pl.multiple_of(p * half, half), half)
        rest = pl.ds(pl.multiple_of((1 - p) * half, half), half)
        results[i][mine, :] = (
            x_start[mine, cols] + earlier[...] + kept[...] + odd * fetched[...].astype(f32)
        )
        results[i][rest, :] = x_start[rest, cols] + other[...] + back[...].astype(f32)
        copies.append(
            pltpu.make_async_copy(results[i], out.at[0, :, pl.ds(first, count)], sem.at[i])
        )
        copies[i].start()
    for copy in copies:
        copy.wait()


def finish_call(parity, x_start, groups, firsts, into):
    rows, width = x_start.shape
    vm = pl.BlockSpec(memory_space=VM)
    smem = pl.BlockSpec(memory_space=pltpu.SMEM)
    hbm = pl.BlockSpec(memory_space=pltpu.HBM)
    given = [parity, x_start] + [one for group in groups for one in group]
    return pl.pallas_call(
        functools.partial(finish_kernel, firsts),
        in_specs=[smem] + [vm] * (len(given) - 1) + [hbm] * len(into),
        out_specs=hbm,
        out_shape=jax.ShapeDtypeStruct((1, rows, width), f32),
        scratch_shapes=[VM((rows, group[1].shape[1]), f32) for group in groups]
        + [pltpu.SemaphoreType.DMA((len(groups),))],
        input_output_aliases={len(given): 0} if into else {},
        compiler_params=params(6),
        name="finish",
    )(*given, *into)


def per_device(
    n_step,
    n_seq,
    trajectory,
    x_start,
    t_idx,
    mod_table,
    step_sizes,
    q_gain,
    k_gain,
    w_qkv,
    w_mlp_in,
    w_out_attn,
    w_out_mlp,
):
    head = q_gain.shape[0]
    rows, width = x_start.shape
    chips = n_seq // 2
    groups = n_step // 2
    half = rows // 2
    unit = width // 24
    counts = [10 * unit, 8 * unit, 6 * unit]
    chunks = len(counts)
    firsts = [sum(counts[:c]) for c in range(chunks)]
    qg, kg = q_gain[None, :], k_gain[None, :]

    def to_core(x):
        return lax.ppermute(x, "seq", [(i, i ^ 1) for i in range(n_seq)])

    def to_chip(x, offset):
        return lax.ppermute(x, "seq", [(i, (i + 2 * offset) % n_seq) for i in range(n_seq)])

    def to_pair(x):
        return lax.ppermute(x, "step", [(i, i ^ 1) for i in range(n_step)])

    def tied(*values):
        return lax.optimization_barrier(values)

    parity = lax.rem(lax.axis_index("step"), 2)
    even = (parity == 0).astype(f32)
    which = parity[None]
    offsets = range(1, chips)

    mine, sg = norm_call(t_idx, trajectory, mod_table, step_sizes)
    far = [to_chip(mine, j) for j in offsets]
    q0, k0, v0, act0, low0, high0, *held = project_call(
        mine, to_core(mine), qg, kg, w_qkv, w_mlp_in, w_out_mlp, None
    )
    far, low0, high0 = tied(far, low0, high0)
    qs, ks, vs, acts = [], [k0], [v0], []
    for block in far:
        q, k, v, act = project_call(block, to_core(block), qg, kg, w_qkv, w_mlp_in, w_out_mlp, held)
        qs.append(q)
        ks.append(k)
        vs.append(v)
        acts.append(act)
    mixed = [attend_call(q, ks, vs, head) for q in qs]

    weights = [w_out_attn, w_out_mlp]
    got = [[] for _ in offsets]

    def jobs_of(c):
        return [([a, b], weights, [], firsts[c], counts[c]) for a, b in zip(mixed, acts)]

    def joined(parts, sent):
        return [join_call(keep, s) for (keep, _), s in zip(parts, sent)]

    def to_chips(ready):
        for j, one in enumerate(ready):
            got[j].append(to_chip(one, chips - 1 - j))

    parts = out_call(jobs_of(0))
    sent = [to_core(send) for _, send in parts]
    q0, parts = tied(q0, parts)
    mixed0 = attend_call(q0, ks, vs, head)
    mixed0, sent = tied(mixed0, sent)
    ready = joined(parts, sent)
    mixed, acts, mixed0, ready = tied(mixed, acts, mixed0, ready)
    to_chips(ready)
    jobs = [job for c in range(1, chunks) for job in jobs_of(c)]
    for c in range(chunks):
        jobs.append(([mixed0], [w_out_attn], [low0, high0], firsts[c], counts[c]))
    parts = out_call(jobs)
    sent = [to_core(send) for _, send in parts]
    keep = [part[0] for part in parts[-chunks:]]
    sent0 = sent[-chunks:]
    others = chips - 1
    first, keep, sent[:others] = tied([row[0] for row in got], keep, sent[:others])
    for row, one in zip(got, first):
        row[0] = one
    ready = joined(parts[:others], sent[:others])
    keep, ready = tied(keep, ready)
    to_chips(ready)
    for c in range(2, chunks):
        here = slice((c - 1) * others, c * others)
        to_chips(joined(parts[here], sent[here]))

    def along(pairs):
        return lambda x: lax.ppermute(x, "step", [(2 * a + i, 2 * b + i) for a, b in pairs for i in (0, 1)])

    group = lax.div(lax.axis_index("step"), 2)
    spans = []
    while 2 ** len(spans) < groups:
        spans.append(2 ** len(spans))

    def swap(span):
        return along([(b, b ^ span) for b in range(groups) if b ^ span < groups])

    def prefix_stages(c, halves):
        held = {}
        quarter = half // 2
        bit = lax.rem(group, 2)

        def drift_of(fetched):
            drift = drift_call(which, keep[c], sent0[c], sg, fetched, firsts[c])
            held["kept"], held["other"], send = drift
            return send

        def pair_sum(fetched):
            held["fetched"] = fetched[0]
            held["total"] = held["kept"] + fetched[0].astype(f32)
            return held["total"].astype(bf16)

        def collect(r, fetched):
            one = fetched[0]
            if halves and spans[r] == 2:
                both = [held["piece"], one]
                one = jnp.where(
                    bit == 0, jnp.concatenate(both, axis=0), jnp.concatenate(both[::-1], axis=0)
                )
            one = one.astype(f32)
            upper = (lax.rem(lax.div(group, spans[r]), 2) == 1).astype(f32)
            held["earlier"] = held["earlier"] + upper * one if r else upper * one
            if r == len(spans) - 1:
                return (held["earlier"] + even * held["kept"]).astype(bf16)
            held["total"] = held["total"] + one
            total = held["total"].astype(bf16)
            if halves and spans[r + 1] == 2:
                return lax.dynamic_slice_in_dim(total, bit * quarter, quarter, 0)
            return total

        def pass_on(fetched):
            held["piece"] = fetched[0]
            return fetched[0]

        def finish(fetched):
            given = [held[name] for name in ("earlier", "kept", "fetched", "other")]
            stash.append((firsts[c], given + [fetched[0]]))
            if len(stash) in (1, chunks):
                mine = stash[len(stash) - 1 :] if len(stash) == 1 else stash[1:]
                places = [place for place, _ in mine]
                groups_in = [group for _, group in mine]
                into = list(written)
                written[:] = [finish_call(which, x_start, groups_in, places, into)]

        stages = [(drift_of, to_pair, "x", 0.5), (pair_sum, swap(1), "z1", 0.5)]
        for r in range(len(spans)):
            take = functools.partial(collect, r)
            if r == len(spans) - 1:
                stages.append((take, to_pair, "x", 0.5))
            elif halves and spans[r + 1] == 2:
                stages.append((take, swap(2), "z2", 0.5))
                stages.append((pass_on, swap(1), "z1", 0.25))
            else:
                stages.append((take, swap(spans[r + 1]), "z2", 1.0))
        stages.append((finish, None, "", 0.0))
        return stages

    plan = [prefix_stages(c, False) for c in range(chunks)]
    inbox = [[got[j][c] for j in range(chips - 1)] for c in range(chunks)]
    shares = [18.5 * n / width for n in counts]
    ends = [2.0 * (c + 1) + sum(shares[: c + 1]) for c in range(chunks)]
    waits = [(end, c, 0) for c, end in enumerate(ends)]
    free = {"x": 0.0, "z1": 0.0, "z2": 0.0, "": 0.0}
    turns = []
    while waits:
        when, c, i = min(waits)
        waits.remove((when, c, i))
        turns.append((c, i))
        if i + 1 < len(plan[c]):
            link, load = plan[c][i][2:]
            begin = max(when + 1.5, free[link])
            free[link] = begin + load * shares[c]
            waits.append((free[link] + 0.7, c, i + 1))
    written, stash = [], []
    last = None
    for c, i in turns:
        compute, move = plan[c][i][:2]
        fetched = inbox[c]
        if last is not None:
            fetched, last = tied(fetched, last)
        out = compute(fetched)
        if move is not None:
            inbox[c] = [move(out)]
            last = out
    return written[0]


def solution(mesh):
    placed = (
        P("step", "seq", None),
        P("seq", None),
        P("step"),
        P(),
        P(),
        P(),
        P(),
        P(None, None, "seq"),
        P(None, "seq"),
        P("seq", None),
        P("seq", None),
    )
    return jax.shard_map(
        functools.partial(per_device, mesh.shape["step"], mesh.shape["seq"]),
        mesh=mesh,
        in_specs=placed,
        out_specs=P("step", "seq", None),
        check_vma=False,
    )
```

```python
import functools
import math

import jax
import jax.numpy as jnp
from jax import lax
from jax.experimental import pallas as pl
from jax.experimental.pallas import tpu as pltpu
from jax.sharding import PartitionSpec as P

eps = 1e-06
f32 = jnp.float32
bf16 = jnp.bfloat16
VM = pltpu.VMEM
MIB = 1024 * 1024


def params(mib):
    return pltpu.CompilerParams(vmem_limit_bytes=mib * MIB)


def cost(flops, moved):
    return pl.CostEstimate(flops=flops, transcendentals=0, bytes_accessed=moved)


def norm_kernel(t_ref, size_ref, x_hbm, mod_hbm, m_ref, sg_ref, x_ref, mod_ref, sem):
    width = x_hbm.shape[-1]
    pieces = sem.shape[0] - 1
    block = x_hbm.shape[1] // pieces
    t = t_ref[0]
    mod_copy = pltpu.make_async_copy(mod_hbm.at[pl.ds(t, 1), :], mod_ref, sem.at[pieces])
    mod_copy.start()
    copies = []
    for i in range(pieces):
        here = pl.ds(i * block, block)
        copies.append(pltpu.make_async_copy(x_hbm.at[0, here, :], x_ref.at[here, :], sem.at[i]))
        copies[i].start()
    mod_copy.wait()
    shift = mod_ref[:, :width]
    scale = 1.0 + mod_ref[:, width : 2 * width]
    sg_ref[...] = size_ref[t] * mod_ref[:, 2 * width :]
    for i in range(pieces):
        copies[i].wait()
        here = slice(i * block, (i + 1) * block)
        x = x_ref[here, :]
        center = x - jnp.mean(x, axis=-1, keepdims=True)
        spread = jnp.mean(center * center, axis=-1, keepdims=True)
        m_ref[here, :] = (center * lax.rsqrt(spread + eps) * scale + shift).astype(bf16)


def norm_call(t_idx, trajectory, mod_table, step_sizes):
    _, rows, width = trajectory.shape
    smem = pl.BlockSpec(memory_space=pltpu.SMEM)
    hbm = pl.BlockSpec(memory_space=pltpu.HBM)
    vm = pl.BlockSpec(memory_space=VM)
    return pl.pallas_call(
        norm_kernel,
        in_specs=[smem, smem, hbm, hbm],
        out_specs=[vm, vm],
        out_shape=[
            jax.ShapeDtypeStruct((rows, width), bf16),
            jax.ShapeDtypeStruct((1, width), f32),
        ],
        scratch_shapes=[
            VM((rows, width), f32),
            VM((1, 3 * width), f32),
            pltpu.SemaphoreType.DMA((5,)),
        ],
        compiler_params=params(60),
        cost_estimate=cost(10 * rows * width, 0),
        name="norm",
    )(t_idx, step_sizes, trajectory, mod_table)


def project_kernel(tile, load, tiles, m0, m1, qg, kg, *refs):
    if load:
        wq_hbm, wm_hbm, wb_hbm, q, k, v, act, low, high = refs[:9]
        held, rows, wb, sem = refs[9:-3], refs[-3], refs[-2], refs[-1]
    else:
        held = refs[:tiles]
        q, k, v, act, rows = refs[tiles:]
    half = m0.shape[0]
    head = qg.shape[1]
    n_q = q.shape[1] // tile
    copies = []
    if load:
        for i in range(tiles):
            if i < 3 * n_q:
                source = wq_hbm.at[i // n_q, :, pl.ds(i % n_q * tile, tile)]
            else:
                source = wm_hbm.at[:, pl.ds((i - 3 * n_q) * tile, tile)]
            copies.append(pltpu.make_async_copy(source, held[i], sem.at[i]))
            copies[i].start()
        span = low.shape[1] // (sem.shape[0] - tiles)
        for at in range(0, low.shape[1], span):
            here = (slice(None), pl.ds(at, span))
            copies.append(pltpu.make_async_copy(wb_hbm.at[here], wb.at[here], sem.at[len(copies)]))
            copies[-1].start()
    rows[:half] = m0[...]
    rows[half:] = m1[...]

    def normed(y, gain):
        parts = []
        for h in range(tile // head):
            one = y[:, h * head : (h + 1) * head]
            square = jnp.mean(one * one, axis=-1, keepdims=True)
            parts.append((one * lax.rsqrt(square + eps) * gain).astype(bf16))
        return jnp.concatenate(parts, axis=1)

    for i in range(tiles):
        if load:
            copies[i].wait()
        y = jnp.dot(rows[...], held[i][...], preferred_element_type=f32)
        cols = slice(i % n_q * tile, (i % n_q + 1) * tile)
        if i < n_q:
            q[:, cols] = normed(y, qg[...])
        elif i < 2 * n_q:
            k[:, cols] = normed(y, kg[...])
        elif i < 3 * n_q:
            v[:, cols] = y.astype(bf16)
        else:
            cols = slice((i - 3 * n_q) * tile, (i - 3 * n_q + 1) * tile)
            act[:, cols] = jax.nn.gelu(y, approximate=True).astype(bf16)
    if load:
        for i, copy in enumerate(copies[tiles:]):
            copy.wait()
            cols = slice(i * span, (i + 1) * span)
            y = jnp.dot(act[...], wb[:, cols], preferred_element_type=f32)
            low[:, cols] = y[:half]
            high[:, cols] = y[half:]


def project_call(m0, m1, q_gain, k_gain, w_qkv, w_mlp_in, w_out_mlp, held):
    half, width = m0.shape
    heads = w_qkv.shape[2]
    hidden = w_mlp_in.shape[1]
    tile = min(512, heads)
    tiles = (3 * heads + hidden) // tile
    rows = 2 * half
    load = held is None
    vm = pl.BlockSpec(memory_space=VM)
    hbm = pl.BlockSpec(memory_space=pltpu.HBM)
    shapes = [jax.ShapeDtypeStruct((rows, heads), bf16)] * 3
    shapes.append(jax.ShapeDtypeStruct((rows, hidden), bf16))
    scratch = [VM((rows, width), bf16)]
    if load:
        shapes += [jax.ShapeDtypeStruct((half, width), f32)] * 2
        shapes += [jax.ShapeDtypeStruct((width, tile), bf16)] * tiles
        scratch.append(VM(w_out_mlp.shape, bf16))
        scratch.append(pltpu.SemaphoreType.DMA((tiles + 4,)))
    return pl.pallas_call(
        functools.partial(project_kernel, tile, load, tiles),
        in_specs=[vm] * 4 + ([hbm] * 3 if load else [vm] * tiles),
        out_specs=[vm] * len(shapes),
        out_shape=shapes,
        scratch_shapes=scratch,
        compiler_params=params(27 if load else 9),
        cost_estimate=cost(2 * rows * width * (3 * heads + hidden), 0),
        name="project",
    )(m0, m1, q_gain, k_gain, *([w_qkv, w_mlp_in, w_out_mlp] if load else held))


def attend_kernel(pairs, head, *refs):
    q_ref = refs[0]
    k_refs = refs[1 : 1 + pairs]
    v_refs = refs[1 + pairs : 1 + 2 * pairs]
    out = refs[1 + 2 * pairs]
    scale = math.log2(math.e) / math.sqrt(head)
    for h in range(q_ref.shape[1] // head):
        cols = slice(h * head, (h + 1) * head)
        q = q_ref[:, cols]
        scores = [
            lax.dot_general(q, k[:, cols], (((1,), (1,)), ((), ())), preferred_element_type=f32)
            for k in k_refs
        ]
        top = functools.reduce(
            jnp.maximum, [jnp.max(s, axis=-1, keepdims=True) for s in scores]
        )
        weights = [jnp.exp2((s - top) * scale) for s in scores]
        total = sum(jnp.sum(w, axis=-1, keepdims=True) for w in weights)
        inverse = 1.0 / total
        mixed = sum(
            jnp.dot((w * inverse).astype(bf16), v[:, cols], preferred_element_type=f32)
            for w, v in zip(weights, v_refs)
        )
        out[:, cols] = mixed.astype(bf16)


def attend_call(q, ks, vs, head):
    vm = pl.BlockSpec(memory_space=VM)
    return pl.pallas_call(
        functools.partial(attend_kernel, len(ks), head),
        in_specs=[vm] * (1 + 2 * len(ks)),
        out_specs=vm,
        out_shape=jax.ShapeDtypeStruct(q.shape, bf16),
        compiler_params=params(9),
        cost_estimate=cost(4 * len(ks) * q.shape[0] ** 2 * q.shape[1] * 3, 0),
        name="attend",
    )(q, *ks, *vs)


def out_kernel(jobs, *refs):
    outs = refs[len(refs) - 2 * len(jobs) :]
    at = 0
    for turn, (parts, extras, first, count) in enumerate(jobs):
        xs = refs[at : at + parts]
        ws = refs[at + parts : at + 2 * parts]
        extra = refs[at + 2 * parts : at + 2 * parts + extras]
        at += 2 * parts + extras
        keep, send = outs[2 * turn : 2 * turn + 2]
        half = keep.shape[0]
        cols = slice(first, first + count)
        terms = [
            jnp.dot(x[...], w[:, cols], preferred_element_type=f32) for x, w in zip(xs, ws)
        ]
        y = functools.reduce(jnp.add, terms)
        low, high = y[:half], y[half:]
        if extra:
            low = low + extra[0][:, cols]
            high = high + extra[1][:, cols]
        keep[...] = low
        send[...] = high.astype(bf16)


def out_call(jobs):
    vm = pl.BlockSpec(memory_space=VM)
    given, plan, shapes, flops = [], [], [], 0
    for xs, ws, extra, first, count in jobs:
        given += [*xs, *ws, *extra]
        plan.append((len(xs), len(extra), first, count))
        half = xs[0].shape[0] // 2
        shapes.append(jax.ShapeDtypeStruct((half, count), f32))
        shapes.append(jax.ShapeDtypeStruct((half, count), bf16))
        flops += 4 * half * count * sum(x.shape[1] for x in xs)
    outs = pl.pallas_call(
        functools.partial(out_kernel, plan),
        in_specs=[vm] * len(given),
        out_specs=[vm] * len(shapes),
        out_shape=shapes,
        compiler_params=params(9),
        cost_estimate=cost(flops, 0),
        name="project_out",
    )(*given)
    return [tuple(outs[i : i + 2]) for i in range(0, len(outs), 2)]


def join_kernel(keep, sent, out):
    out[...] = (keep[...] + sent[...].astype(f32)).astype(bf16)


def join_call(keep, sent):
    vm = pl.BlockSpec(memory_space=VM)
    return pl.pallas_call(
        join_kernel,
        in_specs=[vm, vm],
        out_specs=vm,
        out_shape=jax.ShapeDtypeStruct(keep.shape, bf16),
        compiler_params=params(6),
        name="join",
    )(keep, sent)


def drift_kernel(first, parity, keep, sent, sg, *refs):
    fetched, (kept, other, send) = refs[:-3], refs[-3:]
    half, count = kept.shape
    p = parity[0]

    def part(which):
        rows = pl.ds(pl.multiple_of(which * half, half), half)
        branch = keep[rows, :] + sent[rows, :].astype(f32)
        for one in fetched:
            branch = branch + one[rows, :].astype(f32)
        return sg[:, first : first + count] * branch

    kept[...] = part(p)
    passed = part(1 - p)
    other[...] = passed
    send[...] = passed.astype(bf16)


def drift_call(parity, keep, sent, sg, fetched, first):
    rows, count = fetched[0].shape
    vm = pl.BlockSpec(memory_space=VM)
    smem = pl.BlockSpec(memory_space=pltpu.SMEM)
    shape = (rows // 2, count)
    return pl.pallas_call(
        functools.partial(drift_kernel, first),
        in_specs=[smem] + [vm] * (3 + len(fetched)),
        out_specs=[vm] * 3,
        out_shape=[
            jax.ShapeDtypeStruct(shape, f32),
            jax.ShapeDtypeStruct(shape, f32),
            jax.ShapeDtypeStruct(shape, bf16),
        ],
        compiler_params=params(6),
        name="drift",
    )(parity, keep, sent, sg, *fetched)


def finish_kernel(firsts, parity, x_start, *refs):
    n = len(firsts)
    given, rest = refs[: 5 * n], refs[-2 - n :]
    out, results, sem = rest[0], rest[1 : 1 + n], rest[1 + n]
    p = parity[0]
    odd = p.astype(f32)
    copies = []
    for i, first in enumerate(firsts):
        earlier, kept, fetched, other, back = given[5 * i : 5 * i + 5]
        half, count = kept.shape
        cols = slice(first, first + count)
        mine = pl.ds(pl.multiple_of(p * half, half), half)
        rest = pl.ds(pl.multiple_of((1 - p) * half, half), half)
        results[i][mine, :] = (
            x_start[mine, cols] + earlier[...] + kept[...] + odd * fetched[...].astype(f32)
        )
        results[i][rest, :] = x_start[rest, cols] + other[...] + back[...].astype(f32)
        copies.append(
            pltpu.make_async_copy(results[i], out.at[0, :, pl.ds(first, count)], sem.at[i])
        )
        copies[i].start()
    for copy in copies:
        copy.wait()


def finish_call(parity, x_start, groups, firsts, into):
    rows, width = x_start.shape
    vm = pl.BlockSpec(memory_space=VM)
    smem = pl.BlockSpec(memory_space=pltpu.SMEM)
    hbm = pl.BlockSpec(memory_space=pltpu.HBM)
    given = [parity, x_start] + [one for group in groups for one in group]
    return pl.pallas_call(
        functools.partial(finish_kernel, firsts),
        in_specs=[smem] + [vm] * (len(given) - 1) + [hbm] * len(into),
        out_specs=hbm,
        out_shape=jax.ShapeDtypeStruct((1, rows, width), f32),
        scratch_shapes=[VM((rows, group[1].shape[1]), f32) for group in groups]
        + [pltpu.SemaphoreType.DMA((len(groups),))],
        input_output_aliases={len(given): 0} if into else {},
        compiler_params=params(6),
        name="finish",
    )(*given, *into)


def per_device(
    n_step,
    n_seq,
    trajectory,
    x_start,
    t_idx,
    mod_table,
    step_sizes,
    q_gain,
    k_gain,
    w_qkv,
    w_mlp_in,
    w_out_attn,
    w_out_mlp,
):
    head = q_gain.shape[0]
    rows, width = x_start.shape
    chips = n_seq // 2
    groups = n_step // 2
    half = rows // 2
    unit = width // 24
    counts = [n * unit for n in (9,8,7)]
    chunks = len(counts)
    firsts = [sum(counts[:c]) for c in range(chunks)]
    qg, kg = q_gain[None, :], k_gain[None, :]

    def to_core(x):
        return lax.ppermute(x, "seq", [(i, i ^ 1) for i in range(n_seq)])

    def to_chip(x, offset):
        return lax.ppermute(x, "seq", [(i, (i + 2 * offset) % n_seq) for i in range(n_seq)])

    def to_pair(x):
        return lax.ppermute(x, "step", [(i, i ^ 1) for i in range(n_step)])

    def tied(*values):
        return lax.optimization_barrier(values)

    parity = lax.rem(lax.axis_index("step"), 2)
    even = (parity == 0).astype(f32)
    which = parity[None]
    offsets = range(1, chips)

    mine, sg = norm_call(t_idx, trajectory, mod_table, step_sizes)
    far = [to_chip(mine, j) for j in offsets]
    q0, k0, v0, act0, low0, high0, *held = project_call(
        mine, to_core(mine), qg, kg, w_qkv, w_mlp_in, w_out_mlp, None
    )
    far, low0, high0 = tied(far, low0, high0)
    qs, ks, vs, acts = [], [k0], [v0], []
    for block in far:
        q, k, v, act = project_call(block, to_core(block), qg, kg, w_qkv, w_mlp_in, w_out_mlp, held)
        qs.append(q)
        ks.append(k)
        vs.append(v)
        acts.append(act)
    mixed = [attend_call(q, ks, vs, head) for q in qs]

    weights = [w_out_attn, w_out_mlp]
    got = [[] for _ in offsets]

    def jobs_of(c):
        return [([a, b], weights, [], firsts[c], counts[c]) for a, b in zip(mixed, acts)]

    def joined(parts, sent):
        return [join_call(keep, s) for (keep, _), s in zip(parts, sent)]

    def to_chips(ready):
        for j, one in enumerate(ready):
            got[j].append(to_chip(one, chips - 1 - j))

    parts = out_call(jobs_of(0))
    sent = [to_core(send) for _, send in parts]
    q0, parts = tied(q0, parts)
    mixed0 = attend_call(q0, ks, vs, head)
    mixed0, sent = tied(mixed0, sent)
    ready = joined(parts, sent)
    mixed, acts, mixed0, ready = tied(mixed, acts, mixed0, ready)
    to_chips(ready)
    jobs = [job for c in range(1, chunks) for job in jobs_of(c)]
    for c in range(chunks):
        jobs.append(([mixed0], [w_out_attn], [low0, high0], firsts[c], counts[c]))
    parts = out_call(jobs)
    sent = [to_core(send) for _, send in parts]
    keep = [part[0] for part in parts[-chunks:]]
    sent0 = sent[-chunks:]
    others = chips - 1
    first, keep, sent[:others] = tied([row[0] for row in got], keep, sent[:others])
    for row, one in zip(got, first):
        row[0] = one
    ready = joined(parts[:others], sent[:others])
    keep, ready = tied(keep, ready)
    to_chips(ready)
    for c in range(2, chunks):
        here = slice((c - 1) * others, c * others)
        to_chips(joined(parts[here], sent[here]))

    def along(pairs):
        return lambda x: lax.ppermute(x, "step", [(2 * a + i, 2 * b + i) for a, b in pairs for i in (0, 1)])

    group = lax.div(lax.axis_index("step"), 2)
    rounds = []
    span = 1
    while span < groups:
        pairs = [(b, b ^ span) for b in range(groups) if b ^ span < groups]
        rounds.append((span, along(pairs)))
        span *= 2

    def prefix_stages(c):
        held = {}

        def drift_of(fetched):
            drift = drift_call(which, keep[c], sent0[c], sg, fetched, firsts[c])
            held["kept"], held["other"], send = drift
            return send

        def pair_sum(fetched):
            held["fetched"] = fetched[0]
            held["total"] = held["kept"] + fetched[0].astype(f32)
            return held["total"].astype(bf16)

        def collect(r, fetched):
            one = fetched[0].astype(f32)
            upper = (lax.rem(lax.div(group, rounds[r][0]), 2) == 1).astype(f32)
            held["earlier"] = held["earlier"] + upper * one if r else upper * one
            if r == len(rounds) - 1:
                return (held["earlier"] + even * held["kept"]).astype(bf16)
            held["total"] = held["total"] + one
            return held["total"].astype(bf16)

        def finish(fetched):
            given = [held[name] for name in ("earlier", "kept", "fetched", "other")]
            stash.append((firsts[c], given + [fetched[0]]))
            if len(stash) in (1, chunks):
                mine = stash[len(stash) - 1 :] if len(stash) == 1 else stash[1:]
                places = [place for place, _ in mine]
                groups_in = [group for _, group in mine]
                into = list(written)
                written[:] = [finish_call(which, x_start, groups_in, places, into)]

        stages = [(drift_of, to_pair), (pair_sum, rounds[0][1])]
        for r in range(len(rounds)):
            move = to_pair if r == len(rounds) - 1 else rounds[r + 1][1]
            stages.append((functools.partial(collect, r), move))
        stages.append((finish, None))
        return stages

    plan = [prefix_stages(c) for c in range(chunks)]
    inbox = [[got[j][c] for j in range(chips - 1)] for c in range(chunks)]
    turns = []
    arrival = 2.0
    for c in range(chunks):
        share = 16.0 * (10 - 2 * c) / 24
        arrival += share
        when = arrival
        for i in range(len(plan[c])):
            turns.append((when, c, i))
            when += 2.2 + share * (1.0 if i == len(plan[c]) - 3 else 0.5)
    written, stash = [], []
    last = None
    for _, c, i in sorted(turns):
        compute, move = plan[c][i]
        fetched = inbox[c]
        if last is not None:
            fetched, last = tied(fetched, last)
        out = compute(fetched)
        if move is not None:
            inbox[c] = [move(out)]
            last = out
    return written[0]


def solution(mesh):
    placed = (
        P("step", "seq", None),
        P("seq", None),
        P("step"),
        P(),
        P(),
        P(),
        P(),
        P(None, None, "seq"),
        P(None, "seq"),
        P("seq", None),
        P("seq", None),
    )
    return jax.shard_map(
        functools.partial(per_device, mesh.shape["step"], mesh.shape["seq"]),
        mesh=mesh,
        in_specs=placed,
        out_specs=P("step", "seq", None),
        check_vma=False,
    )
```

```python
import functools
import math

import jax
import jax.numpy as jnp
from jax import lax
from jax.experimental import pallas as pl
from jax.experimental.pallas import tpu as pltpu
from jax.sharding import PartitionSpec as P

eps = 1e-06
f32 = jnp.float32
bf16 = jnp.bfloat16
VM = pltpu.VMEM
MIB = 1024 * 1024


def params(mib):
    return pltpu.CompilerParams(vmem_limit_bytes=mib * MIB)


def cost(flops, moved):
    return pl.CostEstimate(flops=flops, transcendentals=0, bytes_accessed=moved)


def norm_kernel(t_ref, size_ref, x_hbm, mod_hbm, m_hbm, sg_ref, x_ref, m_ref, mod_ref, sem, out_sem):
    width = x_hbm.shape[-1]
    pieces = sem.shape[0] - 1
    block = x_hbm.shape[1] // pieces
    t = t_ref[0]
    mod_copy = pltpu.make_async_copy(mod_hbm.at[pl.ds(t, 1), :], mod_ref, sem.at[pieces])
    mod_copy.start()
    copies = []
    for i in range(pieces):
        here = pl.ds(i * block, block)
        copies.append(pltpu.make_async_copy(x_hbm.at[0, here, :], x_ref.at[here, :], sem.at[i]))
        copies[i].start()
    mod_copy.wait()
    shift = mod_ref[:, :width]
    scale = 1.0 + mod_ref[:, width : 2 * width]
    sg_ref[...] = size_ref[t] * mod_ref[:, 2 * width :]
    for i in range(pieces):
        copies[i].wait()
        here = slice(i * block, (i + 1) * block)
        x = x_ref[here, :]
        center = x - jnp.mean(x, axis=-1, keepdims=True)
        spread = jnp.mean(center * center, axis=-1, keepdims=True)
        m_ref[here, :] = (center * lax.rsqrt(spread + eps) * scale + shift).astype(bf16)
        rows = pl.ds(i * block, block)
        copies[i] = pltpu.make_async_copy(m_ref.at[rows, :], m_hbm.at[rows, :], out_sem.at[i])
        copies[i].start()
    for copy in copies:
        copy.wait()


def norm_call(t_idx, trajectory, mod_table, step_sizes):
    _, rows, width = trajectory.shape
    smem = pl.BlockSpec(memory_space=pltpu.SMEM)
    hbm = pl.BlockSpec(memory_space=pltpu.HBM)
    vm = pl.BlockSpec(memory_space=VM)
    return pl.pallas_call(
        norm_kernel,
        in_specs=[smem, smem, hbm, hbm],
        out_specs=[hbm, vm],
        out_shape=[
            jax.ShapeDtypeStruct((rows, width), bf16),
            jax.ShapeDtypeStruct((1, width), f32),
        ],
        scratch_shapes=[
            VM((rows, width), f32),
            VM((rows, width), bf16),
            VM((1, 3 * width), f32),
            pltpu.SemaphoreType.DMA((5,)),
            pltpu.SemaphoreType.DMA((4,)),
        ],
        compiler_params=params(60),
        cost_estimate=cost(10 * rows * width, 0),
        name="norm",
    )(t_idx, step_sizes, trajectory, mod_table)


def project_kernel(tile, load, tiles, m0, m1, qg, kg, *refs):
    if load:
        wq_hbm, wm_hbm, wb_hbm, q, k, v, act, low, high = refs[:9]
        held, rows, wb, sem = refs[9:-3], refs[-3], refs[-2], refs[-1]
    else:
        held = refs[:tiles]
        q, k, v, act, rows = refs[tiles:]
    half = m0.shape[0]
    head = qg.shape[1]
    n_q = q.shape[1] // tile
    copies = []
    if load:
        for i in range(tiles):
            if i < 3 * n_q:
                source = wq_hbm.at[i // n_q, :, pl.ds(i % n_q * tile, tile)]
            else:
                source = wm_hbm.at[:, pl.ds((i - 3 * n_q) * tile, tile)]
            copies.append(pltpu.make_async_copy(source, held[i], sem.at[i]))
            copies[i].start()
        span = low.shape[1] // (sem.shape[0] - tiles)
        for at in range(0, low.shape[1], span):
            here = (slice(None), pl.ds(at, span))
            copies.append(pltpu.make_async_copy(wb_hbm.at[here], wb.at[here], sem.at[len(copies)]))
            copies[-1].start()
    rows[:half] = m0[...]
    rows[half:] = m1[...]

    def normed(y, gain):
        parts = []
        for h in range(tile // head):
            one = y[:, h * head : (h + 1) * head]
            square = jnp.mean(one * one, axis=-1, keepdims=True)
            parts.append((one * lax.rsqrt(square + eps) * gain).astype(bf16))
        return jnp.concatenate(parts, axis=1)

    for i in range(tiles):
        if load:
            copies[i].wait()
        y = jnp.dot(rows[...], held[i][...], preferred_element_type=f32)
        cols = slice(i % n_q * tile, (i % n_q + 1) * tile)
        if i < n_q:
            q[:, cols] = normed(y, qg[...])
        elif i < 2 * n_q:
            k[:, cols] = normed(y, kg[...])
        elif i < 3 * n_q:
            v[:, cols] = y.astype(bf16)
        else:
            cols = slice((i - 3 * n_q) * tile, (i - 3 * n_q + 1) * tile)
            act[:, cols] = jax.nn.gelu(y, approximate=True).astype(bf16)
    if load:
        for i, copy in enumerate(copies[tiles:]):
            copy.wait()
            cols = slice(i * span, (i + 1) * span)
            y = jnp.dot(act[...], wb[:, cols], preferred_element_type=f32)
            low[:, cols] = y[:half]
            high[:, cols] = y[half:]


def project_call(m0, m1, q_gain, k_gain, w_qkv, w_mlp_in, w_out_mlp, held):
    half, width = m0.shape
    heads = w_qkv.shape[2]
    hidden = w_mlp_in.shape[1]
    tile = min(512, heads)
    tiles = (3 * heads + hidden) // tile
    rows = 2 * half
    load = held is None
    vm = pl.BlockSpec(memory_space=VM)
    hbm = pl.BlockSpec(memory_space=pltpu.HBM)
    shapes = [jax.ShapeDtypeStruct((rows, heads), bf16)] * 3
    shapes.append(jax.ShapeDtypeStruct((rows, hidden), bf16))
    scratch = [VM((rows, width), bf16)]
    if load:
        shapes += [jax.ShapeDtypeStruct((half, width), f32)] * 2
        shapes += [jax.ShapeDtypeStruct((width, tile), bf16)] * tiles
        scratch.append(VM(w_out_mlp.shape, bf16))
        scratch.append(pltpu.SemaphoreType.DMA((tiles + 4,)))
    return pl.pallas_call(
        functools.partial(project_kernel, tile, load, tiles),
        in_specs=[vm] * 4 + ([hbm] * 3 if load else [vm] * tiles),
        out_specs=[vm] * len(shapes),
        out_shape=shapes,
        scratch_shapes=scratch,
        compiler_params=params(27 if load else 9),
        cost_estimate=cost(2 * rows * width * (3 * heads + hidden), 0),
        name="project",
    )(m0, m1, q_gain, k_gain, *([w_qkv, w_mlp_in, w_out_mlp] if load else held))


def attend_kernel(pairs, head, *refs):
    q_ref = refs[0]
    k_refs = refs[1 : 1 + pairs]
    v_refs = refs[1 + pairs : 1 + 2 * pairs]
    out = refs[1 + 2 * pairs]
    scale = math.log2(math.e) / math.sqrt(head)
    heads = [slice(at, at + head) for at in range(0, q_ref.shape[1], head)]
    scores = [
        [
            lax.dot_general(
                q_ref[:, cols], k[:, cols], (((1,), (1,)), ((), ())), preferred_element_type=f32
            )
            for k in k_refs
        ]
        for cols in heads
    ]
    tops = [
        functools.reduce(jnp.maximum, [jnp.max(s, axis=-1, keepdims=True) for s in one])
        for one in scores
    ]
    weights = [[jnp.exp2((s - top) * scale) for s in one] for one, top in zip(scores, tops)]
    totals = [sum(jnp.sum(w, axis=-1, keepdims=True) for w in one) for one in weights]
    for cols, one, total in zip(heads, weights, totals):
        mixed = sum(
            jnp.dot(w.astype(bf16), v[:, cols], preferred_element_type=f32)
            for w, v in zip(one, v_refs)
        )
        out[:, cols] = (mixed / total).astype(bf16)


def attend_call(q, ks, vs, head):
    vm = pl.BlockSpec(memory_space=VM)
    return pl.pallas_call(
        functools.partial(attend_kernel, len(ks), head),
        in_specs=[vm] * (1 + 2 * len(ks)),
        out_specs=vm,
        out_shape=jax.ShapeDtypeStruct(q.shape, bf16),
        compiler_params=params(9),
        cost_estimate=cost(4 * len(ks) * q.shape[0] ** 2 * q.shape[1] * 3, 0),
        name="attend",
    )(q, *ks, *vs)


def out_kernel(jobs, *refs):
    outs = refs[len(refs) - 2 * len(jobs) :]
    at = 0
    for turn, (parts, extras, first, count) in enumerate(jobs):
        xs = refs[at : at + parts]
        ws = refs[at + parts : at + 2 * parts]
        extra = refs[at + 2 * parts : at + 2 * parts + extras]
        at += 2 * parts + extras
        keep, send = outs[2 * turn : 2 * turn + 2]
        half = keep.shape[0]
        cols = slice(first, first + count)
        terms = [
            jnp.dot(x[...], w[:, cols], preferred_element_type=f32) for x, w in zip(xs, ws)
        ]
        y = functools.reduce(jnp.add, terms)
        low, high = y[:half], y[half:]
        if extra:
            low = low + extra[0][:, cols]
            high = high + extra[1][:, cols]
        keep[...] = low
        send[...] = high.astype(bf16)


def out_call(jobs):
    vm = pl.BlockSpec(memory_space=VM)
    given, plan, shapes, flops = [], [], [], 0
    for xs, ws, extra, first, count in jobs:
        given += [*xs, *ws, *extra]
        plan.append((len(xs), len(extra), first, count))
        half = xs[0].shape[0] // 2
        shapes.append(jax.ShapeDtypeStruct((half, count), f32))
        shapes.append(jax.ShapeDtypeStruct((half, count), bf16))
        flops += 4 * half * count * sum(x.shape[1] for x in xs)
    outs = pl.pallas_call(
        functools.partial(out_kernel, plan),
        in_specs=[vm] * len(given),
        out_specs=[vm] * len(shapes),
        out_shape=shapes,
        compiler_params=params(9),
        cost_estimate=cost(flops, 0),
        name="project_out",
    )(*given)
    return [tuple(outs[i : i + 2]) for i in range(0, len(outs), 2)]


def join_kernel(keep, sent, out):
    out[...] = (keep[...] + sent[...].astype(f32)).astype(bf16)


def join_call(keep, sent):
    vm = pl.BlockSpec(memory_space=VM)
    return pl.pallas_call(
        join_kernel,
        in_specs=[vm, vm],
        out_specs=vm,
        out_shape=jax.ShapeDtypeStruct(keep.shape, bf16),
        compiler_params=params(6),
        name="join",
    )(keep, sent)


def drift_kernel(first, parity, keep, sent, sg, *refs):
    fetched, (kept, other, send) = refs[:-3], refs[-3:]
    half, count = kept.shape
    p = parity[0]

    def part(which):
        rows = pl.ds(pl.multiple_of(which * half, half), half)
        branch = keep[rows, :] + sent[rows, :].astype(f32)
        for one in fetched:
            branch = branch + one[rows, :].astype(f32)
        return sg[:, first : first + count] * branch

    kept[...] = part(p)
    passed = part(1 - p)
    other[...] = passed
    send[...] = passed.astype(bf16)


def drift_call(parity, keep, sent, sg, fetched, first):
    rows, count = fetched[0].shape
    vm = pl.BlockSpec(memory_space=VM)
    smem = pl.BlockSpec(memory_space=pltpu.SMEM)
    shape = (rows // 2, count)
    return pl.pallas_call(
        functools.partial(drift_kernel, first),
        in_specs=[smem] + [vm] * (3 + len(fetched)),
        out_specs=[vm] * 3,
        out_shape=[
            jax.ShapeDtypeStruct(shape, f32),
            jax.ShapeDtypeStruct(shape, f32),
            jax.ShapeDtypeStruct(shape, bf16),
        ],
        compiler_params=params(6),
        name="drift",
    )(parity, keep, sent, sg, *fetched)


def finish_kernel(firsts, parity, x_start, *refs):
    n = len(firsts)
    given, rest = refs[: 5 * n], refs[-2 - n :]
    out, results, sem = rest[0], rest[1 : 1 + n], rest[1 + n]
    p = parity[0]
    odd = p.astype(f32)
    copies = []
    for i, first in enumerate(firsts):
        earlier, kept, fetched, other, back = given[5 * i : 5 * i + 5]
        half, count = kept.shape
        cols = slice(first, first + count)
        mine = pl.ds(pl.multiple_of(p * half, half), half)
        rest = pl.ds(pl.multiple_of((1 - p) * half, half), half)
        results[i][mine, :] = (
            x_start[mine, cols] + earlier[...] + kept[...] + odd * fetched[...].astype(f32)
        )
        results[i][rest, :] = x_start[rest, cols] + other[...] + back[...].astype(f32)
        copies.append(
            pltpu.make_async_copy(results[i], out.at[0, :, pl.ds(first, count)], sem.at[i])
        )
        copies[i].start()
    for copy in copies:
        copy.wait()


def finish_call(parity, x_start, groups, firsts, into):
    rows, width = x_start.shape
    vm = pl.BlockSpec(memory_space=VM)
    smem = pl.BlockSpec(memory_space=pltpu.SMEM)
    hbm = pl.BlockSpec(memory_space=pltpu.HBM)
    given = [parity, x_start] + [one for group in groups for one in group]
    return pl.pallas_call(
        functools.partial(finish_kernel, firsts),
        in_specs=[smem] + [vm] * (len(given) - 1) + [hbm] * len(into),
        out_specs=hbm,
        out_shape=jax.ShapeDtypeStruct((1, rows, width), f32),
        scratch_shapes=[VM((rows, group[1].shape[1]), f32) for group in groups]
        + [pltpu.SemaphoreType.DMA((len(groups),))],
        input_output_aliases={len(given): 0} if into else {},
        compiler_params=params(6),
        name="finish",
    )(*given, *into)


def per_device(
    n_step,
    n_seq,
    trajectory,
    x_start,
    t_idx,
    mod_table,
    step_sizes,
    q_gain,
    k_gain,
    w_qkv,
    w_mlp_in,
    w_out_attn,
    w_out_mlp,
):
    head = q_gain.shape[0]
    rows, width = x_start.shape
    chips = n_seq // 2
    groups = n_step // 2
    half = rows // 2
    unit = width // 24
    counts = [n * unit for n in (9,8,7)]
    chunks = len(counts)
    firsts = [sum(counts[:c]) for c in range(chunks)]
    qg, kg = q_gain[None, :], k_gain[None, :]

    def to_core(x):
        return lax.ppermute(x, "seq", [(i, i ^ 1) for i in range(n_seq)])

    def to_chip(x, offset):
        return lax.ppermute(x, "seq", [(i, (i + 2 * offset) % n_seq) for i in range(n_seq)])

    def to_pair(x):
        return lax.ppermute(x, "step", [(i, i ^ 1) for i in range(n_step)])

    def tied(*values):
        return lax.optimization_barrier(values)

    parity = lax.rem(lax.axis_index("step"), 2)
    even = (parity == 0).astype(f32)
    which = parity[None]
    offsets = range(1, chips)

    mine, sg = norm_call(t_idx, trajectory, mod_table, step_sizes)
    far = [to_chip(mine, j) for j in offsets]
    q0, k0, v0, act0, low0, high0, *held = project_call(
        mine, to_core(mine), qg, kg, w_qkv, w_mlp_in, w_out_mlp, None
    )
    far, low0, high0 = tied(far, low0, high0)
    qs, ks, vs, acts = [], [k0], [v0], []
    for block in far:
        q, k, v, act = project_call(block, to_core(block), qg, kg, w_qkv, w_mlp_in, w_out_mlp, held)
        qs.append(q)
        ks.append(k)
        vs.append(v)
        acts.append(act)
    mixed = [attend_call(q, ks, vs, head) for q in qs]

    weights = [w_out_attn, w_out_mlp]
    got = [[] for _ in offsets]

    def jobs_of(c):
        return [([a, b], weights, [], firsts[c], counts[c]) for a, b in zip(mixed, acts)]

    def joined(parts, sent):
        return [join_call(keep, s) for (keep, _), s in zip(parts, sent)]

    def to_chips(ready):
        for j, one in enumerate(ready):
            got[j].append(to_chip(one, chips - 1 - j))

    parts = out_call(jobs_of(0))
    sent = [to_core(send) for _, send in parts]
    q0, parts = tied(q0, parts)
    mixed0 = attend_call(q0, ks, vs, head)
    mixed0, sent = tied(mixed0, sent)
    ready = joined(parts, sent)
    mixed, acts, mixed0, ready = tied(mixed, acts, mixed0, ready)
    to_chips(ready)
    jobs = [job for c in range(1, chunks) for job in jobs_of(c)]
    for c in range(chunks):
        jobs.append(([mixed0], [w_out_attn], [low0, high0], firsts[c], counts[c]))
    parts = out_call(jobs)
    sent = [to_core(send) for _, send in parts]
    keep = [part[0] for part in parts[-chunks:]]
    sent0 = sent[-chunks:]
    others = chips - 1
    first, keep, sent[:others] = tied([row[0] for row in got], keep, sent[:others])
    for row, one in zip(got, first):
        row[0] = one
    ready = joined(parts[:others], sent[:others])
    keep, ready = tied(keep, ready)
    to_chips(ready)
    for c in range(2, chunks):
        here = slice((c - 1) * others, c * others)
        to_chips(joined(parts[here], sent[here]))

    def along(pairs):
        return lambda x: lax.ppermute(x, "step", [(2 * a + i, 2 * b + i) for a, b in pairs for i in (0, 1)])

    group = lax.div(lax.axis_index("step"), 2)
    rounds = []
    span = 1
    while span < groups:
        pairs = [(b, b ^ span) for b in range(groups) if b ^ span < groups]
        rounds.append((span, along(pairs)))
        span *= 2

    def prefix_stages(c):
        held = {}

        def drift_of(fetched):
            drift = drift_call(which, keep[c], sent0[c], sg, fetched, firsts[c])
            held["kept"], held["other"], send = drift
            return send

        def pair_sum(fetched):
            held["fetched"] = fetched[0]
            held["total"] = held["kept"] + fetched[0].astype(f32)
            return held["total"].astype(bf16)

        def collect(r, fetched):
            one = fetched[0].astype(f32)
            upper = (lax.rem(lax.div(group, rounds[r][0]), 2) == 1).astype(f32)
            held["earlier"] = held["earlier"] + upper * one if r else upper * one
            if r == len(rounds) - 1:
                return (held["earlier"] + even * held["kept"]).astype(bf16)
            held["total"] = held["total"] + one
            return held["total"].astype(bf16)

        def finish(fetched):
            given = [held[name] for name in ("earlier", "kept", "fetched", "other")]
            stash.append((firsts[c], given + [fetched[0]]))
            if len(stash) in (1, chunks):
                mine = stash[len(stash) - 1 :] if len(stash) == 1 else stash[1:]
                places = [place for place, _ in mine]
                groups_in = [group for _, group in mine]
                into = list(written)
                written[:] = [finish_call(which, x_start, groups_in, places, into)]

        stages = [(drift_of, to_pair), (pair_sum, rounds[0][1])]
        for r in range(len(rounds)):
            move = to_pair if r == len(rounds) - 1 else rounds[r + 1][1]
            stages.append((functools.partial(collect, r), move))
        stages.append((finish, None))
        return stages

    plan = [prefix_stages(c) for c in range(chunks)]
    inbox = [[got[j][c] for j in range(chips - 1)] for c in range(chunks)]
    turns = []
    arrival = 2.0
    for c in range(chunks):
        share = 16.0 * (10 - 2 * c) / 24
        arrival += share
        when = arrival
        for i in range(len(plan[c])):
            turns.append((when, c, i))
            when += 2.2 + share * (1.0 if i == len(plan[c]) - 3 else 0.5)
    written, stash = [], []
    last = None
    for _, c, i in sorted(turns):
        compute, move = plan[c][i]
        fetched = inbox[c]
        if last is not None:
            fetched, last = tied(fetched, last)
        out = compute(fetched)
        if move is not None:
            inbox[c] = [move(out)]
            last = out
    return written[0]


def solution(mesh):
    placed = (
        P("step", "seq", None),
        P("seq", None),
        P("step"),
        P(),
        P(),
        P(),
        P(),
        P(None, None, "seq"),
        P(None, "seq"),
        P("seq", None),
        P("seq", None),
    )
    return jax.shard_map(
        functools.partial(per_device, mesh.shape["step"], mesh.shape["seq"]),
        mesh=mesh,
        in_specs=placed,
        out_specs=P("step", "seq", None),
        check_vma=False,
    )
```

```python
import functools
import math

import jax
import jax.numpy as jnp
from jax import lax
from jax.experimental import pallas as pl
from jax.experimental.pallas import tpu as pltpu
from jax.sharding import PartitionSpec as P

eps = 1e-06
f32 = jnp.float32
bf16 = jnp.bfloat16
VM = pltpu.VMEM
MIB = 1024 * 1024


def params(mib):
    return pltpu.CompilerParams(vmem_limit_bytes=mib * MIB)


def cost(flops, moved):
    return pl.CostEstimate(flops=flops, transcendentals=0, bytes_accessed=moved)


def norm_kernel(t_ref, size_ref, x_hbm, mod_hbm, top_ref, low_ref, sg_ref, x_ref, mod_ref, sem):
    width = x_hbm.shape[-1]
    pieces = sem.shape[0] - 1
    block = x_hbm.shape[1] // pieces
    t = t_ref[0]
    mod_copy = pltpu.make_async_copy(mod_hbm.at[pl.ds(t, 1), :], mod_ref, sem.at[pieces])
    mod_copy.start()
    copies = []
    for i in range(pieces):
        here = pl.ds(i * block, block)
        copies.append(pltpu.make_async_copy(x_hbm.at[0, here, :], x_ref.at[here, :], sem.at[i]))
        copies[i].start()
    mod_copy.wait()
    shift = mod_ref[:, :width]
    scale = 1.0 + mod_ref[:, width : 2 * width]
    sg_ref[...] = size_ref[t] * mod_ref[:, 2 * width :]
    for i in range(pieces):
        copies[i].wait()
        here = slice(i * block, (i + 1) * block)
        x = x_ref[here, :]
        center = x - jnp.mean(x, axis=-1, keepdims=True)
        spread = jnp.mean(center * center, axis=-1, keepdims=True)
        m = (center * lax.rsqrt(spread + eps) * scale + shift).astype(bf16)
        if 2 * i < pieces:
            top_ref[here, :] = m
        else:
            at = i * block - top_ref.shape[0]
            low_ref[at : at + block, :] = m


def norm_call(t_idx, trajectory, mod_table, step_sizes):
    _, rows, width = trajectory.shape
    smem = pl.BlockSpec(memory_space=pltpu.SMEM)
    hbm = pl.BlockSpec(memory_space=pltpu.HBM)
    vm = pl.BlockSpec(memory_space=VM)
    return pl.pallas_call(
        norm_kernel,
        in_specs=[smem, smem, hbm, hbm],
        out_specs=[vm, vm, vm],
        out_shape=[
            jax.ShapeDtypeStruct((rows // 2, width), bf16),
            jax.ShapeDtypeStruct((rows // 2, width), bf16),
            jax.ShapeDtypeStruct((1, width), f32),
        ],
        scratch_shapes=[
            VM((rows, width), f32),
            VM((1, 3 * width), f32),
            pltpu.SemaphoreType.DMA((5,)),
        ],
        compiler_params=params(60),
        cost_estimate=cost(10 * rows * width, 0),
        name="norm",
    )(t_idx, step_sizes, trajectory, mod_table)


def project_kernel(tile, load, tiles, m0, m1, m2, m3, qg, kg, *refs):
    if load:
        wq_hbm, wm_hbm, wb_hbm, q, k, v, act, low, high = refs[:9]
        held, rows, wb, sem = refs[9:-3], refs[-3], refs[-2], refs[-1]
    else:
        held = refs[:tiles]
        q, k, v, act, rows = refs[tiles:]
    quarter = m0.shape[0]
    half = 2 * quarter
    head = qg.shape[1]
    n_q = q.shape[1] // tile
    copies = []
    if load:
        for i in range(tiles):
            if i < 3 * n_q:
                source = wq_hbm.at[i // n_q, :, pl.ds(i % n_q * tile, tile)]
            else:
                source = wm_hbm.at[:, pl.ds((i - 3 * n_q) * tile, tile)]
            copies.append(pltpu.make_async_copy(source, held[i], sem.at[i]))
            copies[i].start()
        span = low.shape[1] // (sem.shape[0] - tiles)
        for at in range(0, low.shape[1], span):
            here = (slice(None), pl.ds(at, span))
            copies.append(pltpu.make_async_copy(wb_hbm.at[here], wb.at[here], sem.at[len(copies)]))
            copies[-1].start()
    for i, m in enumerate((m0, m1, m2, m3)):
        rows[i * quarter : (i + 1) * quarter] = m[...]

    def normed(y, gain):
        parts = []
        for h in range(tile // head):
            one = y[:, h * head : (h + 1) * head]
            square = jnp.mean(one * one, axis=-1, keepdims=True)
            parts.append((one * lax.rsqrt(square + eps) * gain).astype(bf16))
        return jnp.concatenate(parts, axis=1)

    for i in range(tiles):
        if load:
            copies[i].wait()
        y = jnp.dot(rows[...], held[i][...], preferred_element_type=f32)
        cols = slice(i % n_q * tile, (i % n_q + 1) * tile)
        if i < n_q:
            q[:, cols] = normed(y, qg[...])
        elif i < 2 * n_q:
            k[:, cols] = normed(y, kg[...])
        elif i < 3 * n_q:
            v[:, cols] = y.astype(bf16)
        else:
            cols = slice((i - 3 * n_q) * tile, (i - 3 * n_q + 1) * tile)
            act[:, cols] = jax.nn.gelu(y, approximate=True).astype(bf16)
    if load:
        for i, copy in enumerate(copies[tiles:]):
            copy.wait()
            cols = slice(i * span, (i + 1) * span)
            y = jnp.dot(act[...], wb[:, cols], preferred_element_type=f32)
            low[:, cols] = y[:half]
            high[:, cols] = y[half:]


def project_call(given, q_gain, k_gain, w_qkv, w_mlp_in, w_out_mlp, held):
    half, width = 2 * given[0].shape[0], given[0].shape[1]
    heads = w_qkv.shape[2]
    hidden = w_mlp_in.shape[1]
    tile = min(512, heads)
    tiles = (3 * heads + hidden) // tile
    rows = 2 * half
    load = held is None
    vm = pl.BlockSpec(memory_space=VM)
    hbm = pl.BlockSpec(memory_space=pltpu.HBM)
    shapes = [jax.ShapeDtypeStruct((rows, heads), bf16)] * 3
    shapes.append(jax.ShapeDtypeStruct((rows, hidden), bf16))
    scratch = [VM((rows, width), bf16)]
    if load:
        shapes += [jax.ShapeDtypeStruct((half, width), f32)] * 2
        shapes += [jax.ShapeDtypeStruct((width, tile), bf16)] * tiles
        scratch.append(VM(w_out_mlp.shape, bf16))
        scratch.append(pltpu.SemaphoreType.DMA((tiles + 4,)))
    return pl.pallas_call(
        functools.partial(project_kernel, tile, load, tiles),
        in_specs=[vm] * 6 + ([hbm] * 3 if load else [vm] * tiles),
        out_specs=[vm] * len(shapes),
        out_shape=shapes,
        scratch_shapes=scratch,
        compiler_params=params(27 if load else 9),
        cost_estimate=cost(2 * rows * width * (3 * heads + hidden), 0),
        name="project",
    )(*given, q_gain, k_gain, *([w_qkv, w_mlp_in, w_out_mlp] if load else held))


def attend_kernel(pairs, head, *refs):
    q_ref = refs[0]
    k_refs = refs[1 : 1 + pairs]
    v_refs = refs[1 + pairs : 1 + 2 * pairs]
    out = refs[1 + 2 * pairs]
    scale = math.log2(math.e) / math.sqrt(head)
    heads = [slice(at, at + head) for at in range(0, q_ref.shape[1], head)]
    scores = [
        [
            lax.dot_general(
                q_ref[:, cols], k[:, cols], (((1,), (1,)), ((), ())), preferred_element_type=f32
            )
            for k in k_refs
        ]
        for cols in heads
    ]
    tops = [
        functools.reduce(jnp.maximum, [jnp.max(s, axis=-1, keepdims=True) for s in one])
        for one in scores
    ]
    weights = [[jnp.exp2((s - top) * scale) for s in one] for one, top in zip(scores, tops)]
    totals = [sum(jnp.sum(w, axis=-1, keepdims=True) for w in one) for one in weights]
    for cols, one, total in zip(heads, weights, totals):
        mixed = sum(
            jnp.dot(w.astype(bf16), v[:, cols], preferred_element_type=f32)
            for w, v in zip(one, v_refs)
        )
        out[:, cols] = (mixed / total).astype(bf16)


def attend_call(q, ks, vs, head):
    vm = pl.BlockSpec(memory_space=VM)
    return pl.pallas_call(
        functools.partial(attend_kernel, len(ks), head),
        in_specs=[vm] * (1 + 2 * len(ks)),
        out_specs=vm,
        out_shape=jax.ShapeDtypeStruct(q.shape, bf16),
        compiler_params=params(9),
        cost_estimate=cost(4 * len(ks) * q.shape[0] ** 2 * q.shape[1] * 3, 0),
        name="attend",
    )(q, *ks, *vs)


def out_kernel(jobs, *refs):
    outs = refs[len(refs) - 2 * len(jobs) :]
    at = 0
    for turn, (parts, extras, first, count) in enumerate(jobs):
        xs = refs[at : at + parts]
        ws = refs[at + parts : at + 2 * parts]
        extra = refs[at + 2 * parts : at + 2 * parts + extras]
        at += 2 * parts + extras
        keep, send = outs[2 * turn : 2 * turn + 2]
        half = keep.shape[0]
        cols = slice(first, first + count)
        terms = [
            jnp.dot(x[...], w[:, cols], preferred_element_type=f32) for x, w in zip(xs, ws)
        ]
        y = functools.reduce(jnp.add, terms)
        low, high = y[:half], y[half:]
        if extra:
            low = low + extra[0][:, cols]
            high = high + extra[1][:, cols]
        keep[...] = low
        send[...] = high.astype(bf16)


def out_call(jobs):
    vm = pl.BlockSpec(memory_space=VM)
    given, plan, shapes, flops = [], [], [], 0
    for xs, ws, extra, first, count in jobs:
        given += [*xs, *ws, *extra]
        plan.append((len(xs), len(extra), first, count))
        half = xs[0].shape[0] // 2
        shapes.append(jax.ShapeDtypeStruct((half, count), f32))
        shapes.append(jax.ShapeDtypeStruct((half, count), bf16))
        flops += 4 * half * count * sum(x.shape[1] for x in xs)
    outs = pl.pallas_call(
        functools.partial(out_kernel, plan),
        in_specs=[vm] * len(given),
        out_specs=[vm] * len(shapes),
        out_shape=shapes,
        compiler_params=params(9),
        cost_estimate=cost(flops, 0),
        name="project_out",
    )(*given)
    return [tuple(outs[i : i + 2]) for i in range(0, len(outs), 2)]


def join_kernel(keep, sent, out):
    out[...] = (keep[...] + sent[...].astype(f32)).astype(bf16)


def join_call(keep, sent):
    vm = pl.BlockSpec(memory_space=VM)
    return pl.pallas_call(
        join_kernel,
        in_specs=[vm, vm],
        out_specs=vm,
        out_shape=jax.ShapeDtypeStruct(keep.shape, bf16),
        compiler_params=params(6),
        name="join",
    )(keep, sent)


def drift_kernel(first, parity, keep, sent, sg, *refs):
    fetched, (kept, other, send) = refs[:-3], refs[-3:]
    half, count = kept.shape
    p = parity[0]

    def part(which):
        rows = pl.ds(pl.multiple_of(which * half, half), half)
        branch = keep[rows, :] + sent[rows, :].astype(f32)
        for one in fetched:
            branch = branch + one[rows, :].astype(f32)
        return sg[:, first : first + count] * branch

    kept[...] = part(p)
    passed = part(1 - p)
    other[...] = passed
    send[...] = passed.astype(bf16)


def drift_call(parity, keep, sent, sg, fetched, first):
    rows, count = fetched[0].shape
    vm = pl.BlockSpec(memory_space=VM)
    smem = pl.BlockSpec(memory_space=pltpu.SMEM)
    shape = (rows // 2, count)
    return pl.pallas_call(
        functools.partial(drift_kernel, first),
        in_specs=[smem] + [vm] * (3 + len(fetched)),
        out_specs=[vm] * 3,
        out_shape=[
            jax.ShapeDtypeStruct(shape, f32),
            jax.ShapeDtypeStruct(shape, f32),
            jax.ShapeDtypeStruct(shape, bf16),
        ],
        compiler_params=params(6),
        name="drift",
    )(parity, keep, sent, sg, *fetched)


def finish_kernel(firsts, parity, x_start, *refs):
    n = len(firsts)
    given, rest = refs[: 5 * n], refs[-2 - n :]
    out, results, sem = rest[0], rest[1 : 1 + n], rest[1 + n]
    p = parity[0]
    odd = p.astype(f32)
    copies = []
    for i, first in enumerate(firsts):
        earlier, kept, fetched, other, back = given[5 * i : 5 * i + 5]
        half, count = kept.shape
        cols = slice(first, first + count)
        mine = pl.ds(pl.multiple_of(p * half, half), half)
        rest = pl.ds(pl.multiple_of((1 - p) * half, half), half)
        results[i][mine, :] = (
            x_start[mine, cols] + earlier[...] + kept[...] + odd * fetched[...].astype(f32)
        )
        results[i][rest, :] = x_start[rest, cols] + other[...] + back[...].astype(f32)
        copies.append(
            pltpu.make_async_copy(results[i], out.at[0, :, pl.ds(first, count)], sem.at[i])
        )
        copies[i].start()
    for copy in copies:
        copy.wait()


def finish_call(parity, x_start, groups, firsts, into):
    rows, width = x_start.shape
    vm = pl.BlockSpec(memory_space=VM)
    smem = pl.BlockSpec(memory_space=pltpu.SMEM)
    hbm = pl.BlockSpec(memory_space=pltpu.HBM)
    given = [parity, x_start] + [one for group in groups for one in group]
    return pl.pallas_call(
        functools.partial(finish_kernel, firsts),
        in_specs=[smem] + [vm] * (len(given) - 1) + [hbm] * len(into),
        out_specs=hbm,
        out_shape=jax.ShapeDtypeStruct((1, rows, width), f32),
        scratch_shapes=[VM((rows, group[1].shape[1]), f32) for group in groups]
        + [pltpu.SemaphoreType.DMA((len(groups),))],
        input_output_aliases={len(given): 0} if into else {},
        compiler_params=params(6),
        name="finish",
    )(*given, *into)


def per_device(
    n_step,
    n_seq,
    trajectory,
    x_start,
    t_idx,
    mod_table,
    step_sizes,
    q_gain,
    k_gain,
    w_qkv,
    w_mlp_in,
    w_out_attn,
    w_out_mlp,
):
    head = q_gain.shape[0]
    rows, width = x_start.shape
    chips = n_seq // 2
    groups = n_step // 2
    half = rows // 2
    unit = width // 24
    counts = [n * unit for n in (9,8,7)]
    chunks = len(counts)
    firsts = [sum(counts[:c]) for c in range(chunks)]
    qg, kg = q_gain[None, :], k_gain[None, :]

    def to_core(x):
        return lax.ppermute(x, "seq", [(i, i ^ 1) for i in range(n_seq)])

    def to_chip(x, offset):
        return lax.ppermute(x, "seq", [(i, (i + 2 * offset) % n_seq) for i in range(n_seq)])

    def to_pair(x):
        return lax.ppermute(x, "step", [(i, i ^ 1) for i in range(n_step)])

    def tied(*values):
        return lax.optimization_barrier(values)

    parity = lax.rem(lax.axis_index("step"), 2)
    even = (parity == 0).astype(f32)
    which = parity[None]
    offsets = range(1, chips)

    *mine, sg = norm_call(t_idx, trajectory, mod_table, step_sizes)
    far = [[to_chip(part, j) for part in mine] for j in offsets]
    given = mine + [to_core(part) for part in mine]
    q0, k0, v0, act0, low0, high0, *held = project_call(
        given, qg, kg, w_qkv, w_mlp_in, w_out_mlp, None
    )
    given = []
    for top, low in far:
        top, q0 = tied(top, q0)
        next_top = to_core(top)
        low, next_top = tied(low, next_top)
        given.append([top, low, next_top, to_core(low)])
    qs, ks, vs, acts = [], [k0], [v0], []
    for blocks in given:
        q, k, v, act = project_call(blocks, qg, kg, w_qkv, w_mlp_in, w_out_mlp, held)
        qs.append(q)
        ks.append(k)
        vs.append(v)
        acts.append(act)
    mixed = [attend_call(q, ks, vs, head) for q in qs]

    weights = [w_out_attn, w_out_mlp]
    got = [[] for _ in offsets]

    def jobs_of(c):
        return [([a, b], weights, [], firsts[c], counts[c]) for a, b in zip(mixed, acts)]

    def joined(parts, sent):
        return [join_call(keep, s) for (keep, _), s in zip(parts, sent)]

    def to_chips(ready):
        for j, one in enumerate(ready):
            got[j].append(to_chip(one, chips - 1 - j))

    parts = out_call(jobs_of(0))
    sent = [to_core(send) for _, send in parts]
    q0, parts = tied(q0, parts)
    mixed0 = attend_call(q0, ks, vs, head)
    mixed0, sent = tied(mixed0, sent)
    ready = joined(parts, sent)
    mixed, acts, mixed0, ready = tied(mixed, acts, mixed0, ready)
    to_chips(ready)
    jobs = [job for c in range(1, chunks) for job in jobs_of(c)]
    for c in range(chunks):
        jobs.append(([mixed0], [w_out_attn], [low0, high0], firsts[c], counts[c]))
    parts = out_call(jobs)
    sent = [to_core(send) for _, send in parts]
    keep = [part[0] for part in parts[-chunks:]]
    sent0 = sent[-chunks:]
    others = chips - 1
    first, keep, sent[:others] = tied([row[0] for row in got], keep, sent[:others])
    for row, one in zip(got, first):
        row[0] = one
    ready = joined(parts[:others], sent[:others])
    keep, ready = tied(keep, ready)
    to_chips(ready)
    for c in range(2, chunks):
        here = slice((c - 1) * others, c * others)
        to_chips(joined(parts[here], sent[here]))

    def along(pairs):
        return lambda x: lax.ppermute(x, "step", [(2 * a + i, 2 * b + i) for a, b in pairs for i in (0, 1)])

    group = lax.div(lax.axis_index("step"), 2)
    rounds = []
    span = 1
    while span < groups:
        pairs = [(b, b ^ span) for b in range(groups) if b ^ span < groups]
        rounds.append((span, along(pairs)))
        span *= 2

    def prefix_stages(c):
        held = {}

        def drift_of(fetched):
            drift = drift_call(which, keep[c], sent0[c], sg, fetched, firsts[c])
            held["kept"], held["other"], send = drift
            return send

        def pair_sum(fetched):
            held["fetched"] = fetched[0]
            held["total"] = held["kept"] + fetched[0].astype(f32)
            return held["total"].astype(bf16)

        def collect(r, fetched):
            one = fetched[0].astype(f32)
            upper = (lax.rem(lax.div(group, rounds[r][0]), 2) == 1).astype(f32)
            held["earlier"] = held["earlier"] + upper * one if r else upper * one
            if r == len(rounds) - 1:
                return (held["earlier"] + even * held["kept"]).astype(bf16)
            held["total"] = held["total"] + one
            return held["total"].astype(bf16)

        def finish(fetched):
            given = [held[name] for name in ("earlier", "kept", "fetched", "other")]
            stash.append((firsts[c], given + [fetched[0]]))
            if len(stash) in (1, chunks):
                mine = stash[len(stash) - 1 :] if len(stash) == 1 else stash[1:]
                places = [place for place, _ in mine]
                groups_in = [group for _, group in mine]
                into = list(written)
                written[:] = [finish_call(which, x_start, groups_in, places, into)]

        stages = [(drift_of, to_pair), (pair_sum, rounds[0][1])]
        for r in range(len(rounds)):
            move = to_pair if r == len(rounds) - 1 else rounds[r + 1][1]
            stages.append((functools.partial(collect, r), move))
        stages.append((finish, None))
        return stages

    plan = [prefix_stages(c) for c in range(chunks)]
    inbox = [[got[j][c] for j in range(chips - 1)] for c in range(chunks)]
    turns = []
    arrival = 2.0
    for c in range(chunks):
        share = 16.0 * (10 - 2 * c) / 24
        arrival += share
        when = arrival
        for i in range(len(plan[c])):
            turns.append((when, c, i))
            when += 2.2 + share * (1.0 if i == len(plan[c]) - 3 else 0.5)
    written, stash = [], []
    last = None
    for _, c, i in sorted(turns):
        compute, move = plan[c][i]
        fetched = inbox[c]
        if last is not None:
            fetched, last = tied(fetched, last)
        out = compute(fetched)
        if move is not None:
            inbox[c] = [move(out)]
            last = out
    return written[0]


def solution(mesh):
    placed = (
        P("step", "seq", None),
        P("seq", None),
        P("step"),
        P(),
        P(),
        P(),
        P(),
        P(None, None, "seq"),
        P(None, "seq"),
        P("seq", None),
        P("seq", None),
    )
    return jax.shard_map(
        functools.partial(per_device, mesh.shape["step"], mesh.shape["seq"]),
        mesh=mesh,
        in_specs=placed,
        out_specs=P("step", "seq", None),
        check_vma=False,
    )
```

```python
import functools
import math

import jax
import jax.numpy as jnp
from jax import lax
from jax.experimental import pallas as pl
from jax.experimental.pallas import tpu as pltpu
from jax.sharding import PartitionSpec as P

eps = 1e-06
f32 = jnp.float32
bf16 = jnp.bfloat16
VM = pltpu.VMEM
MIB = 1024 * 1024


def params(mib):
    return pltpu.CompilerParams(vmem_limit_bytes=mib * MIB)


def cost(flops, moved):
    return pl.CostEstimate(flops=flops, transcendentals=0, bytes_accessed=moved)


def norm_kernel(t_ref, size_ref, x_hbm, mod_hbm, top_ref, low_ref, sg_ref, x_ref, mod_ref, sem):
    width = x_hbm.shape[-1]
    pieces = sem.shape[0] - 1
    block = x_hbm.shape[1] // pieces
    t = t_ref[0]
    copies = []
    for i in range(pieces):
        here = pl.ds(i * block, block)
        copies.append(pltpu.make_async_copy(x_hbm.at[0, here, :], x_ref.at[here, :], sem.at[i]))
        copies[i].start()
    mod_copy = pltpu.make_async_copy(mod_hbm.at[pl.ds(t, 1), :], mod_ref, sem.at[pieces])
    mod_copy.start()
    mod_copy.wait()
    shift = mod_ref[:, :width]
    scale = 1.0 + mod_ref[:, width : 2 * width]
    sg_ref[...] = size_ref[t] * mod_ref[:, 2 * width :]
    for i in range(pieces):
        copies[i].wait()
        here = slice(i * block, (i + 1) * block)
        x = x_ref[here, :]
        center = x - jnp.mean(x, axis=-1, keepdims=True)
        spread = jnp.mean(center * center, axis=-1, keepdims=True)
        m = (center * lax.rsqrt(spread + eps) * scale + shift).astype(bf16)
        if 2 * i < pieces:
            top_ref[here, :] = m
        else:
            at = i * block - top_ref.shape[0]
            low_ref[at : at + block, :] = m


def norm_call(t_idx, trajectory, mod_table, step_sizes):
    _, rows, width = trajectory.shape
    smem = pl.BlockSpec(memory_space=pltpu.SMEM)
    hbm = pl.BlockSpec(memory_space=pltpu.HBM)
    vm = pl.BlockSpec(memory_space=VM)
    return pl.pallas_call(
        norm_kernel,
        in_specs=[smem, smem, hbm, hbm],
        out_specs=[vm, vm, vm],
        out_shape=[
            jax.ShapeDtypeStruct((rows // 2, width), bf16),
            jax.ShapeDtypeStruct((rows // 2, width), bf16),
            jax.ShapeDtypeStruct((1, width), f32),
        ],
        scratch_shapes=[
            VM((rows, width), f32),
            VM((1, 3 * width), f32),
            pltpu.SemaphoreType.DMA((5,)),
        ],
        compiler_params=params(60),
        cost_estimate=cost(10 * rows * width, 0),
        name="norm",
    )(t_idx, step_sizes, trajectory, mod_table)


def project_kernel(tile, load, tiles, m0, m1, m2, m3, qg, kg, *refs):
    if load:
        wq_hbm, wm_hbm, wb_hbm, q, k, v, act, low, high = refs[:9]
        held, rows, wb, sem = refs[9:-3], refs[-3], refs[-2], refs[-1]
    else:
        held = refs[:tiles]
        q, k, v, act, rows = refs[tiles:]
    quarter = m0.shape[0]
    half = 2 * quarter
    head = qg.shape[1]
    n_q = q.shape[1] // tile
    copies = []
    if load:
        for i in range(tiles):
            if i < 3 * n_q:
                source = wq_hbm.at[i // n_q, :, pl.ds(i % n_q * tile, tile)]
            else:
                source = wm_hbm.at[:, pl.ds((i - 3 * n_q) * tile, tile)]
            copies.append(pltpu.make_async_copy(source, held[i], sem.at[i]))
            copies[i].start()
        span = low.shape[1] // (sem.shape[0] - tiles)
        for at in range(0, low.shape[1], span):
            here = (slice(None), pl.ds(at, span))
            copies.append(pltpu.make_async_copy(wb_hbm.at[here], wb.at[here], sem.at[len(copies)]))
            copies[-1].start()
    for i, m in enumerate((m0, m1, m2, m3)):
        rows[i * quarter : (i + 1) * quarter] = m[...]

    def normed(y, gain):
        parts = []
        for h in range(tile // head):
            one = y[:, h * head : (h + 1) * head]
            square = jnp.mean(one * one, axis=-1, keepdims=True)
            parts.append((one * lax.rsqrt(square + eps) * gain).astype(bf16))
        return jnp.concatenate(parts, axis=1)

    for i in range(tiles):
        if load:
            copies[i].wait()
        y = jnp.dot(rows[...], held[i][...], preferred_element_type=f32)
        cols = slice(i % n_q * tile, (i % n_q + 1) * tile)
        if i < n_q:
            q[:, cols] = normed(y, qg[...])
        elif i < 2 * n_q:
            k[:, cols] = normed(y, kg[...])
        elif i < 3 * n_q:
            v[:, cols] = y.astype(bf16)
        else:
            cols = slice((i - 3 * n_q) * tile, (i - 3 * n_q + 1) * tile)
            act[:, cols] = jax.nn.gelu(y, approximate=True).astype(bf16)
    if load:
        for i, copy in enumerate(copies[tiles:]):
            copy.wait()
            cols = slice(i * span, (i + 1) * span)
            y = jnp.dot(act[...], wb[:, cols], preferred_element_type=f32)
            low[:, cols] = y[:half]
            high[:, cols] = y[half:]


def project_call(given, q_gain, k_gain, w_qkv, w_mlp_in, w_out_mlp, held):
    half, width = 2 * given[0].shape[0], given[0].shape[1]
    heads = w_qkv.shape[2]
    hidden = w_mlp_in.shape[1]
    tile = min(512, heads)
    tiles = (3 * heads + hidden) // tile
    rows = 2 * half
    load = held is None
    vm = pl.BlockSpec(memory_space=VM)
    hbm = pl.BlockSpec(memory_space=pltpu.HBM)
    shapes = [jax.ShapeDtypeStruct((rows, heads), bf16)] * 3
    shapes.append(jax.ShapeDtypeStruct((rows, hidden), bf16))
    scratch = [VM((rows, width), bf16)]
    if load:
        shapes += [jax.ShapeDtypeStruct((half, width), f32)] * 2
        shapes += [jax.ShapeDtypeStruct((width, tile), bf16)] * tiles
        scratch.append(VM(w_out_mlp.shape, bf16))
        scratch.append(pltpu.SemaphoreType.DMA((tiles + 4,)))
    return pl.pallas_call(
        functools.partial(project_kernel, tile, load, tiles),
        in_specs=[vm] * 6 + ([hbm] * 3 if load else [vm] * tiles),
        out_specs=[vm] * len(shapes),
        out_shape=shapes,
        scratch_shapes=scratch,
        compiler_params=params(27 if load else 9),
        cost_estimate=cost(2 * rows * width * (3 * heads + hidden), 0),
        name="project",
    )(*given, q_gain, k_gain, *([w_qkv, w_mlp_in, w_out_mlp] if load else held))


def attend_kernel(pairs, head, *refs):
    q_ref = refs[0]
    k_refs = refs[1 : 1 + pairs]
    v_refs = refs[1 + pairs : 1 + 2 * pairs]
    out = refs[1 + 2 * pairs]
    scale = math.log2(math.e) / math.sqrt(head)
    heads = [slice(at, at + head) for at in range(0, q_ref.shape[1], head)]
    scores = [
        [
            lax.dot_general(
                q_ref[:, cols], k[:, cols], (((1,), (1,)), ((), ())), preferred_element_type=f32
            )
            for k in k_refs
        ]
        for cols in heads
    ]
    tops = [
        functools.reduce(jnp.maximum, [jnp.max(s, axis=-1, keepdims=True) for s in one])
        for one in scores
    ]
    weights = [[jnp.exp2((s - top) * scale) for s in one] for one, top in zip(scores, tops)]
    totals = [sum(jnp.sum(w, axis=-1, keepdims=True) for w in one) for one in weights]
    for cols, one, total in zip(heads, weights, totals):
        mixed = sum(
            jnp.dot(w.astype(bf16), v[:, cols], preferred_element_type=f32)
            for w, v in zip(one, v_refs)
        )
        out[:, cols] = (mixed / total).astype(bf16)


def attend_call(q, ks, vs, head):
    vm = pl.BlockSpec(memory_space=VM)
    return pl.pallas_call(
        functools.partial(attend_kernel, len(ks), head),
        in_specs=[vm] * (1 + 2 * len(ks)),
        out_specs=vm,
        out_shape=jax.ShapeDtypeStruct(q.shape, bf16),
        compiler_params=params(9),
        cost_estimate=cost(4 * len(ks) * q.shape[0] ** 2 * q.shape[1] * 3, 0),
        name="attend",
    )(q, *ks, *vs)


def out_kernel(jobs, *refs):
    outs = refs[len(refs) - 2 * len(jobs) :]
    at = 0
    for turn, (parts, extras, first, count) in enumerate(jobs):
        xs = refs[at : at + parts]
        ws = refs[at + parts : at + 2 * parts]
        extra = refs[at + 2 * parts : at + 2 * parts + extras]
        at += 2 * parts + extras
        keep, send = outs[2 * turn : 2 * turn + 2]
        half = keep.shape[0]
        cols = slice(first, first + count)
        terms = [
            jnp.dot(x[...], w[:, cols], preferred_element_type=f32) for x, w in zip(xs, ws)
        ]
        y = functools.reduce(jnp.add, terms)
        low, high = y[:half], y[half:]
        if extra:
            low = low + extra[0][:, cols]
            high = high + extra[1][:, cols]
        keep[...] = low
        send[...] = high.astype(bf16)


def out_call(jobs):
    vm = pl.BlockSpec(memory_space=VM)
    given, plan, shapes, flops = [], [], [], 0
    for xs, ws, extra, first, count in jobs:
        given += [*xs, *ws, *extra]
        plan.append((len(xs), len(extra), first, count))
        half = xs[0].shape[0] // 2
        shapes.append(jax.ShapeDtypeStruct((half, count), f32))
        shapes.append(jax.ShapeDtypeStruct((half, count), bf16))
        flops += 4 * half * count * sum(x.shape[1] for x in xs)
    outs = pl.pallas_call(
        functools.partial(out_kernel, plan),
        in_specs=[vm] * len(given),
        out_specs=[vm] * len(shapes),
        out_shape=shapes,
        compiler_params=params(9),
        cost_estimate=cost(flops, 0),
        name="project_out",
    )(*given)
    return [tuple(outs[i : i + 2]) for i in range(0, len(outs), 2)]


def join_kernel(keep, sent, out):
    out[...] = (keep[...] + sent[...].astype(f32)).astype(bf16)


def join_call(keep, sent):
    vm = pl.BlockSpec(memory_space=VM)
    return pl.pallas_call(
        join_kernel,
        in_specs=[vm, vm],
        out_specs=vm,
        out_shape=jax.ShapeDtypeStruct(keep.shape, bf16),
        compiler_params=params(6),
        name="join",
    )(keep, sent)


def drift_kernel(first, parity, keep, sent, sg, *refs):
    fetched, (kept, other, send) = refs[:-3], refs[-3:]
    half, count = kept.shape
    p = parity[0]

    def part(which):
        rows = pl.ds(pl.multiple_of(which * half, half), half)
        branch = keep[rows, :] + sent[rows, :].astype(f32)
        for one in fetched:
            branch = branch + one[rows, :].astype(f32)
        return sg[:, first : first + count] * branch

    kept[...] = part(p)
    passed = part(1 - p)
    other[...] = passed
    send[...] = passed.astype(bf16)


def drift_call(parity, keep, sent, sg, fetched, first):
    rows, count = fetched[0].shape
    vm = pl.BlockSpec(memory_space=VM)
    smem = pl.BlockSpec(memory_space=pltpu.SMEM)
    shape = (rows // 2, count)
    return pl.pallas_call(
        functools.partial(drift_kernel, first),
        in_specs=[smem] + [vm] * (3 + len(fetched)),
        out_specs=[vm] * 3,
        out_shape=[
            jax.ShapeDtypeStruct(shape, f32),
            jax.ShapeDtypeStruct(shape, f32),
            jax.ShapeDtypeStruct(shape, bf16),
        ],
        compiler_params=params(6),
        name="drift",
    )(parity, keep, sent, sg, *fetched)


def finish_kernel(firsts, parity, x_start, *refs):
    n = len(firsts)
    given, rest = refs[: 5 * n], refs[-2 - n :]
    out, results, sem = rest[0], rest[1 : 1 + n], rest[1 + n]
    p = parity[0]
    odd = p.astype(f32)
    copies = []
    for i, first in enumerate(firsts):
        earlier, kept, fetched, other, back = given[5 * i : 5 * i + 5]
        half, count = kept.shape
        cols = slice(first, first + count)
        mine = pl.ds(pl.multiple_of(p * half, half), half)
        rest = pl.ds(pl.multiple_of((1 - p) * half, half), half)
        results[i][mine, :] = (
            x_start[mine, cols] + earlier[...] + kept[...] + odd * fetched[...].astype(f32)
        )
        results[i][rest, :] = x_start[rest, cols] + other[...] + back[...].astype(f32)
        copies.append(
            pltpu.make_async_copy(results[i], out.at[0, :, pl.ds(first, count)], sem.at[i])
        )
        copies[i].start()
    for copy in copies:
        copy.wait()


def finish_call(parity, x_start, groups, firsts, into):
    rows, width = x_start.shape
    vm = pl.BlockSpec(memory_space=VM)
    smem = pl.BlockSpec(memory_space=pltpu.SMEM)
    hbm = pl.BlockSpec(memory_space=pltpu.HBM)
    given = [parity, x_start] + [one for group in groups for one in group]
    return pl.pallas_call(
        functools.partial(finish_kernel, firsts),
        in_specs=[smem] + [vm] * (len(given) - 1) + [hbm] * len(into),
        out_specs=hbm,
        out_shape=jax.ShapeDtypeStruct((1, rows, width), f32),
        scratch_shapes=[VM((rows, group[1].shape[1]), f32) for group in groups]
        + [pltpu.SemaphoreType.DMA((len(groups),))],
        input_output_aliases={len(given): 0} if into else {},
        compiler_params=params(6),
        name="finish",
    )(*given, *into)


def per_device(
    n_step,
    n_seq,
    trajectory,
    x_start,
    t_idx,
    mod_table,
    step_sizes,
    q_gain,
    k_gain,
    w_qkv,
    w_mlp_in,
    w_out_attn,
    w_out_mlp,
):
    head = q_gain.shape[0]
    rows, width = x_start.shape
    chips = n_seq // 2
    groups = n_step // 2
    half = rows // 2
    unit = width // 24
    counts = [n * unit for n in (8, 7, 9)]
    chunks = len(counts)
    firsts = [sum(counts[:c]) for c in range(chunks)]
    qg, kg = q_gain[None, :], k_gain[None, :]

    def to_core(x):
        return lax.ppermute(x, "seq", [(i, i ^ 1) for i in range(n_seq)])

    def to_chip(x, offset):
        return lax.ppermute(x, "seq", [(i, (i + 2 * offset) % n_seq) for i in range(n_seq)])

    def to_pair(x):
        return lax.ppermute(x, "step", [(i, i ^ 1) for i in range(n_step)])

    def tied(*values):
        return lax.optimization_barrier(values)

    parity = lax.rem(lax.axis_index("step"), 2)
    even = (parity == 0).astype(f32)
    which = parity[None]
    offsets = range(1, chips)

    *mine, sg = norm_call(t_idx, trajectory, mod_table, step_sizes)
    far = [[to_chip(part, j) for part in mine] for j in offsets]
    given = mine + [to_core(part) for part in mine]
    q0, k0, v0, act0, low0, high0, *held = project_call(
        given, qg, kg, w_qkv, w_mlp_in, w_out_mlp, None
    )
    given = []
    for top, low in far:
        top, q0 = tied(top, q0)
        next_top = to_core(top)
        low, next_top = tied(low, next_top)
        given.append([top, low, next_top, to_core(low)])
    qs, ks, vs, acts = [], [k0], [v0], []
    for blocks in given:
        q, k, v, act = project_call(blocks, qg, kg, w_qkv, w_mlp_in, w_out_mlp, held)
        qs.append(q)
        ks.append(k)
        vs.append(v)
        acts.append(act)
    mixed = [attend_call(q, ks, vs, head) for q in qs]

    weights = [w_out_attn, w_out_mlp]
    got = [[] for _ in offsets]

    def jobs_of(c):
        return [([a, b], weights, [], firsts[c], counts[c]) for a, b in zip(mixed, acts)]

    def joined(parts, sent):
        return [join_call(keep, s) for (keep, _), s in zip(parts, sent)]

    def to_chips(ready):
        for j, one in enumerate(ready):
            got[j].append(to_chip(one, chips - 1 - j))

    parts = out_call(jobs_of(0))
    sent = [to_core(send) for _, send in parts]
    q0, parts = tied(q0, parts)
    mixed0 = attend_call(q0, ks, vs, head)
    mixed0, sent = tied(mixed0, sent)
    ready = joined(parts, sent)
    mixed, acts, mixed0, ready = tied(mixed, acts, mixed0, ready)
    to_chips(ready)
    jobs = [job for c in range(1, chunks) for job in jobs_of(c)]
    for c in range(chunks):
        jobs.append(([mixed0], [w_out_attn], [low0, high0], firsts[c], counts[c]))
    parts = out_call(jobs)
    sent = [to_core(send) for _, send in parts]
    keep = [part[0] for part in parts[-chunks:]]
    sent0 = sent[-chunks:]
    others = chips - 1
    first, keep, sent[:others] = tied([row[0] for row in got], keep, sent[:others])
    for row, one in zip(got, first):
        row[0] = one
    ready = joined(parts[:others], sent[:others])
    keep, ready = tied(keep, ready)
    to_chips(ready)
    for c in range(2, chunks):
        here = slice((c - 1) * others, c * others)
        to_chips(joined(parts[here], sent[here]))

    def along(pairs):
        return lambda x: lax.ppermute(x, "step", [(2 * a + i, 2 * b + i) for a, b in pairs for i in (0, 1)])

    group = lax.div(lax.axis_index("step"), 2)
    rounds = []
    span = 1
    while span < groups:
        pairs = [(b, b ^ span) for b in range(groups) if b ^ span < groups]
        rounds.append((span, along(pairs)))
        span *= 2

    def prefix_stages(c):
        held = {}

        def drift_of(fetched):
            drift = drift_call(which, keep[c], sent0[c], sg, fetched, firsts[c])
            held["kept"], held["other"], send = drift
            return send

        def pair_sum(fetched):
            held["fetched"] = fetched[0]
            held["total"] = held["kept"] + fetched[0].astype(f32)
            return held["total"].astype(bf16)

        def collect(r, fetched):
            one = fetched[0].astype(f32)
            upper = (lax.rem(lax.div(group, rounds[r][0]), 2) == 1).astype(f32)
            held["earlier"] = held["earlier"] + upper * one if r else upper * one
            if r == len(rounds) - 1:
                return (held["earlier"] + even * held["kept"]).astype(bf16)
            held["total"] = held["total"] + one
            return held["total"].astype(bf16)

        def finish(fetched):
            given = [held[name] for name in ("earlier", "kept", "fetched", "other")]
            stash.append((firsts[c], given + [fetched[0]]))
            if len(stash) in (1, chunks):
                mine = stash[len(stash) - 1 :] if len(stash) == 1 else stash[1:]
                places = [place for place, _ in mine]
                groups_in = [group for _, group in mine]
                into = list(written)
                written[:] = [finish_call(which, x_start, groups_in, places, into)]

        stages = [(drift_of, to_pair), (pair_sum, rounds[0][1])]
        for r in range(len(rounds)):
            move = to_pair if r == len(rounds) - 1 else rounds[r + 1][1]
            stages.append((functools.partial(collect, r), move))
        stages.append((finish, None))
        return stages

    plan = [prefix_stages(c) for c in range(chunks)]
    inbox = [[got[j][c] for j in range(chips - 1)] for c in range(chunks)]
    turns = []
    arrival = 2.0
    for c in range(chunks):
        share = 16.0 * (10 - 2 * c) / 24
        arrival += share
        when = arrival
        for i in range(len(plan[c])):
            turns.append((when, c, i))
            when += 2.2 + share * (1.0 if i == len(plan[c]) - 3 else 0.5)
    written, stash = [], []
    last = None
    for _, c, i in sorted(turns):
        compute, move = plan[c][i]
        if c == chunks - 1 and i == len(plan[c]) - 2:
            inbox[c], inbox[0] = tied(inbox[c], inbox[0])
        fetched = inbox[c]
        if last is not None:
            fetched, last = tied(fetched, last)
        out = compute(fetched)
        if move is not None:
            inbox[c] = [move(out)]
            last = out
    return written[0]


def solution(mesh):
    placed = (
        P("step", "seq", None),
        P("seq", None),
        P("step"),
        P(),
        P(),
        P(),
        P(),
        P(None, None, "seq"),
        P(None, "seq"),
        P("seq", None),
        P("seq", None),
    )
    return jax.shard_map(
        functools.partial(per_device, mesh.shape["step"], mesh.shape["seq"]),
        mesh=mesh,
        in_specs=placed,
        out_specs=P("step", "seq", None),
        check_vma=False,
    )
```

```python
import functools
import math

import jax
import jax.numpy as jnp
from jax import lax
from jax.experimental import pallas as pl
from jax.experimental.pallas import tpu as pltpu
from jax.sharding import PartitionSpec as P

eps = 1e-06
f32 = jnp.float32
bf16 = jnp.bfloat16
VM = pltpu.VMEM
MIB = 1024 * 1024


def params(mib):
    return pltpu.CompilerParams(vmem_limit_bytes=mib * MIB)


def cost(flops, moved):
    return pl.CostEstimate(flops=flops, transcendentals=0, bytes_accessed=moved)


def norm_kernel(t_ref, size_ref, x_hbm, mod_hbm, top_ref, low_ref, sg_ref, x_ref, mod_ref, sem):
    width = x_hbm.shape[-1]
    pieces = sem.shape[0] - 1
    block = x_hbm.shape[1] // pieces
    t = t_ref[0]
    mod_copy = pltpu.make_async_copy(mod_hbm.at[pl.ds(t, 1), :], mod_ref, sem.at[pieces])
    mod_copy.start()
    copies = []
    for i in range(pieces):
        here = pl.ds(i * block, block)
        copies.append(pltpu.make_async_copy(x_hbm.at[0, here, :], x_ref.at[here, :], sem.at[i]))
        copies[i].start()
    mod_copy.wait()
    shift = mod_ref[:, :width]
    scale = 1.0 + mod_ref[:, width : 2 * width]
    sg_ref[...] = size_ref[t] * mod_ref[:, 2 * width :]
    for i in range(pieces):
        copies[i].wait()
        here = slice(i * block, (i + 1) * block)
        x = x_ref[here, :]
        center = x - jnp.mean(x, axis=-1, keepdims=True)
        spread = jnp.mean(center * center, axis=-1, keepdims=True)
        m = (center * lax.rsqrt(spread + eps) * scale + shift).astype(bf16)
        if 2 * i < pieces:
            top_ref[here, :] = m
        else:
            at = i * block - top_ref.shape[0]
            low_ref[at : at + block, :] = m


def norm_call(t_idx, trajectory, mod_table, step_sizes):
    _, rows, width = trajectory.shape
    smem = pl.BlockSpec(memory_space=pltpu.SMEM)
    hbm = pl.BlockSpec(memory_space=pltpu.HBM)
    vm = pl.BlockSpec(memory_space=VM)
    return pl.pallas_call(
        norm_kernel,
        in_specs=[smem, smem, hbm, hbm],
        out_specs=[vm, vm, vm],
        out_shape=[
            jax.ShapeDtypeStruct((rows // 2, width), bf16),
            jax.ShapeDtypeStruct((rows // 2, width), bf16),
            jax.ShapeDtypeStruct((1, width), f32),
        ],
        scratch_shapes=[
            VM((rows, width), f32),
            VM((1, 3 * width), f32),
            pltpu.SemaphoreType.DMA((5,)),
        ],
        compiler_params=params(60),
        cost_estimate=cost(10 * rows * width, 0),
        name="norm",
    )(t_idx, step_sizes, trajectory, mod_table)


def project_kernel(tile, load, tiles, m0, m1, m2, m3, qg, kg, *refs):
    if load:
        wq_hbm, wm_hbm, wb_hbm, q, k, v, act, low, high = refs[:9]
        held, rows, wb, sem = refs[9:-3], refs[-3], refs[-2], refs[-1]
    else:
        held = refs[:tiles]
        q, k, v, act, rows = refs[tiles:]
    quarter = m0.shape[0]
    half = 2 * quarter
    head = qg.shape[1]
    n_q = q.shape[1] // tile
    copies = []
    if load:
        for i in range(tiles):
            if i < 3 * n_q:
                source = wq_hbm.at[i // n_q, :, pl.ds(i % n_q * tile, tile)]
            else:
                source = wm_hbm.at[:, pl.ds((i - 3 * n_q) * tile, tile)]
            copies.append(pltpu.make_async_copy(source, held[i], sem.at[i]))
            copies[i].start()
        span = low.shape[1] // (sem.shape[0] - tiles)
        for at in range(0, low.shape[1], span):
            here = (slice(None), pl.ds(at, span))
            copies.append(pltpu.make_async_copy(wb_hbm.at[here], wb.at[here], sem.at[len(copies)]))
            copies[-1].start()
    for i, m in enumerate((m0, m1, m2, m3)):
        rows[i * quarter : (i + 1) * quarter] = m[...]

    def normed(y, gain):
        parts = []
        for h in range(tile // head):
            one = y[:, h * head : (h + 1) * head]
            square = jnp.mean(one * one, axis=-1, keepdims=True)
            parts.append((one * lax.rsqrt(square + eps) * gain).astype(bf16))
        return jnp.concatenate(parts, axis=1)

    for i in range(tiles):
        if load:
            copies[i].wait()
        y = jnp.dot(rows[...], held[i][...], preferred_element_type=f32)
        cols = slice(i % n_q * tile, (i % n_q + 1) * tile)
        if i < n_q:
            q[:, cols] = normed(y, qg[...])
        elif i < 2 * n_q:
            k[:, cols] = normed(y, kg[...])
        elif i < 3 * n_q:
            v[:, cols] = y.astype(bf16)
        else:
            cols = slice((i - 3 * n_q) * tile, (i - 3 * n_q + 1) * tile)
            act[:, cols] = jax.nn.gelu(y, approximate=True).astype(bf16)
    if load:
        for i, copy in enumerate(copies[tiles:]):
            copy.wait()
            cols = slice(i * span, (i + 1) * span)
            y = jnp.dot(act[...], wb[:, cols], preferred_element_type=f32)
            low[:, cols] = y[:half]
            high[:, cols] = y[half:]


def project_call(given, q_gain, k_gain, w_qkv, w_mlp_in, w_out_mlp, held):
    half, width = 2 * given[0].shape[0], given[0].shape[1]
    heads = w_qkv.shape[2]
    hidden = w_mlp_in.shape[1]
    tile = min(512, heads)
    tiles = (3 * heads + hidden) // tile
    rows = 2 * half
    load = held is None
    vm = pl.BlockSpec(memory_space=VM)
    hbm = pl.BlockSpec(memory_space=pltpu.HBM)
    shapes = [jax.ShapeDtypeStruct((rows, heads), bf16)] * 3
    shapes.append(jax.ShapeDtypeStruct((rows, hidden), bf16))
    scratch = [VM((rows, width), bf16)]
    if load:
        shapes += [jax.ShapeDtypeStruct((half, width), f32)] * 2
        shapes += [jax.ShapeDtypeStruct((width, tile), bf16)] * tiles
        scratch.append(VM(w_out_mlp.shape, bf16))
        scratch.append(pltpu.SemaphoreType.DMA((tiles + 4,)))
    return pl.pallas_call(
        functools.partial(project_kernel, tile, load, tiles),
        in_specs=[vm] * 6 + ([hbm] * 3 if load else [vm] * tiles),
        out_specs=[vm] * len(shapes),
        out_shape=shapes,
        scratch_shapes=scratch,
        compiler_params=params(27 if load else 9),
        cost_estimate=cost(2 * rows * width * (3 * heads + hidden), 0),
        name="project",
    )(*given, q_gain, k_gain, *([w_qkv, w_mlp_in, w_out_mlp] if load else held))


def attend_kernel(pairs, head, *refs):
    q_ref = refs[0]
    k_refs = refs[1 : 1 + pairs]
    v_refs = refs[1 + pairs : 1 + 2 * pairs]
    out = refs[1 + 2 * pairs]
    scale = math.log2(math.e) / math.sqrt(head)
    heads = [slice(at, at + head) for at in range(0, q_ref.shape[1], head)]
    scores = [
        [
            lax.dot_general(
                q_ref[:, cols], k[:, cols], (((1,), (1,)), ((), ())), preferred_element_type=f32
            )
            for k in k_refs
        ]
        for cols in heads
    ]
    tops = [
        functools.reduce(jnp.maximum, [jnp.max(s, axis=-1, keepdims=True) for s in one])
        for one in scores
    ]
    weights = [[jnp.exp2((s - top) * scale) for s in one] for one, top in zip(scores, tops)]
    totals = [sum(jnp.sum(w, axis=-1, keepdims=True) for w in one) for one in weights]
    for cols, one, total in zip(heads, weights, totals):
        mixed = sum(
            jnp.dot(w.astype(bf16), v[:, cols], preferred_element_type=f32)
            for w, v in zip(one, v_refs)
        )
        out[:, cols] = (mixed / total).astype(bf16)


def attend_call(q, ks, vs, head):
    vm = pl.BlockSpec(memory_space=VM)
    return pl.pallas_call(
        functools.partial(attend_kernel, len(ks), head),
        in_specs=[vm] * (1 + 2 * len(ks)),
        out_specs=vm,
        out_shape=jax.ShapeDtypeStruct(q.shape, bf16),
        compiler_params=params(9),
        cost_estimate=cost(4 * len(ks) * q.shape[0] ** 2 * q.shape[1] * 3, 0),
        name="attend",
    )(q, *ks, *vs)


def out_kernel(jobs, *refs):
    outs = refs[len(refs) - 2 * len(jobs) :]
    at = 0
    for turn, (parts, extras, first, count) in enumerate(jobs):
        xs = refs[at : at + parts]
        ws = refs[at + parts : at + 2 * parts]
        extra = refs[at + 2 * parts : at + 2 * parts + extras]
        at += 2 * parts + extras
        keep, send = outs[2 * turn : 2 * turn + 2]
        half = keep.shape[0]
        cols = slice(first, first + count)
        terms = [
            jnp.dot(x[...], w[:, cols], preferred_element_type=f32) for x, w in zip(xs, ws)
        ]
        y = functools.reduce(jnp.add, terms)
        low, high = y[:half], y[half:]
        if extra:
            low = low + extra[0][:, cols]
            high = high + extra[1][:, cols]
        keep[...] = low
        send[...] = high.astype(bf16)


def out_call(jobs):
    vm = pl.BlockSpec(memory_space=VM)
    given, plan, shapes, flops = [], [], [], 0
    for xs, ws, extra, first, count in jobs:
        given += [*xs, *ws, *extra]
        plan.append((len(xs), len(extra), first, count))
        half = xs[0].shape[0] // 2
        shapes.append(jax.ShapeDtypeStruct((half, count), f32))
        shapes.append(jax.ShapeDtypeStruct((half, count), bf16))
        flops += 4 * half * count * sum(x.shape[1] for x in xs)
    outs = pl.pallas_call(
        functools.partial(out_kernel, plan),
        in_specs=[vm] * len(given),
        out_specs=[vm] * len(shapes),
        out_shape=shapes,
        compiler_params=params(9),
        cost_estimate=cost(flops, 0),
        name="project_out",
    )(*given)
    return [tuple(outs[i : i + 2]) for i in range(0, len(outs), 2)]


def join_kernel(keep, sent, out):
    out[...] = (keep[...] + sent[...].astype(f32)).astype(bf16)


def join_call(keep, sent):
    vm = pl.BlockSpec(memory_space=VM)
    return pl.pallas_call(
        join_kernel,
        in_specs=[vm, vm],
        out_specs=vm,
        out_shape=jax.ShapeDtypeStruct(keep.shape, bf16),
        compiler_params=params(6),
        name="join",
    )(keep, sent)


def drift_kernel(first, parity, keep, sent, sg, *refs):
    fetched, (kept, other, send) = refs[:-3], refs[-3:]
    half, count = kept.shape
    p = parity[0]

    def part(which):
        rows = pl.ds(pl.multiple_of(which * half, half), half)
        branch = keep[rows, :] + sent[rows, :].astype(f32)
        for one in fetched:
            branch = branch + one[rows, :].astype(f32)
        return sg[:, first : first + count] * branch

    kept[...] = part(p)
    passed = part(1 - p)
    other[...] = passed
    send[...] = passed.astype(bf16)


def drift_call(parity, keep, sent, sg, fetched, first):
    rows, count = fetched[0].shape
    vm = pl.BlockSpec(memory_space=VM)
    smem = pl.BlockSpec(memory_space=pltpu.SMEM)
    shape = (rows // 2, count)
    return pl.pallas_call(
        functools.partial(drift_kernel, first),
        in_specs=[smem] + [vm] * (3 + len(fetched)),
        out_specs=[vm] * 3,
        out_shape=[
            jax.ShapeDtypeStruct(shape, f32),
            jax.ShapeDtypeStruct(shape, f32),
            jax.ShapeDtypeStruct(shape, bf16),
        ],
        compiler_params=params(6),
        name="drift",
    )(parity, keep, sent, sg, *fetched)


def finish_kernel(firsts, parity, x_start, *refs):
    n = len(firsts)
    given, rest = refs[: 5 * n], refs[-2 - n :]
    out, results, sem = rest[0], rest[1 : 1 + n], rest[1 + n]
    p = parity[0]
    odd = p.astype(f32)
    copies = []
    for i, first in enumerate(firsts):
        earlier, kept, fetched, other, back = given[5 * i : 5 * i + 5]
        half, count = kept.shape
        cols = slice(first, first + count)
        mine = pl.ds(pl.multiple_of(p * half, half), half)
        rest = pl.ds(pl.multiple_of((1 - p) * half, half), half)
        results[i][mine, :] = (
            x_start[mine, cols] + earlier[...] + kept[...] + odd * fetched[...].astype(f32)
        )
        results[i][rest, :] = x_start[rest, cols] + other[...] + back[...].astype(f32)
        copies.append(
            pltpu.make_async_copy(results[i], out.at[0, :, pl.ds(first, count)], sem.at[i])
        )
        copies[i].start()
    for copy in copies:
        copy.wait()


def finish_call(parity, x_start, groups, firsts, into):
    rows, width = x_start.shape
    vm = pl.BlockSpec(memory_space=VM)
    smem = pl.BlockSpec(memory_space=pltpu.SMEM)
    hbm = pl.BlockSpec(memory_space=pltpu.HBM)
    given = [parity, x_start] + [one for group in groups for one in group]
    return pl.pallas_call(
        functools.partial(finish_kernel, firsts),
        in_specs=[smem] + [vm] * (len(given) - 1) + [hbm] * len(into),
        out_specs=hbm,
        out_shape=jax.ShapeDtypeStruct((1, rows, width), f32),
        scratch_shapes=[VM((rows, group[1].shape[1]), f32) for group in groups]
        + [pltpu.SemaphoreType.DMA((len(groups),))],
        input_output_aliases={len(given): 0} if into else {},
        compiler_params=params(6),
        name="finish",
    )(*given, *into)


def per_device(
    n_step,
    n_seq,
    trajectory,
    x_start,
    t_idx,
    mod_table,
    step_sizes,
    q_gain,
    k_gain,
    w_qkv,
    w_mlp_in,
    w_out_attn,
    w_out_mlp,
):
    head = q_gain.shape[0]
    rows, width = x_start.shape
    chips = n_seq // 2
    groups = n_step // 2
    half = rows // 2
    unit = width // 24
    counts = [n * unit for n in (7, 6, 6, 5)]
    chunks = len(counts)
    firsts = [sum(counts[:c]) for c in range(chunks)]
    qg, kg = q_gain[None, :], k_gain[None, :]

    def to_core(x):
        return lax.ppermute(x, "seq", [(i, i ^ 1) for i in range(n_seq)])

    def to_chip(x, offset):
        return lax.ppermute(x, "seq", [(i, (i + 2 * offset) % n_seq) for i in range(n_seq)])

    def to_pair(x):
        return lax.ppermute(x, "step", [(i, i ^ 1) for i in range(n_step)])

    def tied(*values):
        return lax.optimization_barrier(values)

    parity = lax.rem(lax.axis_index("step"), 2)
    even = (parity == 0).astype(f32)
    which = parity[None]
    offsets = range(1, chips)

    *mine, sg = norm_call(t_idx, trajectory, mod_table, step_sizes)
    far = [[to_chip(part, j) for part in mine] for j in offsets]
    given = mine + [to_core(part) for part in mine]
    q0, k0, v0, act0, low0, high0, *held = project_call(
        given, qg, kg, w_qkv, w_mlp_in, w_out_mlp, None
    )
    given = []
    for top, low in far:
        top, q0 = tied(top, q0)
        next_top = to_core(top)
        low, next_top = tied(low, next_top)
        given.append([top, low, next_top, to_core(low)])
    qs, ks, vs, acts = [], [k0], [v0], []
    for blocks in given:
        q, k, v, act = project_call(blocks, qg, kg, w_qkv, w_mlp_in, w_out_mlp, held)
        qs.append(q)
        ks.append(k)
        vs.append(v)
        acts.append(act)
    mixed = [attend_call(q, ks, vs, head) for q in qs]

    weights = [w_out_attn, w_out_mlp]
    got = [[] for _ in offsets]

    def jobs_of(c):
        return [([a, b], weights, [], firsts[c], counts[c]) for a, b in zip(mixed, acts)]

    def joined(parts, sent):
        return [join_call(keep, s) for (keep, _), s in zip(parts, sent)]

    def to_chips(ready):
        for j, one in enumerate(ready):
            got[j].append(to_chip(one, chips - 1 - j))

    parts = out_call(jobs_of(0))
    sent = [to_core(send) for _, send in parts]
    q0, parts = tied(q0, parts)
    mixed0 = attend_call(q0, ks, vs, head)
    mixed0, sent = tied(mixed0, sent)
    ready = joined(parts, sent)
    mixed, acts, mixed0, ready = tied(mixed, acts, mixed0, ready)
    to_chips(ready)
    jobs = [job for c in range(1, chunks) for job in jobs_of(c)]
    for c in range(chunks):
        jobs.append(([mixed0], [w_out_attn], [low0, high0], firsts[c], counts[c]))
    parts = out_call(jobs)
    sent = [to_core(send) for _, send in parts]
    keep = [part[0] for part in parts[-chunks:]]
    sent0 = sent[-chunks:]
    others = chips - 1
    first, keep, sent[:others] = tied([row[0] for row in got], keep, sent[:others])
    for row, one in zip(got, first):
        row[0] = one
    ready = joined(parts[:others], sent[:others])
    keep, ready = tied(keep, ready)
    to_chips(ready)
    for c in range(2, chunks):
        here = slice((c - 1) * others, c * others)
        sent[here], ready = tied(sent[here], ready)
        ready = joined(parts[here], sent[here])
        to_chips(ready)

    def along(pairs):
        return lambda x: lax.ppermute(x, "step", [(2 * a + i, 2 * b + i) for a, b in pairs for i in (0, 1)])

    group = lax.div(lax.axis_index("step"), 2)
    rounds = []
    span = 1
    while span < groups:
        pairs = [(b, b ^ span) for b in range(groups) if b ^ span < groups]
        rounds.append((span, along(pairs)))
        span *= 2

    def prefix_stages(c):
        held = {}

        def drift_of(fetched):
            drift = drift_call(which, keep[c], sent0[c], sg, fetched, firsts[c])
            held["kept"], held["other"], send = drift
            return send

        def pair_sum(fetched):
            held["fetched"] = fetched[0]
            held["total"] = held["kept"] + fetched[0].astype(f32)
            return held["total"].astype(bf16)

        def collect(r, fetched):
            one = fetched[0].astype(f32)
            upper = (lax.rem(lax.div(group, rounds[r][0]), 2) == 1).astype(f32)
            held["earlier"] = held["earlier"] + upper * one if r else upper * one
            if r == len(rounds) - 1:
                return (held["earlier"] + even * held["kept"]).astype(bf16)
            held["total"] = held["total"] + one
            return held["total"].astype(bf16)

        def finish(fetched):
            given = [held[name] for name in ("earlier", "kept", "fetched", "other")]
            stash.append((firsts[c], given + [fetched[0]]))
            if len(stash) != chunks - 1:
                mine = stash[-1:] if len(stash) < chunks else stash[-2:]
                places = [place for place, _ in mine]
                groups_in = [group for _, group in mine]
                into = list(written)
                written[:] = [finish_call(which, x_start, groups_in, places, into)]

        stages = [(drift_of, to_pair), (pair_sum, rounds[0][1])]
        for r in range(len(rounds)):
            move = to_pair if r == len(rounds) - 1 else rounds[r + 1][1]
            stages.append((functools.partial(collect, r), move))
        stages.append((finish, None))
        return stages

    plan = [prefix_stages(c) for c in range(chunks)]
    inbox = [[got[j][c] for j in range(chips - 1)] for c in range(chunks)]
    turns = []
    arrival = 2.0
    for c in range(chunks):
        share = 16.0 * counts[c] / width
        arrival += share
        when = arrival
        for i in range(len(plan[c])):
            turns.append((when, c, i))
            when += 2.2 + share * (1.0 if i == len(plan[c]) - 3 else 0.5)
    written, stash = [], []
    last = None
    for _, c, i in sorted(turns):
        compute, move = plan[c][i]
        fetched = inbox[c]
        if last is not None:
            fetched, last = tied(fetched, last)
        out = compute(fetched)
        if move is not None:
            inbox[c] = [move(out)]
            last = out
    return written[0]


def solution(mesh):
    placed = (
        P("step", "seq", None),
        P("seq", None),
        P("step"),
        P(),
        P(),
        P(),
        P(),
        P(None, None, "seq"),
        P(None, "seq"),
        P("seq", None),
        P("seq", None),
    )
    return jax.shard_map(
        functools.partial(per_device, mesh.shape["step"], mesh.shape["seq"]),
        mesh=mesh,
        in_specs=placed,
        out_specs=P("step", "seq", None),
        check_vma=False,
    )
```

```python
import functools
import math

import jax
import jax.numpy as jnp
from jax import lax
from jax.experimental import pallas as pl
from jax.experimental.pallas import tpu as pltpu
from jax.sharding import PartitionSpec as P

eps = 1e-06
f32 = jnp.float32
bf16 = jnp.bfloat16
VM = pltpu.VMEM
MIB = 1024 * 1024


def params(mib):
    return pltpu.CompilerParams(vmem_limit_bytes=mib * MIB)


def cost(flops, moved):
    return pl.CostEstimate(flops=flops, transcendentals=0, bytes_accessed=moved)


def norm_kernel(t_ref, size_ref, x_hbm, mod_hbm, top_ref, low_ref, sg_ref, x_ref, mod_ref, sem):
    width = x_hbm.shape[-1]
    pieces = sem.shape[0] - 1
    block = x_hbm.shape[1] // pieces
    t = t_ref[0]
    mod_copy = pltpu.make_async_copy(mod_hbm.at[pl.ds(t, 1), :], mod_ref, sem.at[pieces])
    mod_copy.start()
    copies = []
    for i in range(pieces):
        here = pl.ds(i * block, block)
        copies.append(pltpu.make_async_copy(x_hbm.at[0, here, :], x_ref.at[here, :], sem.at[i]))
        copies[i].start()
    mod_copy.wait()
    shift = mod_ref[:, :width]
    scale = 1.0 + mod_ref[:, width : 2 * width]
    sg_ref[...] = size_ref[t] * mod_ref[:, 2 * width :]
    for i in range(pieces):
        copies[i].wait()
        here = slice(i * block, (i + 1) * block)
        x = x_ref[here, :]
        center = x - jnp.mean(x, axis=-1, keepdims=True)
        spread = jnp.mean(center * center, axis=-1, keepdims=True)
        m = (center * lax.rsqrt(spread + eps) * scale + shift).astype(bf16)
        if 2 * i < pieces:
            top_ref[here, :] = m
        else:
            at = i * block - top_ref.shape[0]
            low_ref[at : at + block, :] = m


def norm_call(t_idx, trajectory, mod_table, step_sizes):
    _, rows, width = trajectory.shape
    smem = pl.BlockSpec(memory_space=pltpu.SMEM)
    hbm = pl.BlockSpec(memory_space=pltpu.HBM)
    vm = pl.BlockSpec(memory_space=VM)
    return pl.pallas_call(
        norm_kernel,
        in_specs=[smem, smem, hbm, hbm],
        out_specs=[vm, vm, vm],
        out_shape=[
            jax.ShapeDtypeStruct((rows // 2, width), bf16),
            jax.ShapeDtypeStruct((rows // 2, width), bf16),
            jax.ShapeDtypeStruct((1, width), f32),
        ],
        scratch_shapes=[
            VM((rows, width), f32),
            VM((1, 3 * width), f32),
            pltpu.SemaphoreType.DMA((5,)),
        ],
        compiler_params=params(60),
        cost_estimate=cost(10 * rows * width, 0),
        name="norm",
    )(t_idx, step_sizes, trajectory, mod_table)


def project_kernel(tile, load, tiles, m0, m1, m2, m3, qg, kg, *refs):
    if load:
        wq_hbm, wm_hbm, wb_hbm, q, k, v, act, low, high = refs[:9]
        held, rows, wb, sem = refs[9:-3], refs[-3], refs[-2], refs[-1]
    else:
        held = refs[:tiles]
        q, k, v, act, rows = refs[tiles:]
    quarter = m0.shape[0]
    half = 2 * quarter
    head = qg.shape[1]
    n_q = q.shape[1] // tile
    copies = []
    if load:
        for i in range(tiles):
            if i < 3 * n_q:
                source = wq_hbm.at[i // n_q, :, pl.ds(i % n_q * tile, tile)]
            else:
                source = wm_hbm.at[:, pl.ds((i - 3 * n_q) * tile, tile)]
            copies.append(pltpu.make_async_copy(source, held[i], sem.at[i]))
            copies[i].start()
        span = low.shape[1] // (sem.shape[0] - tiles)
        for at in range(0, low.shape[1], span):
            here = (slice(None), pl.ds(at, span))
            copies.append(pltpu.make_async_copy(wb_hbm.at[here], wb.at[here], sem.at[len(copies)]))
            copies[-1].start()
    for i, m in enumerate((m0, m1, m2, m3)):
        rows[i * quarter : (i + 1) * quarter] = m[...]

    def normed(y, gain):
        parts = []
        for h in range(tile // head):
            one = y[:, h * head : (h + 1) * head]
            square = jnp.mean(one * one, axis=-1, keepdims=True)
            parts.append((one * lax.rsqrt(square + eps) * gain).astype(bf16))
        return jnp.concatenate(parts, axis=1)

    for i in range(tiles):
        if load:
            copies[i].wait()
        y = jnp.dot(rows[...], held[i][...], preferred_element_type=f32)
        cols = slice(i % n_q * tile, (i % n_q + 1) * tile)
        if i < n_q:
            q[:, cols] = normed(y, qg[...])
        elif i < 2 * n_q:
            k[:, cols] = normed(y, kg[...])
        elif i < 3 * n_q:
            v[:, cols] = y.astype(bf16)
        else:
            cols = slice((i - 3 * n_q) * tile, (i - 3 * n_q + 1) * tile)
            act[:, cols] = jax.nn.gelu(y, approximate=True).astype(bf16)
    if load:
        for i, copy in enumerate(copies[tiles:]):
            copy.wait()
            cols = slice(i * span, (i + 1) * span)
            y = jnp.dot(act[...], wb[:, cols], preferred_element_type=f32)
            low[:, cols] = y[:half]
            high[:, cols] = y[half:]


def project_call(given, q_gain, k_gain, w_qkv, w_mlp_in, w_out_mlp, held):
    half, width = 2 * given[0].shape[0], given[0].shape[1]
    heads = w_qkv.shape[2]
    hidden = w_mlp_in.shape[1]
    tile = min(512, heads)
    tiles = (3 * heads + hidden) // tile
    rows = 2 * half
    load = held is None
    vm = pl.BlockSpec(memory_space=VM)
    hbm = pl.BlockSpec(memory_space=pltpu.HBM)
    shapes = [jax.ShapeDtypeStruct((rows, heads), bf16)] * 3
    shapes.append(jax.ShapeDtypeStruct((rows, hidden), bf16))
    scratch = [VM((rows, width), bf16)]
    if load:
        shapes += [jax.ShapeDtypeStruct((half, width), f32)] * 2
        shapes += [jax.ShapeDtypeStruct((width, tile), bf16)] * tiles
        scratch.append(VM(w_out_mlp.shape, bf16))
        scratch.append(pltpu.SemaphoreType.DMA((tiles + 4,)))
    return pl.pallas_call(
        functools.partial(project_kernel, tile, load, tiles),
        in_specs=[vm] * 6 + ([hbm] * 3 if load else [vm] * tiles),
        out_specs=[vm] * len(shapes),
        out_shape=shapes,
        scratch_shapes=scratch,
        compiler_params=params(27 if load else 9),
        cost_estimate=cost(2 * rows * width * (3 * heads + hidden), 0),
        name="project",
    )(*given, q_gain, k_gain, *([w_qkv, w_mlp_in, w_out_mlp] if load else held))


def attend_kernel(pairs, head, *refs):
    q_ref = refs[0]
    k_refs = refs[1 : 1 + pairs]
    v_refs = refs[1 + pairs : 1 + 2 * pairs]
    out = refs[1 + 2 * pairs]
    scale = math.log2(math.e) / math.sqrt(head)
    heads = [slice(at, at + head) for at in range(0, q_ref.shape[1], head)]
    scores = [
        [
            lax.dot_general(
                q_ref[:, cols], k[:, cols], (((1,), (1,)), ((), ())), preferred_element_type=f32
            )
            for k in k_refs
        ]
        for cols in heads
    ]
    tops = [
        functools.reduce(jnp.maximum, [jnp.max(s, axis=-1, keepdims=True) for s in one])
        for one in scores
    ]
    weights = [[jnp.exp2((s - top) * scale) for s in one] for one, top in zip(scores, tops)]
    totals = [sum(jnp.sum(w, axis=-1, keepdims=True) for w in one) for one in weights]
    for cols, one, total in zip(heads, weights, totals):
        mixed = sum(
            jnp.dot(w.astype(bf16), v[:, cols], preferred_element_type=f32)
            for w, v in zip(one, v_refs)
        )
        out[:, cols] = (mixed / total).astype(bf16)


def attend_call(q, ks, vs, head):
    vm = pl.BlockSpec(memory_space=VM)
    return pl.pallas_call(
        functools.partial(attend_kernel, len(ks), head),
        in_specs=[vm] * (1 + 2 * len(ks)),
        out_specs=vm,
        out_shape=jax.ShapeDtypeStruct(q.shape, bf16),
        compiler_params=params(9),
        cost_estimate=cost(4 * len(ks) * q.shape[0] ** 2 * q.shape[1] * 3, 0),
        name="attend",
    )(q, *ks, *vs)


def out_kernel(jobs, *refs):
    outs = refs[len(refs) - 2 * len(jobs) :]
    at = 0
    for turn, (parts, extras, first, count) in enumerate(jobs):
        xs = refs[at : at + parts]
        ws = refs[at + parts : at + 2 * parts]
        extra = refs[at + 2 * parts : at + 2 * parts + extras]
        at += 2 * parts + extras
        keep, send = outs[2 * turn : 2 * turn + 2]
        half = keep.shape[0]
        cols = slice(first, first + count)
        terms = [
            jnp.dot(x[...], w[:, cols], preferred_element_type=f32) for x, w in zip(xs, ws)
        ]
        y = functools.reduce(jnp.add, terms)
        low, high = y[:half], y[half:]
        if extra:
            low = low + extra[0][:, cols]
            high = high + extra[1][:, cols]
        keep[...] = low
        send[...] = high.astype(bf16)


def out_call(jobs):
    vm = pl.BlockSpec(memory_space=VM)
    given, plan, shapes, flops = [], [], [], 0
    for xs, ws, extra, first, count in jobs:
        given += [*xs, *ws, *extra]
        plan.append((len(xs), len(extra), first, count))
        half = xs[0].shape[0] // 2
        shapes.append(jax.ShapeDtypeStruct((half, count), f32))
        shapes.append(jax.ShapeDtypeStruct((half, count), bf16))
        flops += 4 * half * count * sum(x.shape[1] for x in xs)
    outs = pl.pallas_call(
        functools.partial(out_kernel, plan),
        in_specs=[vm] * len(given),
        out_specs=[vm] * len(shapes),
        out_shape=shapes,
        compiler_params=params(9),
        cost_estimate=cost(flops, 0),
        name="project_out",
    )(*given)
    return [tuple(outs[i : i + 2]) for i in range(0, len(outs), 2)]


def join_kernel(keep, sent, out):
    out[...] = (keep[...] + sent[...].astype(f32)).astype(bf16)


def join_call(keep, sent):
    vm = pl.BlockSpec(memory_space=VM)
    return pl.pallas_call(
        join_kernel,
        in_specs=[vm, vm],
        out_specs=vm,
        out_shape=jax.ShapeDtypeStruct(keep.shape, bf16),
        compiler_params=params(6),
        name="join",
    )(keep, sent)


def drift_kernel(first, parity, keep, sent, sg, *refs):
    fetched, (kept, other, send) = refs[:-3], refs[-3:]
    half, count = kept.shape
    p = parity[0]

    def part(which):
        rows = pl.ds(pl.multiple_of(which * half, half), half)
        branch = keep[rows, :] + sent[rows, :].astype(f32)
        for one in fetched:
            branch = branch + one[rows, :].astype(f32)
        return sg[:, first : first + count] * branch

    kept[...] = part(p)
    passed = part(1 - p)
    other[...] = passed
    send[...] = passed.astype(bf16)


def drift_call(parity, keep, sent, sg, fetched, first):
    rows, count = fetched[0].shape
    vm = pl.BlockSpec(memory_space=VM)
    smem = pl.BlockSpec(memory_space=pltpu.SMEM)
    shape = (rows // 2, count)
    return pl.pallas_call(
        functools.partial(drift_kernel, first),
        in_specs=[smem] + [vm] * (3 + len(fetched)),
        out_specs=[vm] * 3,
        out_shape=[
            jax.ShapeDtypeStruct(shape, f32),
            jax.ShapeDtypeStruct(shape, f32),
            jax.ShapeDtypeStruct(shape, bf16),
        ],
        compiler_params=params(6),
        name="drift",
    )(parity, keep, sent, sg, *fetched)


def finish_kernel(firsts, parity, x_start, *refs):
    n = len(firsts)
    given, rest = refs[: 5 * n], refs[-2 - n :]
    out, results, sem = rest[0], rest[1 : 1 + n], rest[1 + n]
    p = parity[0]
    odd = p.astype(f32)
    copies = []
    for i, first in enumerate(firsts):
        earlier, kept, fetched, other, back = given[5 * i : 5 * i + 5]
        half, count = kept.shape
        cols = slice(first, first + count)
        mine = pl.ds(pl.multiple_of(p * half, half), half)
        rest = pl.ds(pl.multiple_of((1 - p) * half, half), half)
        results[i][mine, :] = (
            x_start[mine, cols] + earlier[...] + kept[...] + odd * fetched[...].astype(f32)
        )
        results[i][rest, :] = x_start[rest, cols] + other[...] + back[...].astype(f32)
        copies.append(
            pltpu.make_async_copy(results[i], out.at[0, :, pl.ds(first, count)], sem.at[i])
        )
        copies[i].start()
    for copy in copies:
        copy.wait()


def finish_call(parity, x_start, groups, firsts, into):
    rows, width = x_start.shape
    vm = pl.BlockSpec(memory_space=VM)
    smem = pl.BlockSpec(memory_space=pltpu.SMEM)
    hbm = pl.BlockSpec(memory_space=pltpu.HBM)
    given = [parity, x_start] + [one for group in groups for one in group]
    return pl.pallas_call(
        functools.partial(finish_kernel, firsts),
        in_specs=[smem] + [vm] * (len(given) - 1) + [hbm] * len(into),
        out_specs=hbm,
        out_shape=jax.ShapeDtypeStruct((1, rows, width), f32),
        scratch_shapes=[VM((rows, group[1].shape[1]), f32) for group in groups]
        + [pltpu.SemaphoreType.DMA((len(groups),))],
        input_output_aliases={len(given): 0} if into else {},
        compiler_params=params(6),
        name="finish",
    )(*given, *into)


def per_device(
    n_step,
    n_seq,
    trajectory,
    x_start,
    t_idx,
    mod_table,
    step_sizes,
    q_gain,
    k_gain,
    w_qkv,
    w_mlp_in,
    w_out_attn,
    w_out_mlp,
):
    head = q_gain.shape[0]
    rows, width = x_start.shape
    chips = n_seq // 2
    groups = n_step // 2
    half = rows // 2
    unit = width // 24
    counts = [n * unit for n in (7, 6, 6, 5)]
    chunks = len(counts)
    firsts = [sum(counts[:c]) for c in range(chunks)]
    qg, kg = q_gain[None, :], k_gain[None, :]

    def to_core(x):
        return lax.ppermute(x, "seq", [(i, i ^ 1) for i in range(n_seq)])

    def to_chip(x, offset):
        return lax.ppermute(x, "seq", [(i, (i + 2 * offset) % n_seq) for i in range(n_seq)])

    def to_pair(x):
        return lax.ppermute(x, "step", [(i, i ^ 1) for i in range(n_step)])

    def tied(*values):
        return lax.optimization_barrier(values)

    parity = lax.rem(lax.axis_index("step"), 2)
    even = (parity == 0).astype(f32)
    which = parity[None]
    offsets = range(1, chips)

    *mine, sg = norm_call(t_idx, trajectory, mod_table, step_sizes)
    far = [[to_chip(part, j) for part in mine] for j in offsets]
    given = mine + [to_core(part) for part in mine]
    q0, k0, v0, act0, low0, high0, *held = project_call(
        given, qg, kg, w_qkv, w_mlp_in, w_out_mlp, None
    )
    given = []
    for top, low in far:
        top, q0 = tied(top, q0)
        next_top = to_core(top)
        low, next_top = tied(low, next_top)
        given.append([top, low, next_top, to_core(low)])
    qs, ks, vs, acts = [], [k0], [v0], []
    for blocks in given:
        q, k, v, act = project_call(blocks, qg, kg, w_qkv, w_mlp_in, w_out_mlp, held)
        qs.append(q)
        ks.append(k)
        vs.append(v)
        acts.append(act)
    mixed = [attend_call(q, ks, vs, head) for q in qs]

    weights = [w_out_attn, w_out_mlp]
    got = [[] for _ in offsets]

    def jobs_of(c):
        return [([a, b], weights, [], firsts[c], counts[c]) for a, b in zip(mixed, acts)]

    def joined(parts, sent):
        return [join_call(keep, s) for (keep, _), s in zip(parts, sent)]

    def to_chips(ready):
        for j, one in enumerate(ready):
            got[j].append(to_chip(one, chips - 1 - j))

    parts = out_call(jobs_of(0))
    sent = [to_core(send) for _, send in parts]
    q0, parts = tied(q0, parts)
    mixed0 = attend_call(q0, ks, vs, head)
    mixed0, sent = tied(mixed0, sent)
    ready = joined(parts, sent)
    mixed, acts, mixed0, ready = tied(mixed, acts, mixed0, ready)
    to_chips(ready)
    jobs = [job for c in range(1, chunks) for job in jobs_of(c)]
    for c in range(chunks):
        jobs.append(([mixed0], [w_out_attn], [low0, high0], firsts[c], counts[c]))
    parts = out_call(jobs)
    sent = [to_core(send) for _, send in parts]
    keep = [part[0] for part in parts[-chunks:]]
    sent0 = sent[-chunks:]
    others = chips - 1
    first, keep, sent[:others] = tied([row[0] for row in got], keep, sent[:others])
    for row, one in zip(got, first):
        row[0] = one
    ready = joined(parts[:others], sent[:others])
    keep, ready = tied(keep, ready)
    to_chips(ready)
    for c in range(2, chunks):
        here = slice((c - 1) * others, c * others)
        sent[here], ready = tied(sent[here], ready)
        ready = joined(parts[here], sent[here])
        to_chips(ready)

    def along(pairs):
        return lambda x: lax.ppermute(x, "step", [(2 * a + i, 2 * b + i) for a, b in pairs for i in (0, 1)])

    group = lax.div(lax.axis_index("step"), 2)
    rounds = []
    span = 1
    while span < groups:
        pairs = [(b, b ^ span) for b in range(groups) if b ^ span < groups]
        rounds.append((span, along(pairs)))
        span *= 2

    def prefix_stages(c):
        held = {}

        def drift_of(fetched):
            drift = drift_call(which, keep[c], sent0[c], sg, fetched, firsts[c])
            held["kept"], held["other"], send = drift
            return send

        def pair_sum(fetched):
            held["fetched"] = fetched[0]
            held["total"] = held["kept"] + fetched[0].astype(f32)
            return held["total"].astype(bf16)

        def collect(r, fetched):
            one = fetched[0].astype(f32)
            upper = (lax.rem(lax.div(group, rounds[r][0]), 2) == 1).astype(f32)
            held["earlier"] = held["earlier"] + upper * one if r else upper * one
            if r == len(rounds) - 1:
                return (held["earlier"] + even * held["kept"]).astype(bf16)
            held["total"] = held["total"] + one
            return held["total"].astype(bf16)

        def finish(fetched):
            given = [held[name] for name in ("earlier", "kept", "fetched", "other")]
            stash.append((firsts[c], given + [fetched[0]]))
            if len(stash) == chunks:
                mine = stash
                places = [place for place, _ in mine]
                groups_in = [group for _, group in mine]
                into = list(written)
                written[:] = [finish_call(which, x_start, groups_in, places, into)]

        stages = [(drift_of, to_pair), (pair_sum, rounds[0][1])]
        for r in range(len(rounds)):
            move = to_pair if r == len(rounds) - 1 else rounds[r + 1][1]
            stages.append((functools.partial(collect, r), move))
        stages.append((finish, None))
        return stages

    plan = [prefix_stages(c) for c in range(chunks)]
    inbox = [[got[j][c] for j in range(chips - 1)] for c in range(chunks)]
    turns = []
    arrival = 2.0
    for c in range(chunks):
        share = 16.0 * counts[c] / width
        arrival += share
        when = arrival
        for i in range(len(plan[c])):
            turns.append((when, c, i))
            when += 2.2 + share * (1.0 if i == len(plan[c]) - 3 else 0.5)
    written, stash = [], []
    last = None
    order = [(c, i) for _, c, i in sorted(turns)]
    order.remove((0, 2))
    order.insert(order.index((2, 0)), (0, 2))
    for c, i in order:
        compute, move = plan[c][i]
        fetched = inbox[c]
        if last is not None:
            fetched, last = tied(fetched, last)
        out = compute(fetched)
        if move is not None:
            inbox[c] = [move(out)]
            last = out
    return written[0]


def solution(mesh):
    placed = (
        P("step", "seq", None),
        P("seq", None),
        P("step"),
        P(),
        P(),
        P(),
        P(),
        P(None, None, "seq"),
        P(None, "seq"),
        P("seq", None),
        P("seq", None),
    )
    return jax.shard_map(
        functools.partial(per_device, mesh.shape["step"], mesh.shape["seq"]),
        mesh=mesh,
        in_specs=placed,
        out_specs=P("step", "seq", None),
        check_vma=False,
    )
```

```python
import functools
import math

import jax
import jax.numpy as jnp
from jax import lax
from jax.experimental import pallas as pl
from jax.experimental.pallas import tpu as pltpu
from jax.sharding import PartitionSpec as P

eps = 1e-06
f32 = jnp.float32
bf16 = jnp.bfloat16
VM = pltpu.VMEM
MIB = 1024 * 1024


def params(mib):
    return pltpu.CompilerParams(vmem_limit_bytes=mib * MIB)


def cost(flops, moved):
    return pl.CostEstimate(flops=flops, transcendentals=0, bytes_accessed=moved)


def norm_kernel(t_ref, size_ref, x_hbm, mod_hbm, top_ref, low_ref, sg_ref, x_ref, mod_ref, sem):
    width = x_hbm.shape[-1]
    pieces = sem.shape[0] - 1
    block = x_hbm.shape[1] // pieces
    t = t_ref[0]
    mod_copy = pltpu.make_async_copy(mod_hbm.at[pl.ds(t, 1), :], mod_ref, sem.at[pieces])
    mod_copy.start()
    copies = []
    for i in range(pieces):
        here = pl.ds(i * block, block)
        copies.append(pltpu.make_async_copy(x_hbm.at[0, here, :], x_ref.at[here, :], sem.at[i]))
        copies[i].start()
    mod_copy.wait()
    shift = mod_ref[:, :width]
    scale = 1.0 + mod_ref[:, width : 2 * width]
    sg_ref[...] = size_ref[t] * mod_ref[:, 2 * width :]
    for i in range(pieces):
        copies[i].wait()
        here = slice(i * block, (i + 1) * block)
        x = x_ref[here, :]
        center = x - jnp.mean(x, axis=-1, keepdims=True)
        spread = jnp.mean(center * center, axis=-1, keepdims=True)
        m = (center * lax.rsqrt(spread + eps) * scale + shift).astype(bf16)
        if 2 * i < pieces:
            top_ref[here, :] = m
        else:
            at = i * block - top_ref.shape[0]
            low_ref[at : at + block, :] = m


def norm_call(t_idx, trajectory, mod_table, step_sizes):
    _, rows, width = trajectory.shape
    smem = pl.BlockSpec(memory_space=pltpu.SMEM)
    hbm = pl.BlockSpec(memory_space=pltpu.HBM)
    vm = pl.BlockSpec(memory_space=VM)
    return pl.pallas_call(
        norm_kernel,
        in_specs=[smem, smem, hbm, hbm],
        out_specs=[vm, vm, vm],
        out_shape=[
            jax.ShapeDtypeStruct((rows // 2, width), bf16),
            jax.ShapeDtypeStruct((rows // 2, width), bf16),
            jax.ShapeDtypeStruct((1, width), f32),
        ],
        scratch_shapes=[
            VM((rows, width), f32),
            VM((1, 3 * width), f32),
            pltpu.SemaphoreType.DMA((5,)),
        ],
        compiler_params=params(60),
        cost_estimate=cost(10 * rows * width, 0),
        name="norm",
    )(t_idx, step_sizes, trajectory, mod_table)


def project_kernel(tile, load, tiles, m0, m1, m2, m3, qg, kg, *refs):
    if load:
        wq_hbm, wm_hbm, wb_hbm, q, k, v, act, low, high = refs[:9]
        held, rows, wb, sem = refs[9:-3], refs[-3], refs[-2], refs[-1]
    else:
        held = refs[:tiles]
        q, k, v, act, rows = refs[tiles:]
    quarter = m0.shape[0]
    half = 2 * quarter
    head = qg.shape[1]
    n_q = q.shape[1] // tile
    copies = []
    if load:
        for i in range(tiles):
            if i < 3 * n_q:
                source = wq_hbm.at[i // n_q, :, pl.ds(i % n_q * tile, tile)]
            else:
                source = wm_hbm.at[:, pl.ds((i - 3 * n_q) * tile, tile)]
            copies.append(pltpu.make_async_copy(source, held[i], sem.at[i]))
            copies[i].start()
        span = low.shape[1] // (sem.shape[0] - tiles)
        for at in range(0, low.shape[1], span):
            here = (slice(None), pl.ds(at, span))
            copies.append(pltpu.make_async_copy(wb_hbm.at[here], wb.at[here], sem.at[len(copies)]))
            copies[-1].start()
    for i, m in enumerate((m0, m1, m2, m3)):
        rows[i * quarter : (i + 1) * quarter] = m[...]

    def normed(y, gain):
        parts = []
        for h in range(tile // head):
            one = y[:, h * head : (h + 1) * head]
            square = jnp.mean(one * one, axis=-1, keepdims=True)
            parts.append((one * lax.rsqrt(square + eps) * gain).astype(bf16))
        return jnp.concatenate(parts, axis=1)

    for i in range(tiles):
        if load:
            copies[i].wait()
        y = jnp.dot(rows[...], held[i][...], preferred_element_type=f32)
        cols = slice(i % n_q * tile, (i % n_q + 1) * tile)
        if i < n_q:
            q[:, cols] = normed(y, qg[...])
        elif i < 2 * n_q:
            k[:, cols] = normed(y, kg[...])
        elif i < 3 * n_q:
            v[:, cols] = y.astype(bf16)
        else:
            cols = slice((i - 3 * n_q) * tile, (i - 3 * n_q + 1) * tile)
            act[:, cols] = jax.nn.gelu(y, approximate=True).astype(bf16)
    if load:
        for i, copy in enumerate(copies[tiles:]):
            copy.wait()
            cols = slice(i * span, (i + 1) * span)
            y = jnp.dot(act[...], wb[:, cols], preferred_element_type=f32)
            low[:, cols] = y[:half]
            high[:, cols] = y[half:]


def project_call(given, q_gain, k_gain, w_qkv, w_mlp_in, w_out_mlp, held):
    half, width = 2 * given[0].shape[0], given[0].shape[1]
    heads = w_qkv.shape[2]
    hidden = w_mlp_in.shape[1]
    tile = min(512, heads)
    tiles = (3 * heads + hidden) // tile
    rows = 2 * half
    load = held is None
    vm = pl.BlockSpec(memory_space=VM)
    hbm = pl.BlockSpec(memory_space=pltpu.HBM)
    shapes = [jax.ShapeDtypeStruct((rows, heads), bf16)] * 3
    shapes.append(jax.ShapeDtypeStruct((rows, hidden), bf16))
    scratch = [VM((rows, width), bf16)]
    if load:
        shapes += [jax.ShapeDtypeStruct((half, width), f32)] * 2
        shapes += [jax.ShapeDtypeStruct((width, tile), bf16)] * tiles
        scratch.append(VM(w_out_mlp.shape, bf16))
        scratch.append(pltpu.SemaphoreType.DMA((tiles + 4,)))
    return pl.pallas_call(
        functools.partial(project_kernel, tile, load, tiles),
        in_specs=[vm] * 6 + ([hbm] * 3 if load else [vm] * tiles),
        out_specs=[vm] * len(shapes),
        out_shape=shapes,
        scratch_shapes=scratch,
        compiler_params=params(27 if load else 9),
        cost_estimate=cost(2 * rows * width * (3 * heads + hidden), 0),
        name="project",
    )(*given, q_gain, k_gain, *([w_qkv, w_mlp_in, w_out_mlp] if load else held))


def attend_kernel(pairs, head, *refs):
    q_ref = refs[0]
    k_refs = refs[1 : 1 + pairs]
    v_refs = refs[1 + pairs : 1 + 2 * pairs]
    out = refs[1 + 2 * pairs]
    scale = math.log2(math.e) / math.sqrt(head)
    heads = [slice(at, at + head) for at in range(0, q_ref.shape[1], head)]
    scores = [
        [
            lax.dot_general(
                q_ref[:, cols], k[:, cols], (((1,), (1,)), ((), ())), preferred_element_type=f32
            )
            for k in k_refs
        ]
        for cols in heads
    ]
    tops = [
        functools.reduce(jnp.maximum, [jnp.max(s, axis=-1, keepdims=True) for s in one])
        for one in scores
    ]
    weights = [[jnp.exp2((s - top) * scale) for s in one] for one, top in zip(scores, tops)]
    totals = [sum(jnp.sum(w, axis=-1, keepdims=True) for w in one) for one in weights]
    for cols, one, total in zip(heads, weights, totals):
        mixed = sum(
            jnp.dot(w.astype(bf16), v[:, cols], preferred_element_type=f32)
            for w, v in zip(one, v_refs)
        )
        out[:, cols] = (mixed / total).astype(bf16)


def attend_call(q, ks, vs, head):
    vm = pl.BlockSpec(memory_space=VM)
    return pl.pallas_call(
        functools.partial(attend_kernel, len(ks), head),
        in_specs=[vm] * (1 + 2 * len(ks)),
        out_specs=vm,
        out_shape=jax.ShapeDtypeStruct(q.shape, bf16),
        compiler_params=params(9),
        cost_estimate=cost(4 * len(ks) * q.shape[0] ** 2 * q.shape[1] * 3, 0),
        name="attend",
    )(q, *ks, *vs)


def out_kernel(jobs, *refs):
    outs = refs[len(refs) - 2 * len(jobs) :]
    at = 0
    for turn, (parts, extras, first, count) in enumerate(jobs):
        xs = refs[at : at + parts]
        ws = refs[at + parts : at + 2 * parts]
        extra = refs[at + 2 * parts : at + 2 * parts + extras]
        at += 2 * parts + extras
        keep, send = outs[2 * turn : 2 * turn + 2]
        half = keep.shape[0]
        cols = slice(first, first + count)
        terms = [
            jnp.dot(x[...], w[:, cols], preferred_element_type=f32) for x, w in zip(xs, ws)
        ]
        y = functools.reduce(jnp.add, terms)
        low, high = y[:half], y[half:]
        if extra:
            low = low + extra[0][:, cols]
            high = high + extra[1][:, cols]
        keep[...] = low
        send[...] = high.astype(bf16)


def out_call(jobs):
    vm = pl.BlockSpec(memory_space=VM)
    given, plan, shapes, flops = [], [], [], 0
    for xs, ws, extra, first, count in jobs:
        given += [*xs, *ws, *extra]
        plan.append((len(xs), len(extra), first, count))
        half = xs[0].shape[0] // 2
        shapes.append(jax.ShapeDtypeStruct((half, count), f32))
        shapes.append(jax.ShapeDtypeStruct((half, count), bf16))
        flops += 4 * half * count * sum(x.shape[1] for x in xs)
    outs = pl.pallas_call(
        functools.partial(out_kernel, plan),
        in_specs=[vm] * len(given),
        out_specs=[vm] * len(shapes),
        out_shape=shapes,
        compiler_params=params(9),
        cost_estimate=cost(flops, 0),
        name="project_out",
    )(*given)
    return [tuple(outs[i : i + 2]) for i in range(0, len(outs), 2)]


def join_kernel(keep, sent, out):
    out[...] = (keep[...] + sent[...].astype(f32)).astype(bf16)


def join_call(keep, sent):
    vm = pl.BlockSpec(memory_space=VM)
    return pl.pallas_call(
        join_kernel,
        in_specs=[vm, vm],
        out_specs=vm,
        out_shape=jax.ShapeDtypeStruct(keep.shape, bf16),
        compiler_params=params(6),
        name="join",
    )(keep, sent)


def drift_kernel(first, parity, keep, sent, sg, *refs):
    fetched, (kept, other, send) = refs[:-3], refs[-3:]
    half, count = kept.shape
    p = parity[0]

    def part(which):
        rows = pl.ds(pl.multiple_of(which * half, half), half)
        branch = keep[rows, :] + sent[rows, :].astype(f32)
        for one in fetched:
            branch = branch + one[rows, :].astype(f32)
        return sg[:, first : first + count] * branch

    kept[...] = part(p)
    passed = part(1 - p)
    other[...] = passed
    send[...] = passed.astype(bf16)


def drift_call(parity, keep, sent, sg, fetched, first):
    rows, count = fetched[0].shape
    vm = pl.BlockSpec(memory_space=VM)
    smem = pl.BlockSpec(memory_space=pltpu.SMEM)
    shape = (rows // 2, count)
    return pl.pallas_call(
        functools.partial(drift_kernel, first),
        in_specs=[smem] + [vm] * (3 + len(fetched)),
        out_specs=[vm] * 3,
        out_shape=[
            jax.ShapeDtypeStruct(shape, f32),
            jax.ShapeDtypeStruct(shape, f32),
            jax.ShapeDtypeStruct(shape, bf16),
        ],
        compiler_params=params(6),
        name="drift",
    )(parity, keep, sent, sg, *fetched)


def finish_kernel(firsts, parity, x_start, *refs):
    n = len(firsts)
    given, rest = refs[: 5 * n], refs[-2 - n :]
    out, results, sem = rest[0], rest[1 : 1 + n], rest[1 + n]
    p = parity[0]
    odd = p.astype(f32)
    copies = []
    for i, first in enumerate(firsts):
        earlier, kept, fetched, other, back = given[5 * i : 5 * i + 5]
        half, count = kept.shape
        cols = slice(first, first + count)
        mine = pl.ds(pl.multiple_of(p * half, half), half)
        rest = pl.ds(pl.multiple_of((1 - p) * half, half), half)
        results[i][mine, :] = (
            x_start[mine, cols] + earlier[...] + kept[...] + odd * fetched[...].astype(f32)
        )
        results[i][rest, :] = x_start[rest, cols] + other[...] + back[...].astype(f32)
        copies.append(
            pltpu.make_async_copy(results[i], out.at[0, :, pl.ds(first, count)], sem.at[i])
        )
        copies[i].start()
    for copy in copies:
        copy.wait()


def finish_call(parity, x_start, groups, firsts, into):
    rows, width = x_start.shape
    vm = pl.BlockSpec(memory_space=VM)
    smem = pl.BlockSpec(memory_space=pltpu.SMEM)
    hbm = pl.BlockSpec(memory_space=pltpu.HBM)
    given = [parity, x_start] + [one for group in groups for one in group]
    return pl.pallas_call(
        functools.partial(finish_kernel, firsts),
        in_specs=[smem] + [vm] * (len(given) - 1) + [hbm] * len(into),
        out_specs=hbm,
        out_shape=jax.ShapeDtypeStruct((1, rows, width), f32),
        scratch_shapes=[VM((rows, group[1].shape[1]), f32) for group in groups]
        + [pltpu.SemaphoreType.DMA((len(groups),))],
        input_output_aliases={len(given): 0} if into else {},
        compiler_params=params(6),
        name="finish",
    )(*given, *into)


def per_device(
    n_step,
    n_seq,
    trajectory,
    x_start,
    t_idx,
    mod_table,
    step_sizes,
    q_gain,
    k_gain,
    w_qkv,
    w_mlp_in,
    w_out_attn,
    w_out_mlp,
):
    head = q_gain.shape[0]
    rows, width = x_start.shape
    chips = n_seq // 2
    groups = n_step // 2
    half = rows // 2
    unit = width // 24
    counts = [n * unit for n in (9, 7, 8)]
    chunks = len(counts)
    firsts = [sum(counts[:c]) for c in range(chunks)]
    qg, kg = q_gain[None, :], k_gain[None, :]

    def to_core(x):
        return lax.ppermute(x, "seq", [(i, i ^ 1) for i in range(n_seq)])

    def to_chip(x, offset):
        return lax.ppermute(x, "seq", [(i, (i + 2 * offset) % n_seq) for i in range(n_seq)])

    def to_pair(x):
        return lax.ppermute(x, "step", [(i, i ^ 1) for i in range(n_step)])

    def tied(*values):
        return lax.optimization_barrier(values)

    parity = lax.rem(lax.axis_index("step"), 2)
    even = (parity == 0).astype(f32)
    which = parity[None]
    offsets = range(1, chips)

    *mine, sg = norm_call(t_idx, trajectory, mod_table, step_sizes)
    far = [[to_chip(part, j) for part in mine] for j in offsets]
    given = mine + [to_core(part) for part in mine]
    q0, k0, v0, act0, low0, high0, *held = project_call(
        given, qg, kg, w_qkv, w_mlp_in, w_out_mlp, None
    )
    given = []
    for top, low in far:
        top, q0 = tied(top, q0)
        next_top = to_core(top)
        low, next_top = tied(low, next_top)
        given.append([top, low, next_top, to_core(low)])
    qs, ks, vs, acts = [], [k0], [v0], []
    for blocks in given:
        q, k, v, act = project_call(blocks, qg, kg, w_qkv, w_mlp_in, w_out_mlp, held)
        qs.append(q)
        ks.append(k)
        vs.append(v)
        acts.append(act)
    mixed = [attend_call(q, ks, vs, head) for q in qs]

    weights = [w_out_attn, w_out_mlp]
    got = [[] for _ in offsets]

    def jobs_of(c):
        return [([a, b], weights, [], firsts[c], counts[c]) for a, b in zip(mixed, acts)]

    def joined(parts, sent):
        return [join_call(keep, s) for (keep, _), s in zip(parts, sent)]

    def to_chips(ready):
        for j, one in enumerate(ready):
            got[j].append(to_chip(one, chips - 1 - j))

    parts = out_call(jobs_of(0))
    sent = [to_core(send) for _, send in parts]
    q0, parts = tied(q0, parts)
    mixed0 = attend_call(q0, ks, vs, head)
    mixed0, sent = tied(mixed0, sent)
    ready = joined(parts, sent)
    mixed, acts, mixed0, ready = tied(mixed, acts, mixed0, ready)
    to_chips(ready)
    jobs = [job for c in range(1, chunks) for job in jobs_of(c)]
    for c in range(chunks):
        jobs.append(([mixed0], [w_out_attn], [low0, high0], firsts[c], counts[c]))
    parts = out_call(jobs)
    sent = [to_core(send) for _, send in parts]
    keep = [part[0] for part in parts[-chunks:]]
    sent0 = sent[-chunks:]
    others = chips - 1
    first, keep, sent[:others] = tied([row[0] for row in got], keep, sent[:others])
    for row, one in zip(got, first):
        row[0] = one
    ready = joined(parts[:others], sent[:others])
    keep, ready = tied(keep, ready)
    to_chips(ready)
    for c in range(2, chunks):
        here = slice((c - 1) * others, c * others)
        to_chips(joined(parts[here], sent[here]))

    def along(pairs):
        return lambda x: lax.ppermute(x, "step", [(2 * a + i, 2 * b + i) for a, b in pairs for i in (0, 1)])

    group = lax.div(lax.axis_index("step"), 2)
    rounds = []
    span = 1
    while span < groups:
        pairs = [(b, b ^ span) for b in range(groups) if b ^ span < groups]
        rounds.append((span, along(pairs)))
        span *= 2

    def prefix_stages(c):
        held = {}

        def drift_of(fetched):
            drift = drift_call(which, keep[c], sent0[c], sg, fetched, firsts[c])
            held["kept"], held["other"], send = drift
            return send

        def pair_sum(fetched):
            held["fetched"] = fetched[0]
            held["total"] = held["kept"] + fetched[0].astype(f32)
            return held["total"].astype(bf16)

        def collect(r, fetched):
            one = fetched[0].astype(f32)
            upper = (lax.rem(lax.div(group, rounds[r][0]), 2) == 1).astype(f32)
            held["earlier"] = held["earlier"] + upper * one if r else upper * one
            if r == len(rounds) - 1:
                return (held["earlier"] + even * held["kept"]).astype(bf16)
            held["total"] = held["total"] + one
            return held["total"].astype(bf16)

        def finish(fetched):
            given = [held[name] for name in ("earlier", "kept", "fetched", "other")]
            stash.append((firsts[c], given + [fetched[0]]))
            if len(stash) in (1, chunks):
                mine = stash[len(stash) - 1 :] if len(stash) == 1 else stash[1:]
                places = [place for place, _ in mine]
                groups_in = [group for _, group in mine]
                into = list(written)
                written[:] = [finish_call(which, x_start, groups_in, places, into)]

        stages = [(drift_of, to_pair), (pair_sum, rounds[0][1])]
        for r in range(len(rounds)):
            move = to_pair if r == len(rounds) - 1 else rounds[r + 1][1]
            stages.append((functools.partial(collect, r), move))
        stages.append((finish, None))
        return stages

    plan = [prefix_stages(c) for c in range(chunks)]
    inbox = [[got[j][c] for j in range(chips - 1)] for c in range(chunks)]
    turns = []
    arrival = 2.0
    for c in range(chunks):
        share = 16.0 * (10 - 2 * c) / 24
        arrival += share
        when = arrival
        for i in range(len(plan[c])):
            turns.append((when, c, i))
            when += 2.2 + share * (1.0 if i == len(plan[c]) - 3 else 0.5)
    written, stash = [], []
    last = None
    for _, c, i in sorted(turns):
        compute, move = plan[c][i]
        fetched = inbox[c]
        if last is not None:
            fetched, last = tied(fetched, last)
        out = compute(fetched)
        if move is not None:
            inbox[c] = [move(out)]
            last = out
    return written[0]


def solution(mesh):
    placed = (
        P("step", "seq", None),
        P("seq", None),
        P("step"),
        P(),
        P(),
        P(),
        P(),
        P(None, None, "seq"),
        P(None, "seq"),
        P("seq", None),
        P("seq", None),
    )
    return jax.shard_map(
        functools.partial(per_device, mesh.shape["step"], mesh.shape["seq"]),
        mesh=mesh,
        in_specs=placed,
        out_specs=P("step", "seq", None),
        check_vma=False,
    )
```
